32 devices in a mesh: dp: 2 (over y), seq: 2 (over core), tensor: 8 (over z, x).
Axes of the slice: x: 2, y: 2, z: 4, core: 2. Of those that a mesh axis runs over, the one named last changes fastest.
Arguments:
- tokens: bfloat16 [2, 2048, 2048], P('dp', 'seq'), may hold values from -6 to 6
- cotangent: bfloat16 [2, 2048, 2048], P('dp', 'seq'), may hold values from -6 to 6
- query_weight: float32 [2048, 2048], P(('dp', 'seq'), 'tensor'), may hold values from -0.125 to 0.125
- output_weight: float32 [2048, 2048], P(('dp', 'seq'), 'tensor'), may hold values from -4 to 4
- kv_weight: float32 [2048, 1024], P(('dp', 'seq'), 'tensor'), may hold values from -0.125 to 0.125
- gate_up_weight: float32 [2048, 2, 8192], P(('dp', 'seq'), None, 'tensor'), may hold values from -0.125 to 0.125
- down_weight: float32 [2048, 8192], P(('dp', 'seq'), 'tensor'), may hold values from -0.0625 to 0.0625
- norm_gains: float32 [2048, 2], P(('dp', 'seq')), may hold values from 0.5 to 1.5
- query_first: float32 [2048, 2048], P(('dp', 'seq'), 'tensor'), may hold values from -64 to 64
- output_first: float32 [2048, 2048], P(('dp', 'seq'), 'tensor'), may hold values from -2 to 2
- kv_first: float32 [2048, 1024], P(('dp', 'seq'), 'tensor'), may hold values from -128 to 128
- gate_up_first: float32 [2048, 2, 8192], P(('dp', 'seq'), None, 'tensor'), may hold values from -12 to 12
- down_first: float32 [2048, 8192], P(('dp', 'seq'), 'tensor'), may hold values from -24 to 24
- gains_first: float32 [2048, 2], P(('dp', 'seq')), may hold values from -80 to 80
- query_second: float32 [2048, 2048], P(('dp', 'seq'), 'tensor'), may hold values from 546.816 to 2191.36
- output_second: float32 [2048, 2048], P(('dp', 'seq'), 'tensor'), may hold values from 0.534 to 2.14
- kv_second: float32 [2048, 1024], P(('dp', 'seq'), 'tensor'), may hold values from 2191.36 to 8744.96
- gate_up_second: float32 [2048, 2, 8192], P(('dp', 'seq'), None, 'tensor'), may hold values from 19.3536 to 77.6192
- down_second: float32 [2048, 8192], P(('dp', 'seq'), 'tensor'), may hold values from 77.4144 to 310.4768
- gains_second: float32 [2048, 2], P(('dp', 'seq')), may hold values from 155.2384 to 4915.2
Outputs:
- block_out: bfloat16 [2, 2048, 2048], P('dp', 'seq')
- tokens_grad: float32 [2, 2048, 2048], P('dp', 'seq')
- query_updated: float32 [2048, 2048], P(('dp', 'seq'), 'tensor')
- output_updated: float32 [2048, 2048], P(('dp', 'seq'), 'tensor')
- kv_updated: float32 [2048, 1024], P(('dp', 'seq'), 'tensor')
- gate_up_updated: float32 [2048, 2, 8192], P(('dp', 'seq'), None, 'tensor')
- down_updated: float32 [2048, 8192], P(('dp', 'seq'), 'tensor')
- gains_updated: float32 [2048, 2], P(('dp', 'seq'))
- query_first_out: float32 [2048, 2048], P(('dp', 'seq'), 'tensor')
- output_first_out: float32 [2048, 2048], P(('dp', 'seq'), 'tensor')
- kv_first_out: float32 [2048, 1024], P(('dp', 'seq'), 'tensor')
- gate_up_first_out: float32 [2048, 2, 8192], P(('dp', 'seq'), None, 'tensor')
- down_first_out: float32 [2048, 8192], P(('dp', 'seq'), 'tensor')
- gains_first_out: float32 [2048, 2], P(('dp', 'seq'))
- query_second_out: float32 [2048, 2048], P(('dp', 'seq'), 'tensor')
- output_second_out: float32 [2048, 2048], P(('dp', 'seq'), 'tensor')
- kv_second_out: float32 [2048, 1024], P(('dp', 'seq'), 'tensor')
- gate_up_second_out: float32 [2048, 2, 8192], P(('dp', 'seq'), None, 'tensor')
- down_second_out: float32 [2048, 8192], P(('dp', 'seq'), 'tensor')
- gains_second_out: float32 [2048, 2], P(('dp', 'seq'))
The draws below stay inside these ranges and needn't reach their ends.
All inputs are finite; a program needn't handle non-finite values.
Results may differ from the reference program's by a relative error of at most 0.023.
Values may be sent and summed in bfloat16 or wider, within the bound.
No kernel may reach another device: no remote copies, remote signals or barrier semaphores. Data moves between devices by JAX's collectives and lax.ppermute only.
A program may use at most 256 MiB of HBM per device.

```python
import math
import jax
import jax.numpy as jnp
from jax import lax

D = 2048
FF = 8192
HEADS = 32
KV_HEADS = 8
HEAD_DIM = 64
LENGTH = 2048
STEP = 10
SEQS = 2
FAN_OUT = 2


def level_of(stream_key, extent, cuts, smallest, high):
    factor_of, own = 1.0, jax.random.fold_in(stream_key, 6)
    for position, parts in cuts:
        heights = jnp.exp(jax.random.uniform(jax.random.fold_in(own, position), (parts,), jnp.float32, smallest / len(cuts), high / len(cuts)))
        factor_of = factor_of * jnp.repeat(heights, extent[position] // parts).reshape([-1 if axis == position else 1 for axis in range(len(extent))])
    return factor_of


def gaussian(key, extent, deviation, most, cuts=(), kind=jnp.bfloat16):
    values = deviation * jax.random.normal(key, extent, jnp.float32)
    if cuts:
        values = values * level_of(key, extent, cuts, -0.22, 0.18)
    return jnp.clip(values, -most, most).astype(kind)


def setup_inputs(seed: int = 0) -> dict:
    keys = jax.random.split(jax.random.key(seed), 21)
    tokens = gaussian(keys[0], (SEQS, LENGTH, D), 1.0, 6.0, ((0, 2), (1, 2)))
    cotangent = gaussian(keys[1], (SEQS, LENGTH, D), 1.0, 6.0, ((0, 2), (1, 2)))
    query_weight = gaussian(keys[2], (D, HEADS * HEAD_DIM), D ** -0.5, 0.125, ((0, 4), (1, 8)), jnp.float32)
    output_weight = gaussian(keys[3], (D, HEADS * HEAD_DIM), FAN_OUT ** -0.5, 4.0, ((0, 4), (1, 8)), jnp.float32)
    kv_weight = gaussian(keys[4], (D, 2 * KV_HEADS * HEAD_DIM), D ** -0.5, 0.125, ((0, 4), (1, 8)), jnp.float32)
    gate_up_weight = gaussian(keys[5], (D, 2, FF), D ** -0.5, 0.125, ((0, 4), (2, 8)), jnp.float32)
    down_weight = gaussian(keys[6], (D, FF), FF ** -0.5, 0.0625, ((0, 4), (1, 8)), jnp.float32)
    norm_gains = jnp.clip(1.0 + 0.1 * jax.random.normal(keys[7], (D, 2), jnp.float32), 0.5, 1.5)
    query_first = gaussian(keys[8], (D, HEADS * HEAD_DIM), ((0.0625 * D * SEQS * FAN_OUT ** -1) ** 0.5), 64.0, ((0, 4), (1, 8)), jnp.float32)
    output_first = gaussian(keys[9], (D, HEADS * HEAD_DIM), ((0.0626 * SEQS) ** 0.5), 2.0, ((0, 4), (1, 8)), jnp.float32)
    kv_first = gaussian(keys[10], (D, 2 * KV_HEADS * HEAD_DIM), ((0.25 * D * SEQS * FAN_OUT ** -1) ** 0.5), 128.0, ((0, 4), (1, 8)), jnp.float32)
    gate_up_first = gaussian(keys[11], (D, 2, FF), ((0.00444 * D * SEQS * LENGTH * FF ** -1) ** 0.5), 12.0, ((0, 4), (2, 8)), jnp.float32)
    down_first = gaussian(keys[12], (D, FF), ((0.00444 * SEQS * LENGTH) ** 0.5), 24.0, ((0, 4), (1, 8)), jnp.float32)
    gains_first = gaussian(keys[13], (D, 2), ((0.07 * D * SEQS * FAN_OUT ** -1 + 0.0045 * SEQS * LENGTH) ** 0.5), 80.0, ((0, 4),), jnp.float32)
    query_second = jnp.clip(jnp.exp(math.log(2191.36) - 1.3881654 * jax.random.uniform(keys[14], (D, HEADS * HEAD_DIM), jnp.float32) ** level_of(keys[14], (D, HEADS * HEAD_DIM), ((0, 4), (1, 8)), -0.2, 0.2)), 546.816, 2191.36)
    output_second = jnp.clip(jnp.exp(math.log(2.14) - 1.3881654 * jax.random.uniform(keys[15], (D, HEADS * HEAD_DIM), jnp.float32) ** level_of(keys[15], (D, HEADS * HEAD_DIM), ((0, 4), (1, 8)), -0.2, 0.2)), 0.534, 2.14)
    kv_second = jnp.clip(jnp.exp(math.log(8744.96) - 1.3839551 * jax.random.uniform(keys[16], (D, 2 * KV_HEADS * HEAD_DIM), jnp.float32) ** level_of(keys[16], (D, 2 * KV_HEADS * HEAD_DIM), ((0, 4), (1, 8)), -0.2, 0.2)), 2191.36, 8744.96)
    gate_up_second = jnp.clip(jnp.exp(math.log(77.6192) - 1.3889364 * jax.random.uniform(keys[17], (D, 2, FF), jnp.float32) ** level_of(keys[17], (D, 2, FF), ((0, 4), (2, 8)), -0.2, 0.2)), 19.3536, 77.6192)
    down_second = jnp.clip(jnp.exp(math.log(310.4768) - 1.3889364 * jax.random.uniform(keys[18], (D, FF), jnp.float32) ** level_of(keys[18], (D, FF), ((0, 4), (1, 8)), -0.2, 0.2)), 77.4144, 310.4768)
    gains_second = jnp.clip(jnp.exp(math.log(4915.2) - 3.4551257 * jax.random.uniform(keys[19], (D, 2), jnp.float32) ** level_of(keys[19], (D, 2), ((0, 4),), -0.2, 0.2)), 155.2384, 4915.2)
    return dict(tokens=tokens, cotangent=cotangent, query_weight=query_weight, output_weight=output_weight, kv_weight=kv_weight, gate_up_weight=gate_up_weight, down_weight=down_weight, norm_gains=norm_gains, query_first=query_first, output_first=output_first, kv_first=kv_first, gate_up_first=gate_up_first, down_first=down_first, gains_first=gains_first, query_second=query_second, output_second=output_second, kv_second=kv_second, gate_up_second=gate_up_second, down_second=down_second, gains_second=gains_second)


EPS_NORM = 1e-05
ROPE_BASE = 500000.0
BETA_ONE = 0.9
BETA_TWO = 0.95
ADAM_EPS = 1e-08
DECAY = 0.1
RATE_FACTOR = 3.0
GAIN_RATE = 1.0
MASKED = -1e+30
HIGH = lax.Precision.HIGHEST

@jax.custom_vjp
def low(v):
    return lax.optimization_barrier(v.astype(jnp.bfloat16)).astype(jnp.float32)

@jax.custom_vjp
def low_back(v):
    return v

def low_keep(v):
    return (low(v), None)

def low_pass(kept, grad):
    return (grad,)

def back_keep(v):
    return (v, None)

def back_low(kept, grad):
    return (low(grad),)
low.defvjp(low_keep, low_pass)
low_back.defvjp(back_keep, back_low)

def rope_tables(positions):
    half_dim = HEAD_DIM // 2
    exponent = jnp.arange(half_dim, dtype=jnp.float32) * (2.0 / HEAD_DIM)
    inverse = jnp.power(jnp.float32(ROPE_BASE), -exponent)
    angles = positions.astype(jnp.float32)[:, None] * inverse[None, :]
    return (jnp.cos(angles), jnp.sin(angles))

def rotate(values, cosine, sine_table):
    half_dim = values.shape[-1] // 2
    first_half = values[..., :half_dim]
    second_half = values[..., half_dim:]
    cos_rows = cosine[:, None, :]
    sin_rows = sine_table[:, None, :]
    return jnp.concatenate([first_half * cos_rows - second_half * sin_rows, second_half * cos_rows + first_half * sin_rows], axis=-1)

def normalize(values, gain):
    return values * lax.rsqrt(lax.optimization_barrier(jnp.mean(values * values, axis=-1, keepdims=True)) + EPS_NORM) * gain

def head_attention(operands):
    query_rows, key_rows, value_rows = operands
    length = key_rows.shape[0]
    scores = jnp.einsum('gqd,kd->gqk', query_rows, key_rows, precision=HIGH) * HEAD_DIM ** (-0.5)
    scores = low_back(scores)
    places = jnp.arange(length)
    visible = places[:, None] >= places[None, :]
    scores = jnp.where(visible[None], scores, MASKED)
    highest = lax.optimization_barrier(jnp.max(scores, axis=-1, keepdims=True))
    weights = jnp.exp(scores - highest)
    chances = weights / lax.optimization_barrier(jnp.sum(weights, axis=-1, keepdims=True))
    return jnp.einsum('gqk,kd->gqd', low(chances), value_rows, precision=HIGH)

def layer(tokens_seq, query_weight, output_weight, kv_weight, gate_up_weight, down_weight, norm_gains):
    query_low = low(query_weight)
    output_low = low(output_weight)
    kv_low = low(kv_weight)
    gate_up_low = low(gate_up_weight)
    down_low = low(down_weight)
    gains_low = low(norm_gains)
    length = tokens_seq.shape[0]
    group_size = HEADS // KV_HEADS
    normed_one = low(normalize(tokens_seq, gains_low[:, 0]))
    query_raw = low_back(jnp.dot(normed_one, query_low, precision=HIGH))
    kv_raw = low_back(jnp.dot(normed_one, kv_low, precision=HIGH)).reshape(length, KV_HEADS, 2, HEAD_DIM)
    cosine, sine_table = rope_tables(jnp.arange(length, dtype=jnp.int32))
    queries = low(rotate(query_raw.reshape(length, HEADS, HEAD_DIM), cosine, sine_table))
    key_heads = low(rotate(kv_raw[:, :, 0], cosine, sine_table))
    value_heads = low(kv_raw[:, :, 1])
    query_heads = queries.reshape(length, KV_HEADS, group_size, HEAD_DIM).transpose(1, 2, 0, 3)
    attended = lax.map(jax.checkpoint(head_attention), (query_heads, key_heads.transpose(1, 0, 2), value_heads.transpose(1, 0, 2)))
    attended = low(low_back(attended.transpose(2, 0, 1, 3).reshape(length, HEADS * HEAD_DIM)))
    attn_out = low_back(jnp.dot(attended, output_low.T, precision=HIGH))
    resid_one = tokens_seq + attn_out
    normed_two = low(normalize(resid_one, gains_low[:, 1]))
    gate_part = low_back(jnp.dot(normed_two, gate_up_low[:, 0], precision=HIGH))
    up_part = low_back(jnp.dot(normed_two, gate_up_low[:, 1], precision=HIGH))
    hidden = low(gate_part * jax.nn.sigmoid(gate_part) * up_part)
    mlp_out = jnp.dot(hidden, down_low.T, precision=HIGH)
    return resid_one + mlp_out

def adam_step(weight, grad_sum, moment_one, moment_two, step_rate, decay_rate):
    first_new = BETA_ONE * moment_one + (1.0 - BETA_ONE) * grad_sum
    second_new = BETA_TWO * moment_two + (1.0 - BETA_TWO) * grad_sum * grad_sum
    first_hat = first_new / (1.0 - BETA_ONE ** STEP)
    second_hat = second_new / (1.0 - BETA_TWO ** STEP)
    updated = weight - step_rate * (first_hat / (jnp.sqrt(second_hat) + ADAM_EPS) + decay_rate * weight)
    return (updated, first_new, second_new)

def reference(tokens, cotangent, query_weight, output_weight, kv_weight, gate_up_weight, down_weight, norm_gains, query_first, output_first, kv_first, gate_up_first, down_first, gains_first, query_second, output_second, kv_second, gate_up_second, down_second, gains_second):
    weights = (query_weight, output_weight, kv_weight, gate_up_weight, down_weight, norm_gains)

    def one_sequence(totals, operands):
        tokens_seq, cot_seq = operands
        outputs, pullback = jax.vjp(layer, tokens_seq, *weights)
        gradients = pullback(cot_seq)
        totals = tuple((running + grad_part for running, grad_part in zip(totals, gradients[1:])))
        return (totals, (outputs.astype(jnp.bfloat16), gradients[0]))
    zeros_init = tuple((jnp.zeros_like(weight) for weight in weights))
    totals, (block_out, tokens_grad) = lax.scan(one_sequence, zeros_init, (tokens.astype(jnp.float32), cotangent.astype(jnp.float32)))
    query_updated, query_first_out, query_second_out = adam_step(query_weight, totals[0], query_first, query_second, RATE_FACTOR * D ** (-0.5), DECAY)
    output_updated, output_first_out, output_second_out = adam_step(output_weight, totals[1], output_first, output_second, RATE_FACTOR * FAN_OUT ** (-0.5), DECAY)
    kv_updated, kv_first_out, kv_second_out = adam_step(kv_weight, totals[2], kv_first, kv_second, RATE_FACTOR * D ** (-0.5), DECAY)
    gate_up_updated, gate_up_first_out, gate_up_second_out = adam_step(gate_up_weight, totals[3], gate_up_first, gate_up_second, RATE_FACTOR * D ** (-0.5), DECAY)
    down_updated, down_first_out, down_second_out = adam_step(down_weight, totals[4], down_first, down_second, RATE_FACTOR * FF ** (-0.5), DECAY)
    gains_updated, gains_first_out, gains_second_out = adam_step(norm_gains, totals[5], gains_first, gains_second, GAIN_RATE, 0.0)
    return (block_out, tokens_grad, query_updated, output_updated, kv_updated, gate_up_updated, down_updated, gains_updated, query_first_out, output_first_out, kv_first_out, gate_up_first_out, down_first_out, gains_first_out, query_second_out, output_second_out, kv_second_out, gate_up_second_out, down_second_out, gains_second_out)
```

```python
import functools

import jax
import jax.numpy as jnp
from jax import lax
from jax.experimental import pallas as pl
from jax.experimental.pallas import tpu as pltpu
from jax.sharding import PartitionSpec as P

D = 2048
FF = 8192
HEADS = 32
KV_HEADS = 8
HEAD_DIM = 64
STEP = 10
FAN_OUT = 2

EPS_NORM = 1e-05
ROPE_BASE = 500000.0
BETA_ONE = 0.9
BETA_TWO = 0.95
ADAM_EPS = 1e-08
DECAY = 0.1
RATE_FACTOR = 3.0
GAIN_RATE = 1.0
MASKED = -1e30

F32 = jnp.float32
BF16 = jnp.bfloat16
GROUP = HEADS // KV_HEADS
QUARTER = D // 4
ORDER = (0, 2, 4, 6, 1, 3, 5, 7)
WIDTH_ORDER = (0, 2, 1, 3)
HIGH_GROUPS = [[0, 2, 4, 6], [1, 3, 5, 7]]
AT_TENSOR, AT_OFFSET, AT_SEQ, AT_LOW, AT_HIGH = 4, 5, 6, 7, 8


def vmem(mib):
    return pltpu.CompilerParams(vmem_limit_bytes=mib * 1024 * 1024)


COST_SCALE = 0.5


def cost(us):
    return pl.CostEstimate(flops=0, bytes_accessed=int(COST_SCALE * us * 3.69e6), transcendentals=0)


def dot(a, b):
    return lax.dot_general(a, b, (((1,), (0,)), ((), ())), preferred_element_type=F32)


def dot_nt(a, b):
    return lax.dot_general(a, b, (((1,), (1,)), ((), ())), preferred_element_type=F32)


def swap_halves(values):
    lane = lax.broadcasted_iota(jnp.int32, values.shape, 1)
    half = HEAD_DIM // 2
    return jnp.where(
        lane % HEAD_DIM < half,
        pltpu.roll(values, 128 - half, 1),
        pltpu.roll(values, half, 1),
    )


def width_block(info, place):
    return pl.ds(pl.multiple_of(info[place] * QUARTER, QUARTER), QUARTER)


def project_kernel(info, tok, w0, w1, w2, w3, cosine, sine, normed, q_out, kv_out, gains, gain_rows):
    pieces = (w0, w1, w2, w3)

    @pl.when(pl.program_id(0) == 0)
    def _():
        for place, piece in enumerate(pieces):
            turned = piece[:, 384:512].astype(F32).T
            gain_rows[:, place * QUARTER : (place + 1) * QUARTER] = turned[0:8]
        natural_store(info, gains, gain_rows[...])

    parts = [tok[:, width_block(info, place)].astype(F32) for place in range(4)]
    square = sum(jnp.sum(part * part, axis=1, keepdims=True) for part in parts)
    inverse = lax.rsqrt(square * (1.0 / D) + EPS_NORM)
    total = None
    for place, (part, piece) in enumerate(zip(parts, pieces)):
        cols = slice(place * QUARTER, (place + 1) * QUARTER)
        low = (part * inverse * gain_rows[0:1, cols]).astype(BF16)
        normed[:, cols] = low
        term = dot(low, piece[:, 0:384])
        total = term if total is None else total + term
    cos, sin = cosine[...], sine[...]
    for c in (0, 128):
        raw = total[:, c : c + 128]
        q_out[:, c : c + 128] = (raw * cos + swap_halves(raw) * sin).astype(BF16)
    raw = total[:, 256:384]
    turned = raw * cos + swap_halves(raw) * sin
    lane = lax.broadcasted_iota(jnp.int32, raw.shape, 1)
    kv_out[...] = jnp.where(lane < HEAD_DIM, turned, raw).astype(BF16)


def heads_wide(turned):
    return jnp.concatenate(
        [turned[h * HEAD_DIM : (h + 1) * HEAD_DIM] for h in range(GROUP)], axis=1
    )


def heads_tall(wide, rows):
    return jnp.concatenate([wide[:, h * rows : (h + 1) * rows] for h in range(GROUP)], axis=0)


def diagonal_mask(rows, keys, shift):
    key = lax.broadcasted_iota(jnp.int32, (keys, GROUP * rows), 0)
    query = lax.broadcasted_iota(jnp.int32, (keys, GROUP * rows), 1) % rows
    return key <= query + shift


def diagonal_block(rows, keys, step, info):
    start = info[AT_OFFSET] + step
    ratio = keys // rows
    diagonal = lax.div(start, jnp.int32(ratio))
    return diagonal, (start - diagonal * ratio) * rows


def attend_kernel(
    rows, keys, info, q, kv, out, log_out, piece0, piece1, piece2, piece3, kv_turned, acc, high
):
    step = pl.program_id(0)

    @pl.when(step == 0)
    def _():
        turned = kv[...].T
        row = lax.broadcasted_iota(jnp.int32, turned.shape, 0)
        kv_turned[...] = jnp.where(row < HEAD_DIM, jnp.ones_like(turned), turned)

    wide = heads_wide((q[...] * (HEAD_DIM**-0.5)).astype(F32).T).astype(BF16)
    wide = jnp.concatenate([wide, jnp.zeros_like(wide)], axis=0)
    diagonal, shift = diagonal_block(rows, keys, step, info)

    def scores_of(j):
        return dot(kv[pl.ds(pl.multiple_of(j * keys, keys), keys), :], wide)

    def values_of(j):
        return kv_turned[:, pl.ds(pl.multiple_of(j * keys, keys), keys)]

    scores = jnp.where(diagonal_mask(rows, keys, shift), scores_of(diagonal), MASKED)
    top = jnp.max(scores, axis=0, keepdims=True)
    high[...] = top
    acc[...] = dot(values_of(diagonal), jnp.exp(scores - top).astype(BF16))

    def body(j, carry):
        scores = scores_of(j)
        old = high[...]
        top = jnp.maximum(old, jnp.max(scores, axis=0, keepdims=True))
        high[...] = top
        chances = jnp.exp(scores - top).astype(BF16)
        acc[...] = acc[...] * jnp.exp(old - top) + dot(values_of(j), chances)
        return carry

    lax.fori_loop(0, diagonal, body, 0)
    total = acc[0:1, :]
    log_out[0] = high[...] + jnp.log(total)
    result = acc[HEAD_DIM:, :] * (1.0 / total)
    out[...] = heads_tall(result, rows).T.astype(BF16)
    for k, piece in enumerate((piece0, piece1, piece2, piece3)):

        @pl.when(lax.bitwise_xor(step, info[AT_HIGH]) == k)
        def _():
            piece[...] = out[...]


def attend_back_kernel(
    rows, keys, spans, info, q, grad0, grad1, grad2, grad3, att, log_in, kv, cosine, sine,
    dq_out, piece0, piece1, piece2, piece3, dkv_out, kv_turned, dkv, dq_acc, grad,
):
    step = pl.program_id(0)

    @pl.when(step == 0)
    def _():
        kv_turned[...] = kv[...].T[0:HEAD_DIM]
        dkv[...] = jnp.zeros_like(dkv)

    for k, piece in enumerate((grad0, grad1, grad2, grad3)):

        @pl.when(lax.bitwise_xor(step, info[AT_HIGH]) == k)
        def _():
            grad[...] = piece[...]

    scaled = q[...] * (HEAD_DIM**-0.5)
    grads = grad[...]
    zero_tall = jnp.zeros((GROUP * rows, HEAD_DIM), BF16)
    q_tall = jnp.concatenate(
        [scaled[:, h * HEAD_DIM : (h + 1) * HEAD_DIM] for h in range(GROUP)], axis=0
    ).astype(BF16)
    g_tall = jnp.concatenate(
        [grads[:, h * HEAD_DIM : (h + 1) * HEAD_DIM] for h in range(GROUP)], axis=0
    )
    q_tall = jnp.concatenate([q_tall, zero_tall], axis=1)
    g_tall = jnp.concatenate([zero_tall, g_tall], axis=1)
    q_wide = heads_wide(scaled.astype(F32).T).astype(BF16)
    g_turned = grads.astype(F32).T
    g_wide = heads_wide(g_turned).astype(BF16)
    zero_wide = jnp.zeros_like(g_wide)
    product = heads_wide(g_turned * att[...].astype(F32).T)
    delta = jnp.sum(product, axis=0, keepdims=True)
    q_wide = jnp.concatenate([q_wide, zero_wide], axis=0)
    g_wide = jnp.concatenate([zero_wide, g_wide], axis=0)
    logs = log_in[0]
    diagonal, shift = diagonal_block(rows, keys, step, info)

    def one_block(j, mask):
        place = pl.ds(pl.multiple_of(j * keys, keys), keys)
        block = kv[place, :]
        chances = jnp.exp(dot(block, q_wide) - logs)
        if mask is not None:
            chances = jnp.where(mask, chances, 0.0)
        chance_grad = dot(block, g_wide)
        score_grad = (chances * (chance_grad - delta)).astype(BF16)
        dkv[place, :] += dot(score_grad, q_tall) + dot(chances.astype(BF16), g_tall)
        return dot(kv_turned[:, place], score_grad)

    dq_acc[...] = one_block(diagonal, diagonal_mask(rows, keys, shift))

    def body(j, carry):
        dq_acc[...] += one_block(j, None)
        return carry

    lax.fori_loop(0, diagonal, body, 0)
    dq = heads_tall(dq_acc[...] * (HEAD_DIM**-0.5), rows).T
    cos, sin = cosine[...], sine[...]
    for c in (0, 128):
        raw = dq[:, c : c + 128]
        dq_out[:, c : c + 128] = (raw * cos - swap_halves(raw) * sin).astype(BF16)
    for k, piece in enumerate((piece0, piece1, piece2, piece3)):

        @pl.when(lax.bitwise_xor(step, info[AT_HIGH]) == k)
        def _():
            piece[...] = dq_out[...]

    @pl.when(step == pl.num_programs(0) - 1)
    def _():
        span = dkv_out.shape[1]
        for r in range(spans):
            at = lax.bitwise_xor(info[AT_SEQ], jnp.int32(r)) * span
            dkv_out[r] = dkv[pl.ds(pl.multiple_of(at, span), span), :].astype(BF16)


def out_kernel(info, a0, a1, a2, a3, w0, w1, w2, w3, keep, send, total):
    half = keep.shape[0]
    low = info[AT_LOW]
    for place, w in enumerate((w0, w1, w2, w3)):
        cols = width_block(info, place)
        total[...] = sum(
            dot_nt(a[...], w[lax.bitwise_xor(info[AT_HIGH], jnp.int32(k))])
            for k, a in enumerate((a0, a1, a2, a3))
        )
        keep[:, cols] = total[pl.ds(pl.multiple_of(low * half, half), half), :]
        send[:, cols] = total[pl.ds(pl.multiple_of((1 - low) * half, half), half), :].astype(BF16)


def norm_kernel(info, keep, got, tok, gains, resid_out, low_a, low_b):
    resid = tok[...].astype(F32) + keep[...] + got[...].astype(F32)
    resid_out[...] = resid
    inverse = lax.rsqrt(jnp.mean(resid * resid, axis=1, keepdims=True) + EPS_NORM)
    low = (resid * inverse * gains[1:2, :]).astype(BF16)
    half = low.shape[0] // 2
    low_a[...] = low[:half]
    low_b[...] = low[half:]


def mlp_kernel(
    info, near, far, dy, gate_up_all, down_all, *rest,
):
    mlp_keep, mlp_send, two_keep, two_send, hidden_out, grad_out, x, gate_up, down, sems = rest[-10:]
    step = pl.program_id(0)
    wide = FF // 8
    n = x.shape[0]

    def copies(group):
        cols = pl.ds(group * 256, 256)
        up_cols = pl.ds(wide + group * 256, 256)
        for k, (src, dst, c) in enumerate(
            ((gate_up_all, gate_up, cols), (gate_up_all, gate_up, up_cols), (down_all, down, cols))
        ):
            yield pltpu.make_async_copy(src.at[:, c], dst.at[:, c], sems.at[group, k])

    @pl.when(step == 0)
    def _():
        for group in range(4):
            for copy in copies(group):
                copy.start()
        x[: n // 2] = near[...]
        x[n // 2 :] = far[...]

    for group in range(4):

        @pl.when(step == group)
        def _():
            for copy in copies(group):
                copy.wait()
            cols = slice(group * 256, (group + 1) * 256)
            up_cols = slice(wide + group * 256, wide + (group + 1) * 256)
            gate = dot(x[...], gate_up[:, cols])
            up = dot(x[...], gate_up[:, up_cols])
            hidden_grad = dot(dy[0], down[:, cols])
            sigmoid = 1.0 / (1.0 + jnp.exp(-gate))
            silu = gate * sigmoid
            hidden_out[:, cols] = (silu * up).astype(BF16)
            grad_out[:, cols] = (
                hidden_grad * up * (sigmoid * (1.0 + gate * (1.0 - sigmoid)))
            ).astype(BF16)
            grad_out[:, up_cols] = (hidden_grad * silu).astype(BF16)

    @pl.when(step >= 4)
    def _():
        rows = pl.ds(pl.multiple_of((step - 4) * QUARTER, QUARTER), QUARTER)
        two = dot_nt(grad_out[...], gate_up[rows, :]).astype(BF16)
        two_keep[...] = two[: n // 2]
        two_send[...] = two[n // 2 :]
        mlp = dot_nt(hidden_out[...], down[rows, :]).astype(BF16)
        size = n // 8
        for i in range(4):
            owner = lax.bitwise_xor(info[AT_HIGH], jnp.int32(i))
            mlp_keep[owner] = mlp[i * size : (i + 1) * size]
            mlp_send[owner] = mlp[n // 2 + i * size : n // 2 + (i + 1) * size]


def norm_back(values, incoming, gain):
    inverse = lax.rsqrt(jnp.mean(values * values, axis=1, keepdims=True) + EPS_NORM)
    scaled = incoming * gain
    gain_grad = jnp.sum(incoming * values * inverse, axis=0, keepdims=True)
    inner = jnp.mean(scaled * values, axis=1, keepdims=True)
    return inverse * scaled - values * (inverse * inverse * inverse * inner), gain_grad


def summed(parts):
    return sum(part[...].astype(F32) for part in parts)


def norm_back_kernel(info, *refs):
    parts_a, parts_b = refs[0:4], refs[4:8]
    resid, dy, gains, resid_grad, resid_low, gain_grad = refs[8:]
    half = dy.shape[1]
    sums = []
    for i, parts in enumerate((parts_a, parts_b)):
        rows = slice(i * half, (i + 1) * half)
        back, gain_part = norm_back(resid[rows], summed(parts), gains[1:2, :])
        full = dy[i].astype(F32) + back
        resid_grad[rows] = full
        resid_low[rows] = full.astype(BF16)
        sums.append(gain_part)
    gain_grad[...] = sums[0] + sums[1]


def out_back_kernel(info, own, other, w0, w1, w2, w3, both, g0, g1, g2, g3):
    half = own.shape[0]
    low = info[AT_LOW]
    for place in range(4):
        cols = slice(place * QUARTER, (place + 1) * QUARTER)
        natural = width_block(info, place)
        both[pl.ds(pl.multiple_of(low * half, half), half), cols] = own[:, natural]
        both[pl.ds(pl.multiple_of((1 - low) * half, half), half), cols] = other[:, natural]
    for k, out in enumerate((g0, g1, g2, g3)):
        high = lax.bitwise_xor(info[AT_HIGH], jnp.int32(k))
        out[...] = sum(
            dot(both[:, place * QUARTER : (place + 1) * QUARTER], w[high])
            for place, w in enumerate((w0, w1, w2, w3))
        ).astype(BF16)


def natural_store(info, out, value):
    for place in range(4):
        out[:, width_block(info, place)] = value[:, place * QUARTER : (place + 1) * QUARTER]


def kv_back_kernel(info, dkv, dkv_more, cosine, sine, out, p0, p1, p2, p3):
    raw = dkv[...].astype(F32) + dkv_more[...].astype(F32)
    turned = raw * cosine[...] - swap_halves(raw) * sine[...]
    lane = lax.broadcasted_iota(jnp.int32, raw.shape, 1)
    out[...] = jnp.where(lane < HEAD_DIM, turned, raw).astype(BF16)
    rows = p0.shape[0]
    for k, piece in enumerate((p0, p1, p2, p3)):
        at = lax.bitwise_xor(info[AT_HIGH], jnp.int32(k)) * rows
        piece[...] = out[pl.ds(pl.multiple_of(at, rows), rows), :]


def one_kernel(info, q0, q1, q2, q3, k0, k1, k2, k3, w, keep, send, total):
    half = keep.shape[0]
    low = info[AT_LOW]
    both = [
        jnp.concatenate([q[...], k[...]], axis=1)
        for q, k in zip((q0, q1, q2, q3), (k0, k1, k2, k3))
    ]
    for place in range(4):
        cols = width_block(info, place)
        total[...] = sum(
            dot_nt(part, w[k, info[place]])
            for k, part in enumerate(both)
        )
        keep[:, cols] = total[pl.ds(pl.multiple_of(low * half, half), half), :]
        send[:, cols] = total[pl.ds(pl.multiple_of((1 - low) * half, half), half), :].astype(BF16)


def tokens_back_kernel(info, keep, got, tok, resid_grad, gains, low):
    back, unused = norm_back(
        tok[...].astype(F32), keep[...] + got[...].astype(F32), gains[0:1, :]
    )
    low[...] = (resid_grad[...] + back).astype(BF16)


def block_out_kernel(parts_a, parts_b, resid, low):
    half = parts_a.shape[1]
    for i, parts in enumerate((parts_a, parts_b)):
        rows = slice(i * half, (i + 1) * half)
        low[rows] = (sum(parts[k].astype(F32) for k in range(4)) + resid[rows]).astype(BF16)


def reorder_kernel(info, src, out):
    half = out.shape[1]
    out[0] = src[:half]
    out[1] = src[half:]


def place_kernel(info, near, far, out):
    size = near.shape[1]
    at = info[AT_LOW] * size
    out[pl.ds(pl.multiple_of(at, size), size), :] = near[0].astype(out.dtype)
    out[pl.ds(pl.multiple_of(size - at, size), size), :] = far[0].astype(out.dtype)


def weight_grad_kernel(a, b, *outs):
    result = lax.dot_general(
        a[...], b[...], (((0,), (0,)), ((), ())), preferred_element_type=F32
    ).astype(BF16)
    if len(outs) == 1:
        outs[0][...] = result
        return

    @pl.when(pl.program_id(0) < 2)
    def _():
        outs[0][...] = result

    @pl.when(pl.program_id(0) >= 2)
    def _():
        outs[1][...] = result


def pair_sum_kernel(a, b, out):
    out[...] = (a[...].astype(F32) + b[...].astype(F32)).astype(BF16)


def adam_kernel(rate, decay, weight, one, two, *refs):
    outs = refs[-3:]
    if len(weight.shape) == 2:
        grad = summed(refs[:-3])
        results = adam_step(weight[...], grad, one[...], two[...], rate, decay)
        for out, result in zip(outs, results):
            out[...] = result
        return
    wide = weight.shape[2]
    for k in range(2):
        cols = slice(k * wide, (k + 1) * wide)
        grad = sum(ref[:, cols].astype(F32) for ref in refs[:-3])
        results = adam_step(weight[:, k, :], grad, one[:, k, :], two[:, k, :], rate, decay)
        for out, result in zip(outs, results):
            out[:, k, :] = result


def step_owner(step):
    return lax.rem(step, 4) * 2 + lax.div(step, 4)


def tensor_block(step, info):
    return lax.bitwise_xor(info[AT_TENSOR], step_owner(step))


def adam_step(weight, grad_sum, moment_one, moment_two, step_rate, decay_rate):
    first_new = BETA_ONE * moment_one + (1.0 - BETA_ONE) * grad_sum
    second_new = BETA_TWO * moment_two + (1.0 - BETA_TWO) * grad_sum * grad_sum
    first_hat = first_new / (1.0 - BETA_ONE**STEP)
    second_hat = second_new / (1.0 - BETA_TWO**STEP)
    updated = weight - step_rate * (
        first_hat / (jnp.sqrt(second_hat) + ADAM_EPS) + decay_rate * weight
    )
    return (updated, first_new, second_new)


def rope_tables(positions):
    half_dim = HEAD_DIM // 2
    exponent = jnp.arange(half_dim, dtype=F32) * (2.0 / HEAD_DIM)
    inverse = jnp.power(F32(ROPE_BASE), -exponent)
    angles = positions.astype(F32)[:, None] * inverse[None, :]
    cosine, sine = jnp.cos(angles), jnp.sin(angles)
    return (
        jnp.concatenate([cosine] * 4, axis=1),
        jnp.concatenate([-sine, sine, -sine, sine], axis=1),
    )


def whole(shape, dims=None):
    zeros = (0,) * len(shape)
    return pl.BlockSpec(shape, lambda *unused: zeros)


def body(
    tokens, cotangent, query_weight, output_weight, kv_weight, gate_up_weight, down_weight, norm_gains,
    query_first, output_first, kv_first, gate_up_first, down_first, gains_first,
    query_second, output_second, kv_second, gate_up_second, down_second, gains_second,
    *, dp_size, seq_size,
):
    fast = dp_size == 2 and seq_size == 2
    span = tokens.shape[1]
    length = span * seq_size
    rows = span // 4
    keys = max(rows, 128)
    block = span // 8
    half_block = block // 2
    tensor_id = lax.axis_index("tensor").astype(jnp.int32)
    seq_id = lax.axis_index("seq").astype(jnp.int32)
    dp_id = lax.axis_index("dp").astype(jnp.int32)
    own_width = dp_id * 2 + seq_id if fast else jnp.int32(0)
    order = WIDTH_ORDER if fast else (0, 1, 2, 3)
    info = jnp.stack(
        [lax.bitwise_xor(own_width, jnp.int32(o)) for o in order]
        + [tensor_id, seq_id * 4, seq_id if fast else jnp.int32(0), tensor_id % 2, tensor_id // 2]
    )

    def after(value, point):
        return lax.optimization_barrier((value, point))[0]

    def swap_tensor(value, mask):
        return lax.ppermute(value, "tensor", [(i, i ^ mask) for i in range(8)])

    def swap_dp(value):
        return lax.ppermute(value, "dp", [(0, 1), (1, 0)])

    def swap_seq(value):
        return lax.ppermute(value, "seq", [(0, 1), (1, 0)])

    def gather_width(shard, point=None, last=None):
        if fast:
            other = swap_dp(shard)
            own = shard
            if last is not None:
                own, other = after(own, point), after(other, last)
            return [shard, other, swap_seq(own), swap_seq(other)]
        axis = shard.ndim - 2
        full = lax.all_gather(shard, ("dp", "seq"), axis=axis, tiled=True)
        return [lax.slice_in_dim(full, i * QUARTER, (i + 1) * QUARTER, axis=axis) for i in range(4)]

    def gather_all(shard):
        return lax.all_gather(shard, ("dp", "seq"), axis=0, tiled=True)

    def scatter_all(full):
        return lax.psum_scatter(full, ("dp", "seq"), scatter_dimension=0, tiled=True)

    def weight_full(a, b, halves=False):
        n, width = b.shape
        if halves:
            specs = [
                pl.BlockSpec((QUARTER, width), lambda i: (jnp.minimum(i, 1), 0)),
                pl.BlockSpec((QUARTER, width), lambda i: (jnp.maximum(i - 2, 0), 0)),
            ]
        else:
            specs = [pl.BlockSpec((QUARTER, width), lambda i: (i, 0))]
        outs = pl.pallas_call(
            weight_grad_kernel,
            grid=(4,),
            in_specs=[pl.BlockSpec((n, QUARTER), lambda i: (0, i)), whole((n, width))],
            out_specs=specs,
            out_shape=[jax.ShapeDtypeStruct((D // len(specs), width), BF16)] * len(specs),
            compiler_params=vmem(56),
            cost_estimate=cost(n * width / 160000),
            name="weight_grad",
        )(a, b)
        return tuple(outs) if halves else outs[0]

    def weight_halves(a, b):
        return weight_full(a, b, True)

    def pair_sum(a, b, place):
        part = pl.BlockSpec((QUARTER, a.shape[1]), lambda i: (place, 0))
        return pl.pallas_call(
            pair_sum_kernel,
            grid=(1,),
            in_specs=[part, part],
            out_specs=whole((QUARTER, a.shape[1])),
            out_shape=jax.ShapeDtypeStruct((QUARTER, a.shape[1]), BF16),
            compiler_params=vmem(48),
            cost_estimate=cost(1.5),
            name="pair_sum",
        )(a, b)

    def scatter_near(halves, point):
        keep, send = halves
        if not fast:
            return keep, send, None
        got = after(swap_seq(send), point)
        return keep, got, pair_sum(keep, got, 1)

    def send_far(near):
        return swap_dp(near[2]) if fast else None

    def scatter_far(near, far):
        keep, got, low = near
        if fast:
            return [keep, got, far]
        full = jnp.concatenate([keep, got], axis=0)
        return [lax.psum_scatter(full, ("dp", "seq"), scatter_dimension=0, tiled=True)]

    def swap_high(pieces):
        return [pieces[0]] + [swap_tensor(pieces[k], 2 * k) for k in (1, 2, 3)]

    def scatter_parts(total):
        n = total.shape[0] // 4
        return [total[:n]] + [
            swap_tensor(total[i * n : (i + 1) * n].astype(BF16), mask)
            for i, mask in ((1, 2), (2, 4), (3, 6))
        ]

    def gather_near(own):
        return jnp.concatenate([own] + [swap_tensor(own, mask) for mask in (2, 4, 6)], axis=0)

    attn_low = jnp.concatenate(
        [query_weight, kv_weight, jnp.pad(norm_gains, ((0, 0), (0, 126)))], axis=1
    ).astype(BF16)
    back_low = jnp.concatenate([query_weight, kv_weight], axis=1).astype(BF16)
    output_low = after(output_weight.astype(BF16), attn_low)
    output_near = lax.all_gather(output_low, "tensor", axis=0, axis_index_groups=HIGH_GROUPS)
    token_rows = tokens.reshape(span, D)
    cot_rows = cotangent.reshape(span, D)
    positions = seq_id * span + jnp.arange(span, dtype=jnp.int32)
    cosine, sine = rope_tables(positions)
    attn_w = gather_width(attn_low, attn_low, (cosine, sine))
    back_parts = [swap_tensor(after(back_low, attn_w[1]), mask) for mask in (2, 4, 6)]
    gate_up_late, down_late = after((gate_up_weight, down_weight), attn_w[1])
    gate_up_low = jnp.concatenate(
        [gate_up_late[:, 0, :], gate_up_late[:, 1, :]], axis=1
    ).astype(BF16)
    down_low = down_late.astype(BF16)

    half_span = span // 2
    dy = pl.pallas_call(
        reorder_kernel,
        grid_spec=pltpu.PrefetchScalarGridSpec(
            num_scalar_prefetch=1,
            grid=(8,),
            in_specs=[pl.BlockSpec((block, D), lambda i, info: (tensor_block(i, info), 0))],
            out_specs=pl.BlockSpec((2, half_block, D), lambda i, info: (0, i, 0)),
        ),
        out_shape=jax.ShapeDtypeStruct((2, half_span, D), BF16),
        cost_estimate=cost(7.5),
        name="reorder",
    )(info, cot_rows)

    normed_one, queries, kv_own, gains = pl.pallas_call(
        project_kernel,
        grid_spec=pltpu.PrefetchScalarGridSpec(
            num_scalar_prefetch=1,
            grid=(span // rows,),
            in_specs=[pl.BlockSpec((rows, D), lambda i, info: (i, 0))]
            + [whole((QUARTER, 512))] * 4
            + [pl.BlockSpec((rows, 128), lambda i, info: (i, 0))] * 2,
            out_specs=[
                pl.BlockSpec((rows, D), lambda i, info: (i, 0)),
                pl.BlockSpec((rows, 256), lambda i, info: (i, 0)),
                pl.BlockSpec((rows, 128), lambda i, info: (i, 0)),
                whole((8, D)),
            ],
            scratch_shapes=[pltpu.VMEM((8, D), F32)],
        ),
        out_shape=[
            jax.ShapeDtypeStruct((span, D), BF16),
            jax.ShapeDtypeStruct((span, 256), BF16),
            jax.ShapeDtypeStruct((span, 128), BF16),
            jax.ShapeDtypeStruct((8, D), F32),
        ],
        compiler_params=vmem(48),
        cost_estimate=cost(7),
        name="project",
    )(info, token_rows, *attn_w, cosine, sine)

    if fast:
        kv_other = swap_seq(kv_own)
        kv_all = jnp.where(
            seq_id == 0,
            jnp.concatenate([kv_own, kv_other], axis=0),
            jnp.concatenate([kv_other, kv_own], axis=0),
        )
    else:
        kv_all = lax.all_gather(kv_own, "seq", axis=0, tiled=True)

    steps = 4
    attended, logs, *att_pieces = pl.pallas_call(
        functools.partial(attend_kernel, rows, keys),
        grid_spec=pltpu.PrefetchScalarGridSpec(
            num_scalar_prefetch=1,
            grid=(steps,),
            in_specs=[
                pl.BlockSpec((rows, 256), lambda i, info: (i, 0)),
                whole((length, 128)),
            ],
            out_specs=[
                pl.BlockSpec((rows, 256), lambda i, info: (i, 0)),
                pl.BlockSpec((1, 1, GROUP * rows), lambda i, info: (i, 0, 0)),
            ]
            + [whole((rows, 256))] * 4,
            scratch_shapes=[
                pltpu.VMEM((128, length), BF16),
                pltpu.VMEM((128, GROUP * rows), F32),
                pltpu.VMEM((1, GROUP * rows), F32),
            ],
        ),
        out_shape=[
            jax.ShapeDtypeStruct((span, 256), BF16),
            jax.ShapeDtypeStruct((steps, 1, GROUP * rows), F32),
        ]
        + [jax.ShapeDtypeStruct((rows, 256), BF16)] * 4,
        compiler_params=vmem(48),
        cost_estimate=cost(18),
        name="attend",
    )(info, queries, kv_all)

    gate_up_w = gather_all(gate_up_low)
    down_w = gather_all(down_low)
    output_w = gather_width(after(output_near, queries), attended, attended)

    back_near = jnp.stack(after([back_low] + back_parts, output_w[1]), axis=0)
    back_w = lax.all_gather(back_near, ("dp", "seq"), axis=1, tiled=True)
    back_w = back_w.reshape(4, 4, QUARTER, 384)

    att_parts = after(swap_high(att_pieces), dy)
    out_keep, out_send = pl.pallas_call(
        out_kernel,
        grid_spec=pltpu.PrefetchScalarGridSpec(
            num_scalar_prefetch=1,
            grid=(1,),
            in_specs=[whole((rows, 256))] * 4 + [whole((4, QUARTER, 256))] * 4,
            out_specs=[whole((block, D))] * 2,
            scratch_shapes=[pltpu.VMEM((rows, QUARTER), F32)],
        ),
        out_shape=[jax.ShapeDtypeStruct((block, D), F32), jax.ShapeDtypeStruct((block, D), BF16)],
        compiler_params=vmem(48),
        cost_estimate=cost(3.8),
        name="attention_out",
    )(info, *att_parts, *output_w)
    out_got = swap_tensor(out_send, 1)
    own_rows = pl.BlockSpec((block, D), lambda i, info: (info[AT_TENSOR], 0))
    resid_one, low_a, low_b = pl.pallas_call(
        norm_kernel,
        grid_spec=pltpu.PrefetchScalarGridSpec(
            num_scalar_prefetch=1,
            grid=(1,),
            in_specs=[whole((block, D))] * 2 + [own_rows, whole((8, D))],
            out_specs=[whole((block, D)), whole((half_block, D)), whole((half_block, D))],
        ),
        out_shape=[
            jax.ShapeDtypeStruct((block, D), F32),
            jax.ShapeDtypeStruct((half_block, D), BF16),
            jax.ShapeDtypeStruct((half_block, D), BF16),
        ],
        cost_estimate=cost(3.5),
        name="second_norm",
    )(info, out_keep, out_got, token_rows, gains)

    def mlp(chunk, near, far, before):
        n = half_span
        anywhere = pl.BlockSpec(memory_space=pl.ANY)
        late_columns = pl.BlockSpec(
            (4, half_block, QUARTER), lambda i, info: (0, 0, jnp.maximum(i - 4, 0))
        )
        late_half = pl.BlockSpec((n // 2, QUARTER), lambda i, info: (0, jnp.maximum(i - 4, 0)))
        return pl.pallas_call(
            mlp_kernel,
            grid_spec=pltpu.PrefetchScalarGridSpec(
                num_scalar_prefetch=1,
                grid=(8,),
                in_specs=[whole((n // 2, D))] * 2
                + [pl.BlockSpec((1, n, D), lambda i, info: (chunk, 0, 0))]
                + [anywhere] * (2 + len(before)),
                out_specs=[
                    late_columns,
                    late_columns,
                    late_half,
                    late_half,
                    pl.BlockSpec((n, 1024), lambda i, info: (chunk, 0)),
                    pl.BlockSpec((n, 2048), lambda i, info: (chunk, 0)),
                    pl.BlockSpec((n, D), lambda i, info: (chunk, 0)),
                ],
                scratch_shapes=[
                    pltpu.VMEM((D, 2048), BF16),
                    pltpu.VMEM((D, 1024), BF16),
                    pltpu.SemaphoreType.DMA((4, 3)),
                ],
            ),
            out_shape=[
                jax.ShapeDtypeStruct((4, half_block, D), BF16),
                jax.ShapeDtypeStruct((4, half_block, D), BF16),
                jax.ShapeDtypeStruct((n // 2, D), BF16),
                jax.ShapeDtypeStruct((n // 2, D), BF16),
                jax.ShapeDtypeStruct((span, 1024), BF16),
                jax.ShapeDtypeStruct((span, 2048), BF16),
                jax.ShapeDtypeStruct((span, D), BF16),
            ],
            input_output_aliases={6: 4, 7: 5, 8: 6} if before else {},
            compiler_params=vmem(56),
            cost_estimate=cost(22.5),
            name="mlp",
        )(info, near, far, dy, gate_up_w, down_w, *before)

    near_a = gather_near(low_a)
    near_b = gather_near(low_b)
    far_a = after(swap_tensor(near_a, 1), near_b)
    far_b = swap_tensor(near_b, 1)
    mlp_keep_a, mlp_send_a, two_keep_a, two_send_a, hidden, gate_up_back, x = mlp(
        0, near_a, far_a, ()
    )
    two_got_a = swap_tensor(two_send_a, 1)
    mlp_keep_b, mlp_send_b, two_keep_b, two_send_b, hidden, gate_up_back, x = mlp(
        1, near_b, far_b, (hidden, gate_up_back, x)
    )
    two_got_b = swap_tensor(two_send_b, 1)
    total_a = two_keep_a.astype(F32) + after(two_got_a, two_send_b).astype(F32)
    two_a = scatter_parts(total_a)
    hidden, gate_up_back = after((hidden, gate_up_back), total_a)
    down_full = weight_full(dy.reshape(span, D), hidden)
    gate_up_full = weight_full(x, gate_up_back)
    total_b = two_keep_b.astype(F32) + after(
        two_got_b, (down_full, gate_up_full, two_a)
    ).astype(F32)
    two_b = scatter_parts(total_b)
    down_grad, gate_up_grad = (scatter_all(full) for full in after((down_full, gate_up_full), total_b))
    mlp_got_a = swap_tensor(after(mlp_send_a, total_b), 1)

    resid_grad, resid_low, gain_two_grad = pl.pallas_call(
        norm_back_kernel,
        grid_spec=pltpu.PrefetchScalarGridSpec(
            num_scalar_prefetch=1,
            grid=(1,),
            in_specs=[whole((half_block, D))] * 8
            + [
                whole((block, D)),
                pl.BlockSpec((2, half_block, D), lambda i, info: (0, 0, 0)),
                whole((8, D)),
            ],
            out_specs=[whole((block, D)), whole((block, D)), whole((1, D))],
        ),
        out_shape=[
            jax.ShapeDtypeStruct((block, D), F32),
            jax.ShapeDtypeStruct((block, D), BF16),
            jax.ShapeDtypeStruct((1, D), F32),
        ],
        cost_estimate=cost(4.7),
        name="second_norm_back",
    )(info, *two_a, *two_b, resid_one, dy, gains)
    resid_other = swap_tensor(resid_low, 1)
    mlp_total_a = (mlp_keep_a.astype(F32) + after(mlp_got_a, resid_low).astype(F32)).astype(BF16)
    mlp_parts_a = lax.all_to_all(mlp_total_a, "tensor", 0, 0, axis_index_groups=HIGH_GROUPS)
    resid_other = after(resid_other, mlp_total_a)
    mlp_got_b = swap_tensor(after(mlp_send_b, resid_other), 1)
    resid_both, *grad_pieces = pl.pallas_call(
        out_back_kernel,
        grid_spec=pltpu.PrefetchScalarGridSpec(
            num_scalar_prefetch=1,
            grid=(1,),
            in_specs=[whole((block, D))] * 2 + [whole((4, QUARTER, 256))] * 4,
            out_specs=[whole((rows, D))] + [whole((rows, 256))] * 4,
        ),
        out_shape=[jax.ShapeDtypeStruct((rows, D), BF16)]
        + [jax.ShapeDtypeStruct((rows, 256), BF16)] * 4,
        compiler_params=vmem(48),
        cost_estimate=cost(3.9),
        name="attention_out_back",
    )(info, resid_low, resid_other, *output_w)
    grad_parts = swap_high(grad_pieces)
    mlp_total_b = (mlp_keep_b.astype(F32) + after(mlp_got_b, grad_parts).astype(F32)).astype(BF16)
    mlp_parts_b = lax.all_to_all(mlp_total_b, "tensor", 0, 0, axis_index_groups=HIGH_GROUPS)
    grad_parts = after(grad_parts, (mlp_total_b, down_grad, back_w))

    spans = seq_size if fast else length // span
    dq, *dq_pieces, dkv = pl.pallas_call(
        functools.partial(attend_back_kernel, rows, keys, spans),
        grid_spec=pltpu.PrefetchScalarGridSpec(
            num_scalar_prefetch=1,
            grid=(steps,),
            in_specs=[pl.BlockSpec((rows, 256), lambda i, info: (i, 0))]
            + [whole((rows, 256))] * 4
            + [
                pl.BlockSpec((rows, 256), lambda i, info: (i, 0)),
                pl.BlockSpec((1, 1, GROUP * rows), lambda i, info: (i, 0, 0)),
                whole((length, 128)),
                pl.BlockSpec((rows, 128), lambda i, info: (i, 0)),
                pl.BlockSpec((rows, 128), lambda i, info: (i, 0)),
            ],
            out_specs=[pl.BlockSpec((rows, 256), lambda i, info: (i, 0))]
            + [whole((rows, 256))] * 4
            + [whole((spans, span, 128))],
            scratch_shapes=[
                pltpu.VMEM((HEAD_DIM, length), BF16),
                pltpu.VMEM((length, 128), F32),
                pltpu.VMEM((HEAD_DIM, GROUP * rows), F32),
                pltpu.VMEM((rows, 256), BF16),
            ],
        ),
        out_shape=[jax.ShapeDtypeStruct((span, 256), BF16)]
        + [jax.ShapeDtypeStruct((rows, 256), BF16)] * 4
        + [jax.ShapeDtypeStruct((spans, span, 128), BF16)],
        compiler_params=vmem(48),
        cost_estimate=cost(23),
        name="attend_back",
    )(info, queries, *grad_parts, attended, logs, kv_all, cosine, sine)

    if fast:
        dkv_own, dkv_more = dkv[0], swap_seq(dkv[1])
    else:
        dkv_own = lax.psum_scatter(dkv.reshape(length, 128), "seq", scatter_dimension=0, tiled=True)
        dkv_more = jnp.zeros_like(dkv_own)
    dq_parts = swap_high(dq_pieces)
    dkv_more = after(dkv_more, dq_parts)
    dkv_low, *dkv_pieces = pl.pallas_call(
        kv_back_kernel,
        grid_spec=pltpu.PrefetchScalarGridSpec(
            num_scalar_prefetch=1,
            grid=(1,),
            in_specs=[whole((span, 128))] * 4,
            out_specs=[whole((span, 128))] + [whole((rows, 128))] * 4,
        ),
        out_shape=[jax.ShapeDtypeStruct((span, 128), BF16)]
        + [jax.ShapeDtypeStruct((rows, 128), BF16)] * 4,
        cost_estimate=cost(3.2),
        name="kv_back",
    )(info, dkv_own, dkv_more, cosine, sine)

    dkv_parts = swap_high(dkv_pieces)
    block_low = pl.pallas_call(
        block_out_kernel,
        out_shape=jax.ShapeDtypeStruct((block, D), BF16),
        cost_estimate=cost(3),
        name="block_out",
    )(*after((mlp_parts_a, mlp_parts_b), dkv_low), resid_one)
    dkv_parts = after(dkv_parts, (gate_up_grad, block_low))
    one_keep, one_send = pl.pallas_call(
        one_kernel,
        grid_spec=pltpu.PrefetchScalarGridSpec(
            num_scalar_prefetch=1,
            grid=(1,),
            in_specs=[whole((rows, 256))] * 4
            + [whole((rows, 128))] * 4
            + [whole((4, 4, QUARTER, 384))],
            out_specs=[whole((block, D))] * 2,
            scratch_shapes=[pltpu.VMEM((rows, QUARTER), F32)],
        ),
        out_shape=[jax.ShapeDtypeStruct((block, D), F32), jax.ShapeDtypeStruct((block, D), BF16)],
        compiler_params=vmem(48),
        cost_estimate=cost(5.8),
        name="attention_in_back",
    )(info, *dq_parts, *dkv_parts, back_w)
    one_got = swap_tensor(one_send, 1)
    dqkv = after(jnp.concatenate([dq, dkv_low], axis=1), one_send)
    attn_halves = weight_halves(normed_one, dqkv)
    out_halves = weight_halves(
        after(resid_both, one_send), jnp.concatenate(att_parts, axis=1)
    )

    block_near = lax.all_gather(block_low, "tensor", axis=0, axis_index_groups=HIGH_GROUPS)
    one_got = after(one_got, (attn_halves, out_halves))
    out_near = scatter_near(out_halves, one_got)
    out_far = send_far(out_near)

    tokens_low = pl.pallas_call(
        tokens_back_kernel,
        grid_spec=pltpu.PrefetchScalarGridSpec(
            num_scalar_prefetch=1,
            grid=(1,),
            in_specs=[whole((block, D))] * 2 + [own_rows, whole((block, D)), whole((8, D))],
            out_specs=whole((block, D)),
        ),
        out_shape=jax.ShapeDtypeStruct((block, D), BF16),
        cost_estimate=cost(4.3),
        name="first_norm_back",
    )(info, one_keep, one_got, token_rows, resid_grad, gains)
    tokens_near = lax.all_gather(tokens_low, "tensor", axis=0, axis_index_groups=HIGH_GROUPS)

    attn_near = scatter_near(attn_halves, one_send)
    attn_far = send_far(attn_near)

    def adam(weight, one, two, terms, rate, decay):
        size = weight.shape[0] // 4
        if weight.ndim == 3:
            mine = pl.BlockSpec((size, 2, weight.shape[2]), lambda i: (i, 0, 0))
            wide = 2 * weight.shape[2]
        else:
            mine = pl.BlockSpec((size, weight.shape[1]), lambda i: (i, 0))
            wide = weight.shape[1]
        return pl.pallas_call(
            functools.partial(adam_kernel, rate, decay),
            grid=(4,),
            in_specs=[mine] * 3
            + [
                pl.BlockSpec((size, wide), lambda i, column=column: (i, column))
                for term, column in terms
            ],
            out_specs=[mine] * 3,
            out_shape=[jax.ShapeDtypeStruct(weight.shape, F32)] * 3,
            compiler_params=vmem(56),
            cost_estimate=cost(weight.size / 75000),
            name="adam",
        )(weight, one, two, *[term for term, column in terms])

    fan_in = RATE_FACTOR * D ** (-0.5)
    gate_up_grad, down_grad = after((gate_up_grad, down_grad), tokens_low)
    gate_up_new = adam(
        gate_up_weight, gate_up_first, gate_up_second, [(gate_up_grad, 0)], fan_in, DECAY
    )
    down_new = adam(
        down_weight, down_first, down_second, [(down_grad, 0)], RATE_FACTOR * FF ** (-0.5), DECAY
    )

    products = jnp.concatenate(
        [
            jnp.sum(
                attn_halves[i // 2][(i % 2) * QUARTER : (i % 2 + 1) * QUARTER].astype(F32)
                * w[:, :384].astype(F32),
                axis=1,
            )
            / w[:, 384].astype(F32)
            for i, w in enumerate(attn_w)
        ]
    )
    gain_grads = jnp.stack(
        [
            products,
            jnp.concatenate(
                [lax.dynamic_slice(gain_two_grad[0], (info[i] * QUARTER,), (QUARTER,)) for i in range(4)]
            ),
        ]
    )
    if fast:
        gain_grads = gain_grads[:, : 2 * QUARTER] + swap_seq(gain_grads[:, 2 * QUARTER :])
        gains_grad = gain_grads[:, :QUARTER] + swap_dp(gain_grads[:, QUARTER:])
    else:
        shard = norm_gains.shape[0]
        gains_grad = lax.dynamic_slice(
            lax.psum(gain_grads, ("dp", "seq")),
            (0, (dp_id * seq_size + seq_id) * shard),
            (2, shard),
        )
    gains_grad = gains_grad + swap_tensor(gains_grad, 1)
    block_far = swap_tensor(after(block_near, gains_grad), 1)
    tokens_near = after(tokens_near, (gate_up_new, down_new, block_far, gains_grad))
    tokens_far = swap_tensor(tokens_near, 1)

    attn_terms = after(scatter_far(attn_near, attn_far), tokens_near)
    query_new = adam(
        query_weight, query_first, query_second, [(term, 0) for term in attn_terms], fan_in, DECAY
    )
    kv_new = adam(kv_weight, kv_first, kv_second, [(term, 2) for term in attn_terms], fan_in, DECAY)

    out_terms = scatter_far(out_near, out_far)
    out_rows = sum(term[: out_terms[-1].shape[0]].astype(F32) for term in after(out_terms, tokens_near))
    output_terms = swap_high([out_rows[:, k * 256 : (k + 1) * 256].astype(BF16) for k in range(4)])
    output_new = adam(
        output_weight,
        output_first,
        output_second,
        [(term, 0) for term in output_terms],
        RATE_FACTOR * FAN_OUT ** (-0.5),
        DECAY,
    )

    gains_grad = after(gains_grad, tokens_near)
    for mask in (2, 4):
        gains_grad = gains_grad + swap_tensor(gains_grad, mask)
    gains_grad = gains_grad.T
    gains_new = adam_step(norm_gains, gains_grad, gains_first, gains_second, GAIN_RATE, 0.0)


    def place(parts, dtype, name):
        return pl.pallas_call(
            place_kernel,
            grid_spec=pltpu.PrefetchScalarGridSpec(
                num_scalar_prefetch=1,
                grid=(4,),
                in_specs=[pl.BlockSpec((1, block, D), lambda i, info: (i, 0, 0))] * 2,
                out_specs=pl.BlockSpec((rows, D), lambda i, info: (i, 0)),
            ),
            out_shape=jax.ShapeDtypeStruct((span, D), dtype),
            compiler_params=vmem(48),
            cost_estimate=cost(5),
            name=name,
        )(info, *parts).reshape(tokens.shape)

    tokens_grad = place((tokens_near, tokens_far), F32, "tokens_grad")
    block_out = place((block_near, block_far), BF16, "block_out_rows")

    results = (query_new, output_new, kv_new, gate_up_new, down_new, gains_new)
    return (block_out, tokens_grad) + tuple(r[i] for i in range(3) for r in results)


def solution(mesh):
    wide = P(("dp", "seq"), "tensor")
    weights = (wide, wide, wide, P(("dp", "seq"), None, "tensor"), wide, P(("dp", "seq"), None))
    rows = P("dp", "seq", None)
    return jax.shard_map(
        functools.partial(body, dp_size=mesh.shape["dp"], seq_size=mesh.shape["seq"]),
        mesh=mesh,
        in_specs=(rows, rows) + weights * 3,
        out_specs=(rows, rows) + weights * 3,
        check_vma=False,
    )
```

```python
import functools

import jax
import jax.numpy as jnp
from jax import lax
from jax.experimental import pallas as pl
from jax.experimental.pallas import tpu as pltpu
from jax.sharding import PartitionSpec as P

D = 2048
FF = 8192
HEADS = 32
KV_HEADS = 8
HEAD_DIM = 64
STEP = 10
FAN_OUT = 2

EPS_NORM = 1e-05
ROPE_BASE = 500000.0
BETA_ONE = 0.9
BETA_TWO = 0.95
ADAM_EPS = 1e-08
DECAY = 0.1
RATE_FACTOR = 3.0
GAIN_RATE = 1.0
MASKED = -1e30

F32 = jnp.float32
BF16 = jnp.bfloat16
GROUP = HEADS // KV_HEADS
QUARTER = D // 4
ORDER = (0, 2, 4, 6, 1, 3, 5, 7)
WIDTH_ORDER = (0, 2, 1, 3)
HIGH_GROUPS = [[0, 2, 4, 6], [1, 3, 5, 7]]
AT_TENSOR, AT_OFFSET, AT_SEQ, AT_LOW, AT_HIGH = 4, 5, 6, 7, 8


def vmem(mib):
    return pltpu.CompilerParams(vmem_limit_bytes=mib * 1024 * 1024)


COST_SCALE = 0.5


def cost(us):
    return pl.CostEstimate(flops=0, bytes_accessed=int(COST_SCALE * us * 3.69e6), transcendentals=0)


def dot(a, b):
    return lax.dot_general(a, b, (((1,), (0,)), ((), ())), preferred_element_type=F32)


def dot_nt(a, b):
    return lax.dot_general(a, b, (((1,), (1,)), ((), ())), preferred_element_type=F32)


def swap_halves(values):
    lane = lax.broadcasted_iota(jnp.int32, values.shape, 1)
    half = HEAD_DIM // 2
    return jnp.where(
        lane % HEAD_DIM < half,
        pltpu.roll(values, 128 - half, 1),
        pltpu.roll(values, half, 1),
    )


def width_block(info, place):
    return pl.ds(pl.multiple_of(info[place] * QUARTER, QUARTER), QUARTER)


def project_kernel(info, tok, w0, w1, w2, w3, cosine, sine, normed, q_out, kv_out, gains, gain_rows):
    pieces = (w0, w1, w2, w3)

    @pl.when(pl.program_id(0) == 0)
    def _():
        for place, piece in enumerate(pieces):
            turned = piece[:, 384:512].astype(F32).T
            gain_rows[:, place * QUARTER : (place + 1) * QUARTER] = turned[0:8]
        natural_store(info, gains, gain_rows[...])

    parts = [tok[:, width_block(info, place)].astype(F32) for place in range(4)]
    square = sum(jnp.sum(part * part, axis=1, keepdims=True) for part in parts)
    inverse = lax.rsqrt(square * (1.0 / D) + EPS_NORM)
    total = None
    for place, (part, piece) in enumerate(zip(parts, pieces)):
        cols = slice(place * QUARTER, (place + 1) * QUARTER)
        low = (part * inverse * gain_rows[0:1, cols]).astype(BF16)
        normed[:, cols] = low
        term = dot(low, piece[:, 0:384])
        total = term if total is None else total + term
    cos, sin = cosine[...], sine[...]
    for c in (0, 128):
        raw = total[:, c : c + 128]
        q_out[:, c : c + 128] = (raw * cos + swap_halves(raw) * sin).astype(BF16)
    raw = total[:, 256:384]
    turned = raw * cos + swap_halves(raw) * sin
    lane = lax.broadcasted_iota(jnp.int32, raw.shape, 1)
    kv_out[...] = jnp.where(lane < HEAD_DIM, turned, raw).astype(BF16)


def heads_wide(turned):
    return jnp.concatenate(
        [turned[h * HEAD_DIM : (h + 1) * HEAD_DIM] for h in range(GROUP)], axis=1
    )


def heads_tall(wide, rows):
    return jnp.concatenate([wide[:, h * rows : (h + 1) * rows] for h in range(GROUP)], axis=0)


def diagonal_mask(rows, keys, shift):
    key = lax.broadcasted_iota(jnp.int32, (keys, GROUP * rows), 0)
    query = lax.broadcasted_iota(jnp.int32, (keys, GROUP * rows), 1) % rows
    return key <= query + shift


def diagonal_block(rows, keys, step, info):
    start = info[AT_OFFSET] + step
    ratio = keys // rows
    diagonal = lax.div(start, jnp.int32(ratio))
    return diagonal, (start - diagonal * ratio) * rows


def attend_kernel(
    rows, keys, info, q, kv, out, log_out, kv_turned, acc, high
):
    step = pl.program_id(0)

    @pl.when(step == 0)
    def _():
        turned = kv[...].T
        row = lax.broadcasted_iota(jnp.int32, turned.shape, 0)
        kv_turned[...] = jnp.where(row < HEAD_DIM, jnp.ones_like(turned), turned)

    wide = heads_wide((q[...] * (HEAD_DIM**-0.5)).astype(F32).T).astype(BF16)
    wide = jnp.concatenate([wide, jnp.zeros_like(wide)], axis=0)
    diagonal, shift = diagonal_block(rows, keys, step, info)

    def scores_of(j):
        return dot(kv[pl.ds(pl.multiple_of(j * keys, keys), keys), :], wide)

    def values_of(j):
        return kv_turned[:, pl.ds(pl.multiple_of(j * keys, keys), keys)]

    scores = jnp.where(diagonal_mask(rows, keys, shift), scores_of(diagonal), MASKED)
    top = jnp.max(scores, axis=0, keepdims=True)
    high[...] = top
    acc[...] = dot(values_of(diagonal), jnp.exp(scores - top).astype(BF16))

    def body(j, carry):
        scores = scores_of(j)
        old = high[...]
        top = jnp.maximum(old, jnp.max(scores, axis=0, keepdims=True))
        high[...] = top
        chances = jnp.exp(scores - top).astype(BF16)
        acc[...] = acc[...] * jnp.exp(old - top) + dot(values_of(j), chances)
        return carry

    lax.fori_loop(0, diagonal, body, 0)
    total = acc[0:1, :]
    log_out[0] = high[...] + jnp.log(total)
    result = acc[HEAD_DIM:, :] * (1.0 / total)
    out[...] = heads_tall(result, rows).T.astype(BF16)


def attend_back_kernel(
    rows, keys, spans, info, q, grad0, grad1, grad2, grad3, att, log_in, kv, cosine, sine,
    dq_out, piece0, piece1, piece2, piece3, dkv_out, kv_turned, dkv, dq_acc, grad,
):
    step = pl.program_id(0)

    @pl.when(step == 0)
    def _():
        kv_turned[...] = kv[...].T[0:HEAD_DIM]
        dkv[...] = jnp.zeros_like(dkv)

    for k, piece in enumerate((grad0, grad1, grad2, grad3)):

        @pl.when(lax.bitwise_xor(step, info[AT_HIGH]) == k)
        def _():
            grad[...] = piece[...]

    scaled = q[...] * (HEAD_DIM**-0.5)
    grads = grad[...]
    zero_tall = jnp.zeros((GROUP * rows, HEAD_DIM), BF16)
    q_tall = jnp.concatenate(
        [scaled[:, h * HEAD_DIM : (h + 1) * HEAD_DIM] for h in range(GROUP)], axis=0
    ).astype(BF16)
    g_tall = jnp.concatenate(
        [grads[:, h * HEAD_DIM : (h + 1) * HEAD_DIM] for h in range(GROUP)], axis=0
    )
    q_tall = jnp.concatenate([q_tall, zero_tall], axis=1)
    g_tall = jnp.concatenate([zero_tall, g_tall], axis=1)
    q_wide = heads_wide(scaled.astype(F32).T).astype(BF16)
    g_turned = grads.astype(F32).T
    g_wide = heads_wide(g_turned).astype(BF16)
    zero_wide = jnp.zeros_like(g_wide)
    product = heads_wide(g_turned * att[...].astype(F32).T)
    delta = jnp.sum(product, axis=0, keepdims=True)
    q_wide = jnp.concatenate([q_wide, zero_wide], axis=0)
    g_wide = jnp.concatenate([zero_wide, g_wide], axis=0)
    logs = log_in[0]
    diagonal, shift = diagonal_block(rows, keys, step, info)

    def one_block(j, mask):
        place = pl.ds(pl.multiple_of(j * keys, keys), keys)
        block = kv[place, :]
        chances = jnp.exp(dot(block, q_wide) - logs)
        if mask is not None:
            chances = jnp.where(mask, chances, 0.0)
        chance_grad = dot(block, g_wide)
        score_grad = (chances * (chance_grad - delta)).astype(BF16)
        dkv[place, :] += dot(score_grad, q_tall) + dot(chances.astype(BF16), g_tall)
        return dot(kv_turned[:, place], score_grad)

    dq_acc[...] = one_block(diagonal, diagonal_mask(rows, keys, shift))

    def body(j, carry):
        dq_acc[...] += one_block(j, None)
        return carry

    lax.fori_loop(0, diagonal, body, 0)
    dq = heads_tall(dq_acc[...] * (HEAD_DIM**-0.5), rows).T
    cos, sin = cosine[...], sine[...]
    for c in (0, 128):
        raw = dq[:, c : c + 128]
        dq_out[:, c : c + 128] = (raw * cos - swap_halves(raw) * sin).astype(BF16)
    for k, piece in enumerate((piece0, piece1, piece2, piece3)):

        @pl.when(lax.bitwise_xor(step, info[AT_HIGH]) == k)
        def _():
            piece[...] = dq_out[...]

    @pl.when(step == pl.num_programs(0) - 1)
    def _():
        span = dkv_out.shape[1]
        for r in range(spans):
            at = lax.bitwise_xor(info[AT_SEQ], jnp.int32(r)) * span
            dkv_out[r] = dkv[pl.ds(pl.multiple_of(at, span), span), :].astype(BF16)


def out_kernel(info, att, w0, w1, w2, w3, keep, send, total):
    half = keep.shape[0]
    low = info[AT_LOW]
    for place, w in enumerate((w0, w1, w2, w3)):
        cols = width_block(info, place)
        total[...] = sum(dot_nt(att[k], w[k]) for k in range(4))
        keep[:, cols] = total[pl.ds(pl.multiple_of(low * half, half), half), :]
        send[:, cols] = total[pl.ds(pl.multiple_of((1 - low) * half, half), half), :].astype(BF16)


def norm_kernel(info, keep, got, tok, gains, resid_out, low_a, low_b):
    resid = tok[...].astype(F32) + keep[...] + got[...].astype(F32)
    resid_out[...] = resid
    inverse = lax.rsqrt(jnp.mean(resid * resid, axis=1, keepdims=True) + EPS_NORM)
    low = (resid * inverse * gains[1:2, :]).astype(BF16)
    half = low.shape[0] // 2
    low_a[...] = low[:half]
    low_b[...] = low[half:]


def mlp_kernel(
    info, near, far, dy, gate_up_all, down_all, *rest,
):
    mlp_keep, mlp_send, two_keep, two_send, hidden_out, grad_out, x, gate_up, down, sems = rest[-10:]
    step = pl.program_id(0)
    wide = FF // 8
    n = x.shape[0]

    def copies(group):
        cols = pl.ds(group * 256, 256)
        up_cols = pl.ds(wide + group * 256, 256)
        for k, (src, dst, c) in enumerate(
            ((gate_up_all, gate_up, cols), (gate_up_all, gate_up, up_cols), (down_all, down, cols))
        ):
            yield pltpu.make_async_copy(src.at[:, c], dst.at[:, c], sems.at[group, k])

    @pl.when(step == 0)
    def _():
        for group in range(4):
            for copy in copies(group):
                copy.start()
        x[: n // 2] = near[...]
        x[n // 2 :] = far[...]

    for group in range(4):

        @pl.when(step == group)
        def _():
            for copy in copies(group):
                copy.wait()
            cols = slice(group * 256, (group + 1) * 256)
            up_cols = slice(wide + group * 256, wide + (group + 1) * 256)
            gate = dot(x[...], gate_up[:, cols])
            up = dot(x[...], gate_up[:, up_cols])
            hidden_grad = dot(dy[0], down[:, cols])
            sigmoid = 1.0 / (1.0 + jnp.exp(-gate))
            silu = gate * sigmoid
            hidden_out[:, cols] = (silu * up).astype(BF16)
            grad_out[:, cols] = (
                hidden_grad * up * (sigmoid * (1.0 + gate * (1.0 - sigmoid)))
            ).astype(BF16)
            grad_out[:, up_cols] = (hidden_grad * silu).astype(BF16)

    @pl.when(step >= 4)
    def _():
        rows = pl.ds(pl.multiple_of((step - 4) * QUARTER, QUARTER), QUARTER)
        two = dot_nt(grad_out[...], gate_up[rows, :]).astype(BF16)
        two_keep[...] = two[: n // 2]
        two_send[...] = two[n // 2 :]
        mlp = dot_nt(hidden_out[...], down[rows, :]).astype(BF16)
        size = n // 8
        for i in range(4):
            owner = lax.bitwise_xor(info[AT_HIGH], jnp.int32(i))
            mlp_keep[owner] = mlp[i * size : (i + 1) * size]
            mlp_send[owner] = mlp[n // 2 + i * size : n // 2 + (i + 1) * size]


def norm_back(values, incoming, gain):
    inverse = lax.rsqrt(jnp.mean(values * values, axis=1, keepdims=True) + EPS_NORM)
    scaled = incoming * gain
    gain_grad = jnp.sum(incoming * values * inverse, axis=0, keepdims=True)
    inner = jnp.mean(scaled * values, axis=1, keepdims=True)
    return inverse * scaled - values * (inverse * inverse * inverse * inner), gain_grad


def summed(parts):
    return sum(part[...].astype(F32) for part in parts)


def norm_back_kernel(info, *refs):
    parts_a, parts_b = refs[0:4], refs[4:8]
    resid, dy, gains, resid_grad, resid_low, gain_grad = refs[8:]
    half = dy.shape[1]
    sums = []
    for i, parts in enumerate((parts_a, parts_b)):
        rows = slice(i * half, (i + 1) * half)
        back, gain_part = norm_back(resid[rows], summed(parts), gains[1:2, :])
        full = dy[i].astype(F32) + back
        resid_grad[rows] = full
        resid_low[rows] = full.astype(BF16)
        sums.append(gain_part)
    gain_grad[...] = sums[0] + sums[1]


def out_back_kernel(info, own, other, w0, w1, w2, w3, both, g0, g1, g2, g3):
    half = own.shape[0]
    low = info[AT_LOW]
    for place in range(4):
        cols = slice(place * QUARTER, (place + 1) * QUARTER)
        natural = width_block(info, place)
        both[pl.ds(pl.multiple_of(low * half, half), half), cols] = own[:, natural]
        both[pl.ds(pl.multiple_of((1 - low) * half, half), half), cols] = other[:, natural]
    for k, out in enumerate((g0, g1, g2, g3)):
        high = lax.bitwise_xor(info[AT_HIGH], jnp.int32(k))
        out[...] = sum(
            dot(both[:, place * QUARTER : (place + 1) * QUARTER], w[high])
            for place, w in enumerate((w0, w1, w2, w3))
        ).astype(BF16)


def natural_store(info, out, value):
    for place in range(4):
        out[:, width_block(info, place)] = value[:, place * QUARTER : (place + 1) * QUARTER]


def kv_back_kernel(info, dkv, dkv_more, cosine, sine, out, p0, p1, p2, p3):
    raw = dkv[...].astype(F32) + dkv_more[...].astype(F32)
    turned = raw * cosine[...] - swap_halves(raw) * sine[...]
    lane = lax.broadcasted_iota(jnp.int32, raw.shape, 1)
    out[...] = jnp.where(lane < HEAD_DIM, turned, raw).astype(BF16)
    rows = p0.shape[0]
    for k, piece in enumerate((p0, p1, p2, p3)):
        at = lax.bitwise_xor(info[AT_HIGH], jnp.int32(k)) * rows
        piece[...] = out[pl.ds(pl.multiple_of(at, rows), rows), :]


def one_kernel(info, q0, q1, q2, q3, k0, k1, k2, k3, w0, w1, w2, w3, keep, send, total):
    half = keep.shape[0]
    low = info[AT_LOW]
    both = [
        jnp.concatenate([q[...], k[...]], axis=1)
        for q, k in zip((q0, q1, q2, q3), (k0, k1, k2, k3))
    ]
    for place, w in enumerate((w0, w1, w2, w3)):
        cols = width_block(info, place)
        total[...] = sum(
            dot_nt(part, w[k]) for k, part in enumerate(both)
        )
        keep[:, cols] = total[pl.ds(pl.multiple_of(low * half, half), half), :]
        send[:, cols] = total[pl.ds(pl.multiple_of((1 - low) * half, half), half), :].astype(BF16)


def tokens_back_kernel(info, keep, got, tok, resid_grad, gains, low):
    back, unused = norm_back(
        tok[...].astype(F32), keep[...] + got[...].astype(F32), gains[0:1, :]
    )
    low[...] = (resid_grad[...] + back).astype(BF16)


def block_out_kernel(parts_a, parts_b, resid, low):
    half = parts_a.shape[1]
    for i, parts in enumerate((parts_a, parts_b)):
        rows = slice(i * half, (i + 1) * half)
        low[rows] = (sum(parts[k].astype(F32) for k in range(4)) + resid[rows]).astype(BF16)


def reorder_kernel(info, src, out):
    half = out.shape[1]
    out[0] = src[:half]
    out[1] = src[half:]


def place_kernel(info, near, far, out):
    size = near.shape[1]
    at = info[AT_LOW] * size
    out[pl.ds(pl.multiple_of(at, size), size), :] = near[0].astype(out.dtype)
    out[pl.ds(pl.multiple_of(size - at, size), size), :] = far[0].astype(out.dtype)


def place_own_kernel(info, near, own, far, out):
    size = near.shape[1]
    at = info[AT_LOW] * size
    out[pl.ds(pl.multiple_of(at, size), size), :] = near[0].astype(out.dtype)
    other = pl.ds(pl.multiple_of(size - at, size), size)

    @pl.when(pl.program_id(0) == 0)
    def _():
        out[other, :] = own[...].astype(out.dtype)

    @pl.when(pl.program_id(0) > 0)
    def _():
        out[other, :] = far[0].astype(out.dtype)


def weight_grad_kernel(a, b, *outs):
    result = lax.dot_general(
        a[...], b[...], (((0,), (0,)), ((), ())), preferred_element_type=F32
    ).astype(BF16)
    if len(outs) == 1:
        outs[0][...] = result
        return

    @pl.when(pl.program_id(0) < 2)
    def _():
        outs[0][...] = result

    @pl.when(pl.program_id(0) >= 2)
    def _():
        outs[1][...] = result


def pair_sum_kernel(a, b, out):
    out[...] = (a[...].astype(F32) + b[...].astype(F32)).astype(BF16)


def adam_kernel(rate, decay, weight, one, two, *refs):
    outs = refs[-3:]
    if len(weight.shape) == 2:
        grad = summed(refs[:-3])
        results = adam_step(weight[...], grad, one[...], two[...], rate, decay)
        for out, result in zip(outs, results):
            out[...] = result
        return
    wide = weight.shape[2]
    for k in range(2):
        cols = slice(k * wide, (k + 1) * wide)
        grad = sum(ref[:, cols].astype(F32) for ref in refs[:-3])
        results = adam_step(weight[:, k, :], grad, one[:, k, :], two[:, k, :], rate, decay)
        for out, result in zip(outs, results):
            out[:, k, :] = result


def step_owner(step):
    return lax.rem(step, 4) * 2 + lax.div(step, 4)


def tensor_block(step, info):
    return lax.bitwise_xor(info[AT_TENSOR], step_owner(step))


def adam_step(weight, grad_sum, moment_one, moment_two, step_rate, decay_rate):
    first_new = BETA_ONE * moment_one + (1.0 - BETA_ONE) * grad_sum
    second_new = BETA_TWO * moment_two + (1.0 - BETA_TWO) * grad_sum * grad_sum
    first_hat = first_new / (1.0 - BETA_ONE**STEP)
    second_hat = second_new / (1.0 - BETA_TWO**STEP)
    updated = weight - step_rate * (
        first_hat / (jnp.sqrt(second_hat) + ADAM_EPS) + decay_rate * weight
    )
    return (updated, first_new, second_new)


def rope_tables(positions):
    half_dim = HEAD_DIM // 2
    exponent = jnp.arange(half_dim, dtype=F32) * (2.0 / HEAD_DIM)
    inverse = jnp.power(F32(ROPE_BASE), -exponent)
    angles = positions.astype(F32)[:, None] * inverse[None, :]
    cosine, sine = jnp.cos(angles), jnp.sin(angles)
    return (
        jnp.concatenate([cosine] * 4, axis=1),
        jnp.concatenate([-sine, sine, -sine, sine], axis=1),
    )


def whole(shape, dims=None):
    zeros = (0,) * len(shape)
    return pl.BlockSpec(shape, lambda *unused: zeros)


def body(
    tokens, cotangent, query_weight, output_weight, kv_weight, gate_up_weight, down_weight, norm_gains,
    query_first, output_first, kv_first, gate_up_first, down_first, gains_first,
    query_second, output_second, kv_second, gate_up_second, down_second, gains_second,
    *, dp_size, seq_size,
):
    fast = dp_size == 2 and seq_size == 2
    span = tokens.shape[1]
    length = span * seq_size
    rows = span // 4
    keys = max(rows, 128)
    block = span // 8
    half_block = block // 2
    tensor_id = lax.axis_index("tensor").astype(jnp.int32)
    seq_id = lax.axis_index("seq").astype(jnp.int32)
    dp_id = lax.axis_index("dp").astype(jnp.int32)
    own_width = dp_id * 2 + seq_id if fast else jnp.int32(0)
    order = WIDTH_ORDER if fast else (0, 1, 2, 3)
    info = jnp.stack(
        [lax.bitwise_xor(own_width, jnp.int32(o)) for o in order]
        + [tensor_id, seq_id * 4, seq_id if fast else jnp.int32(0), tensor_id % 2, tensor_id // 2]
    )

    def by_xor(parts):
        return [
            lax.dynamic_index_in_dim(
                parts, lax.bitwise_xor(info[AT_HIGH], jnp.int32(k)), 0, keepdims=False
            )
            for k in range(4)
        ]

    def others(near):
        return jnp.stack(by_xor(near)[1:], axis=0)

    def after(value, point):
        return lax.optimization_barrier((value, point))[0]

    def swap_tensor(value, mask):
        return lax.ppermute(value, "tensor", [(i, i ^ mask) for i in range(8)])

    def swap_dp(value):
        return lax.ppermute(value, "dp", [(0, 1), (1, 0)])

    def swap_seq(value):
        return lax.ppermute(value, "seq", [(0, 1), (1, 0)])

    def gather_width(shard, point=None, last=None):
        if fast:
            other = swap_dp(shard)
            own = shard
            if last is not None:
                own, other = after(own, point), after(other, last)
            return [shard, other, swap_seq(own), swap_seq(other)]
        axis = shard.ndim - 2
        full = lax.all_gather(shard, ("dp", "seq"), axis=axis, tiled=True)
        return [lax.slice_in_dim(full, i * QUARTER, (i + 1) * QUARTER, axis=axis) for i in range(4)]

    def gather_all(shard):
        return lax.all_gather(shard, ("dp", "seq"), axis=0, tiled=True)

    def scatter_all(full):
        return lax.psum_scatter(full, ("dp", "seq"), scatter_dimension=0, tiled=True)

    def weight_full(a, b, halves=False):
        n, width = b.shape
        if halves:
            specs = [
                pl.BlockSpec((QUARTER, width), lambda i: (jnp.minimum(i, 1), 0)),
                pl.BlockSpec((QUARTER, width), lambda i: (jnp.maximum(i - 2, 0), 0)),
            ]
        else:
            specs = [pl.BlockSpec((QUARTER, width), lambda i: (i, 0))]
        outs = pl.pallas_call(
            weight_grad_kernel,
            grid=(4,),
            in_specs=[pl.BlockSpec((n, QUARTER), lambda i: (0, i)), whole((n, width))],
            out_specs=specs,
            out_shape=[jax.ShapeDtypeStruct((D // len(specs), width), BF16)] * len(specs),
            compiler_params=vmem(56),
            cost_estimate=cost(n * width / 160000),
            name="weight_grad",
        )(a, b)
        return tuple(outs) if halves else outs[0]

    def weight_halves(a, b):
        return weight_full(a, b, True)

    def pair_sum(a, b, place):
        part = pl.BlockSpec((QUARTER, a.shape[1]), lambda i: (place, 0))
        return pl.pallas_call(
            pair_sum_kernel,
            grid=(1,),
            in_specs=[part, part],
            out_specs=whole((QUARTER, a.shape[1])),
            out_shape=jax.ShapeDtypeStruct((QUARTER, a.shape[1]), BF16),
            compiler_params=vmem(48),
            cost_estimate=cost(1.5),
            name="pair_sum",
        )(a, b)

    def scatter_near(halves, point):
        keep, send = halves
        if not fast:
            return keep, send, None
        got = after(swap_seq(send), point)
        return keep, got, pair_sum(keep, got, 1)

    def send_far(near):
        return swap_dp(near[2]) if fast else None

    def scatter_far(near, far):
        keep, got, low = near
        if fast:
            return [keep, got, far]
        full = jnp.concatenate([keep, got], axis=0)
        return [lax.psum_scatter(full, ("dp", "seq"), scatter_dimension=0, tiled=True)]

    def swap_high(pieces):
        return [pieces[0]] + [swap_tensor(pieces[k], 2 * k) for k in (1, 2, 3)]

    def scatter_parts(total):
        n = total.shape[0] // 4
        return [total[:n]] + [
            swap_tensor(total[i * n : (i + 1) * n].astype(BF16), mask)
            for i, mask in ((1, 2), (2, 4), (3, 6))
        ]

    def gather_near(own):
        return jnp.concatenate([own] + [swap_tensor(own, mask) for mask in (2, 4, 6)], axis=0)

    attn_low = jnp.concatenate(
        [query_weight, kv_weight, jnp.pad(norm_gains, ((0, 0), (0, 126)))], axis=1
    ).astype(BF16)
    back_low = jnp.concatenate([query_weight, kv_weight], axis=1).astype(BF16)
    output_low = after(output_weight.astype(BF16), attn_low)
    output_near = lax.all_gather(output_low, "tensor", axis=0, axis_index_groups=HIGH_GROUPS)
    token_rows = tokens.reshape(span, D)
    cot_rows = cotangent.reshape(span, D)
    positions = seq_id * span + jnp.arange(span, dtype=jnp.int32)
    cosine, sine = rope_tables(positions)
    attn_w = gather_width(attn_low, attn_low, (cosine, sine))
    half_span = span // 2
    dy = pl.pallas_call(
        reorder_kernel,
        grid_spec=pltpu.PrefetchScalarGridSpec(
            num_scalar_prefetch=1,
            grid=(8,),
            in_specs=[pl.BlockSpec((block, D), lambda i, info: (tensor_block(i, info), 0))],
            out_specs=pl.BlockSpec((2, half_block, D), lambda i, info: (0, i, 0)),
        ),
        out_shape=jax.ShapeDtypeStruct((2, half_span, D), BF16),
        cost_estimate=cost(7.5),
        name="reorder",
    )(info, cot_rows)

    normed_one, queries, kv_own, gains = pl.pallas_call(
        project_kernel,
        grid_spec=pltpu.PrefetchScalarGridSpec(
            num_scalar_prefetch=1,
            grid=(span // rows,),
            in_specs=[pl.BlockSpec((rows, D), lambda i, info: (i, 0))]
            + [whole((QUARTER, 512))] * 4
            + [pl.BlockSpec((rows, 128), lambda i, info: (i, 0))] * 2,
            out_specs=[
                pl.BlockSpec((rows, D), lambda i, info: (i, 0)),
                pl.BlockSpec((rows, 256), lambda i, info: (i, 0)),
                pl.BlockSpec((rows, 128), lambda i, info: (i, 0)),
                whole((8, D)),
            ],
            scratch_shapes=[pltpu.VMEM((8, D), F32)],
        ),
        out_shape=[
            jax.ShapeDtypeStruct((span, D), BF16),
            jax.ShapeDtypeStruct((span, 256), BF16),
            jax.ShapeDtypeStruct((span, 128), BF16),
            jax.ShapeDtypeStruct((8, D), F32),
        ],
        compiler_params=vmem(48),
        cost_estimate=cost(7),
        name="project",
    )(info, token_rows, *attn_w, cosine, sine)

    gate_up_late, down_late = after((gate_up_weight, down_weight), queries)
    gate_up_low = jnp.concatenate(
        [gate_up_late[:, 0, :], gate_up_late[:, 1, :]], axis=1
    ).astype(BF16)
    down_low = down_late.astype(BF16)

    if fast:
        kv_other = swap_seq(kv_own)
        kv_all = jnp.where(
            seq_id == 0,
            jnp.concatenate([kv_own, kv_other], axis=0),
            jnp.concatenate([kv_other, kv_own], axis=0),
        )
    else:
        kv_all = lax.all_gather(kv_own, "seq", axis=0, tiled=True)

    steps = 4
    attended, logs = pl.pallas_call(
        functools.partial(attend_kernel, rows, max(keys, 2 * rows)),
        grid_spec=pltpu.PrefetchScalarGridSpec(
            num_scalar_prefetch=1,
            grid=(steps,),
            in_specs=[
                pl.BlockSpec((rows, 256), lambda i, info: (i, 0)),
                whole((length, 128)),
            ],
            out_specs=[
                pl.BlockSpec((rows, 256), lambda i, info: (i, 0)),
                pl.BlockSpec((1, 1, GROUP * rows), lambda i, info: (i, 0, 0)),
            ],
            scratch_shapes=[
                pltpu.VMEM((128, length), BF16),
                pltpu.VMEM((128, GROUP * rows), F32),
                pltpu.VMEM((1, GROUP * rows), F32),
            ],
        ),
        out_shape=[
            jax.ShapeDtypeStruct((span, 256), BF16),
            jax.ShapeDtypeStruct((steps, 1, GROUP * rows), F32),
        ],
        compiler_params=vmem(48),
        cost_estimate=cost(18),
        name="attend",
    )(info, queries, kv_all)

    gate_up_w = gather_all(gate_up_low)
    down_w = gather_all(down_low)
    att_parts = lax.all_to_all(
        attended.reshape(4, rows, 256), "tensor", 0, 0, axis_index_groups=HIGH_GROUPS
    )
    att_parts = after(att_parts, dy)
    output_w = gather_width(after(output_near, queries), att_parts, att_parts)

    out_keep, out_send = pl.pallas_call(
        out_kernel,
        grid_spec=pltpu.PrefetchScalarGridSpec(
            num_scalar_prefetch=1,
            grid=(1,),
            in_specs=[whole((4, rows, 256))] + [whole((4, QUARTER, 256))] * 4,
            out_specs=[whole((block, D))] * 2,
            scratch_shapes=[pltpu.VMEM((rows, QUARTER), F32)],
        ),
        out_shape=[jax.ShapeDtypeStruct((block, D), F32), jax.ShapeDtypeStruct((block, D), BF16)],
        compiler_params=vmem(48),
        cost_estimate=cost(3.8),
        name="attention_out",
    )(info, att_parts, *output_w)
    out_got = swap_tensor(out_send, 1)
    own_rows = pl.BlockSpec((block, D), lambda i, info: (info[AT_TENSOR], 0))
    resid_one, low_a, low_b = pl.pallas_call(
        norm_kernel,
        grid_spec=pltpu.PrefetchScalarGridSpec(
            num_scalar_prefetch=1,
            grid=(1,),
            in_specs=[whole((block, D))] * 2 + [own_rows, whole((8, D))],
            out_specs=[whole((block, D)), whole((half_block, D)), whole((half_block, D))],
        ),
        out_shape=[
            jax.ShapeDtypeStruct((block, D), F32),
            jax.ShapeDtypeStruct((half_block, D), BF16),
            jax.ShapeDtypeStruct((half_block, D), BF16),
        ],
        cost_estimate=cost(3.5),
        name="second_norm",
    )(info, out_keep, out_got, token_rows, gains)

    def mlp(chunk, near, far, before):
        n = half_span
        anywhere = pl.BlockSpec(memory_space=pl.ANY)
        late_columns = pl.BlockSpec(
            (4, half_block, QUARTER), lambda i, info: (0, 0, jnp.maximum(i - 4, 0))
        )
        late_half = pl.BlockSpec((n // 2, QUARTER), lambda i, info: (0, jnp.maximum(i - 4, 0)))
        return pl.pallas_call(
            mlp_kernel,
            grid_spec=pltpu.PrefetchScalarGridSpec(
                num_scalar_prefetch=1,
                grid=(8,),
                in_specs=[whole((n // 2, D))] * 2
                + [pl.BlockSpec((1, n, D), lambda i, info: (chunk, 0, 0))]
                + [anywhere] * (2 + len(before)),
                out_specs=[
                    late_columns,
                    late_columns,
                    late_half,
                    late_half,
                    pl.BlockSpec((n, 1024), lambda i, info: (chunk, 0)),
                    pl.BlockSpec((n, 2048), lambda i, info: (chunk, 0)),
                    pl.BlockSpec((n, D), lambda i, info: (chunk, 0)),
                ],
                scratch_shapes=[
                    pltpu.VMEM((D, 2048), BF16),
                    pltpu.VMEM((D, 1024), BF16),
                    pltpu.SemaphoreType.DMA((4, 3)),
                ],
            ),
            out_shape=[
                jax.ShapeDtypeStruct((4, half_block, D), BF16),
                jax.ShapeDtypeStruct((4, half_block, D), BF16),
                jax.ShapeDtypeStruct((n // 2, D), BF16),
                jax.ShapeDtypeStruct((n // 2, D), BF16),
                jax.ShapeDtypeStruct((span, 1024), BF16),
                jax.ShapeDtypeStruct((span, 2048), BF16),
                jax.ShapeDtypeStruct((span, D), BF16),
            ],
            input_output_aliases={6: 4, 7: 5, 8: 6} if before else {},
            compiler_params=vmem(56),
            cost_estimate=cost(22.5),
            name="mlp",
        )(info, near, far, dy, gate_up_w, down_w, *before)

    near_a = gather_near(low_a)
    near_b = gather_near(low_b)
    far_a = after(swap_tensor(near_a, 1), near_b)
    far_b = swap_tensor(near_b, 1)
    mlp_keep_a, mlp_send_a, two_keep_a, two_send_a, hidden, gate_up_back, x = mlp(
        0, near_a, far_a, ()
    )
    two_got_a = swap_tensor(two_send_a, 1)
    back_low = after(back_low, near_b)
    back_parts = [swap_tensor(back_low, mask) for mask in (2, 4, 6)]
    mlp_keep_b, mlp_send_b, two_keep_b, two_send_b, hidden, gate_up_back, x = mlp(
        1, near_b, far_b, (hidden, gate_up_back, x)
    )
    two_got_b = swap_tensor(two_send_b, 1)
    total_a = two_keep_a.astype(F32) + after(two_got_a, two_send_b).astype(F32)
    two_a = scatter_parts(total_a)
    back_near = jnp.stack(after([back_low] + back_parts, two_send_b), axis=0)
    hidden, gate_up_back = after((hidden, gate_up_back), (total_a, back_near))
    down_full = weight_full(dy.reshape(span, D), hidden)
    gate_up_full = weight_full(x, gate_up_back)
    total_b = two_keep_b.astype(F32) + after(
        two_got_b, (down_full, gate_up_full, two_a)
    ).astype(F32)
    two_b = scatter_parts(total_b)
    down_grad, gate_up_grad = (scatter_all(full) for full in after((down_full, gate_up_full), total_b))
    mlp_got_a = swap_tensor(after(mlp_send_a, total_b), 1)

    resid_grad, resid_low, gain_two_grad = pl.pallas_call(
        norm_back_kernel,
        grid_spec=pltpu.PrefetchScalarGridSpec(
            num_scalar_prefetch=1,
            grid=(1,),
            in_specs=[whole((half_block, D))] * 8
            + [
                whole((block, D)),
                pl.BlockSpec((2, half_block, D), lambda i, info: (0, 0, 0)),
                whole((8, D)),
            ],
            out_specs=[whole((block, D)), whole((block, D)), whole((1, D))],
        ),
        out_shape=[
            jax.ShapeDtypeStruct((block, D), F32),
            jax.ShapeDtypeStruct((block, D), BF16),
            jax.ShapeDtypeStruct((1, D), F32),
        ],
        cost_estimate=cost(4.7),
        name="second_norm_back",
    )(info, *two_a, *two_b, resid_one, dy, gains)
    resid_other = swap_tensor(resid_low, 1)
    mlp_total_a = (mlp_keep_a.astype(F32) + after(mlp_got_a, resid_low).astype(F32)).astype(BF16)
    mlp_parts_a = lax.all_to_all(mlp_total_a, "tensor", 0, 0, axis_index_groups=HIGH_GROUPS)
    resid_other = after(resid_other, mlp_total_a)
    mlp_got_b = swap_tensor(after(mlp_send_b, resid_other), 1)
    resid_both, *grad_pieces = pl.pallas_call(
        out_back_kernel,
        grid_spec=pltpu.PrefetchScalarGridSpec(
            num_scalar_prefetch=1,
            grid=(1,),
            in_specs=[whole((block, D))] * 2 + [whole((4, QUARTER, 256))] * 4,
            out_specs=[whole((rows, D))] + [whole((rows, 256))] * 4,
        ),
        out_shape=[jax.ShapeDtypeStruct((rows, D), BF16)]
        + [jax.ShapeDtypeStruct((rows, 256), BF16)] * 4,
        compiler_params=vmem(48),
        cost_estimate=cost(3.9),
        name="attention_out_back",
    )(info, resid_low, resid_other, *output_w)
    grad_parts = swap_high(grad_pieces)
    mlp_total_b = (mlp_keep_b.astype(F32) + after(mlp_got_b, grad_parts).astype(F32)).astype(BF16)
    mlp_parts_b = lax.all_to_all(mlp_total_b, "tensor", 0, 0, axis_index_groups=HIGH_GROUPS)
    back_w = gather_width(back_near, resid_low, resid_low)
    grad_parts = after(grad_parts, (mlp_total_b, down_grad, back_w))

    spans = seq_size if fast else length // span
    dq, *dq_pieces, dkv = pl.pallas_call(
        functools.partial(attend_back_kernel, rows, keys, spans),
        grid_spec=pltpu.PrefetchScalarGridSpec(
            num_scalar_prefetch=1,
            grid=(steps,),
            in_specs=[pl.BlockSpec((rows, 256), lambda i, info: (i, 0))]
            + [whole((rows, 256))] * 4
            + [
                pl.BlockSpec((rows, 256), lambda i, info: (i, 0)),
                pl.BlockSpec((1, 1, GROUP * rows), lambda i, info: (i, 0, 0)),
                whole((length, 128)),
                pl.BlockSpec((rows, 128), lambda i, info: (i, 0)),
                pl.BlockSpec((rows, 128), lambda i, info: (i, 0)),
            ],
            out_specs=[pl.BlockSpec((rows, 256), lambda i, info: (i, 0))]
            + [whole((rows, 256))] * 4
            + [whole((spans, span, 128))],
            scratch_shapes=[
                pltpu.VMEM((HEAD_DIM, length), BF16),
                pltpu.VMEM((length, 128), F32),
                pltpu.VMEM((HEAD_DIM, GROUP * rows), F32),
                pltpu.VMEM((rows, 256), BF16),
            ],
        ),
        out_shape=[jax.ShapeDtypeStruct((span, 256), BF16)]
        + [jax.ShapeDtypeStruct((rows, 256), BF16)] * 4
        + [jax.ShapeDtypeStruct((spans, span, 128), BF16)],
        compiler_params=vmem(48),
        cost_estimate=cost(23),
        name="attend_back",
    )(info, queries, *grad_parts, attended, logs, kv_all, cosine, sine)

    if fast:
        dkv_own, dkv_more = dkv[0], swap_seq(dkv[1])
    else:
        dkv_own = lax.psum_scatter(dkv.reshape(length, 128), "seq", scatter_dimension=0, tiled=True)
        dkv_more = jnp.zeros_like(dkv_own)
    dq_parts = swap_high(dq_pieces)
    dkv_more = after(dkv_more, dq_parts)
    dkv_low, *dkv_pieces = pl.pallas_call(
        kv_back_kernel,
        grid_spec=pltpu.PrefetchScalarGridSpec(
            num_scalar_prefetch=1,
            grid=(1,),
            in_specs=[whole((span, 128))] * 4,
            out_specs=[whole((span, 128))] + [whole((rows, 128))] * 4,
        ),
        out_shape=[jax.ShapeDtypeStruct((span, 128), BF16)]
        + [jax.ShapeDtypeStruct((rows, 128), BF16)] * 4,
        cost_estimate=cost(3.2),
        name="kv_back",
    )(info, dkv_own, dkv_more, cosine, sine)

    dkv_parts = swap_high(dkv_pieces)
    block_low = pl.pallas_call(
        block_out_kernel,
        out_shape=jax.ShapeDtypeStruct((block, D), BF16),
        cost_estimate=cost(3),
        name="block_out",
    )(*after((mlp_parts_a, mlp_parts_b), dkv_low), resid_one)
    dkv_parts = after(dkv_parts, (gate_up_grad, block_low))
    one_keep, one_send = pl.pallas_call(
        one_kernel,
        grid_spec=pltpu.PrefetchScalarGridSpec(
            num_scalar_prefetch=1,
            grid=(1,),
            in_specs=[whole((rows, 256))] * 4
            + [whole((rows, 128))] * 4
            + [whole((4, QUARTER, 384))] * 4,
            out_specs=[whole((block, D))] * 2,
            scratch_shapes=[pltpu.VMEM((rows, QUARTER), F32)],
        ),
        out_shape=[jax.ShapeDtypeStruct((block, D), F32), jax.ShapeDtypeStruct((block, D), BF16)],
        compiler_params=vmem(48),
        cost_estimate=cost(5.8),
        name="attention_in_back",
    )(info, *dq_parts, *dkv_parts, *back_w)
    one_got = swap_tensor(one_send, 1)
    dqkv = after(jnp.concatenate([dq, dkv_low], axis=1), one_send)
    attn_halves = weight_halves(normed_one, dqkv)
    out_halves = weight_halves(
        after(resid_both, one_send), jnp.concatenate(by_xor(att_parts), axis=1)
    )

    block_near = lax.all_gather(block_low, "tensor", axis=0, axis_index_groups=HIGH_GROUPS)
    one_got = after(one_got, (attn_halves, out_halves))
    out_near = scatter_near(out_halves, one_got)
    out_far = send_far(out_near)

    tokens_low = pl.pallas_call(
        tokens_back_kernel,
        grid_spec=pltpu.PrefetchScalarGridSpec(
            num_scalar_prefetch=1,
            grid=(1,),
            in_specs=[whole((block, D))] * 2 + [own_rows, whole((block, D)), whole((8, D))],
            out_specs=whole((block, D)),
        ),
        out_shape=jax.ShapeDtypeStruct((block, D), BF16),
        cost_estimate=cost(4.3),
        name="first_norm_back",
    )(info, one_keep, one_got, token_rows, resid_grad, gains)
    tokens_own = swap_tensor(tokens_low, 1)
    tokens_near = lax.all_gather(tokens_low, "tensor", axis=0, axis_index_groups=HIGH_GROUPS)

    attn_near = scatter_near(attn_halves, one_send)
    attn_far = send_far(attn_near)

    def adam(weight, one, two, terms, rate, decay):
        size = weight.shape[0] // 4
        if weight.ndim == 3:
            mine = pl.BlockSpec((size, 2, weight.shape[2]), lambda i: (i, 0, 0))
            wide = 2 * weight.shape[2]
        else:
            mine = pl.BlockSpec((size, weight.shape[1]), lambda i: (i, 0))
            wide = weight.shape[1]
        return pl.pallas_call(
            functools.partial(adam_kernel, rate, decay),
            grid=(4,),
            in_specs=[mine] * 3
            + [
                pl.BlockSpec((size, wide), lambda i, column=column: (i, column))
                for term, column in terms
            ],
            out_specs=[mine] * 3,
            out_shape=[jax.ShapeDtypeStruct(weight.shape, F32)] * 3,
            compiler_params=vmem(56),
            cost_estimate=cost(weight.size / 75000),
            name="adam",
        )(weight, one, two, *[term for term, column in terms])

    fan_in = RATE_FACTOR * D ** (-0.5)
    gate_up_grad, down_grad = after((gate_up_grad, down_grad), tokens_low)
    gate_up_new = adam(
        gate_up_weight, gate_up_first, gate_up_second, [(gate_up_grad, 0)], fan_in, DECAY
    )
    down_new = adam(
        down_weight, down_first, down_second, [(down_grad, 0)], RATE_FACTOR * FF ** (-0.5), DECAY
    )

    products = jnp.concatenate(
        [
            jnp.sum(
                attn_halves[i // 2][(i % 2) * QUARTER : (i % 2 + 1) * QUARTER].astype(F32)
                * w[:, :384].astype(F32),
                axis=1,
            )
            / w[:, 384].astype(F32)
            for i, w in enumerate(attn_w)
        ]
    )
    gain_grads = jnp.stack(
        [
            products,
            jnp.concatenate(
                [lax.dynamic_slice(gain_two_grad[0], (info[i] * QUARTER,), (QUARTER,)) for i in range(4)]
            ),
        ]
    )
    if fast:
        gain_grads = gain_grads[:, : 2 * QUARTER] + swap_seq(gain_grads[:, 2 * QUARTER :])
        gain_grads = gain_grads + swap_tensor(gain_grads, 1)
    else:
        shard = norm_gains.shape[0]
        gains_grad = lax.dynamic_slice(
            lax.psum(gain_grads, ("dp", "seq")),
            (0, (dp_id * seq_size + seq_id) * shard),
            (2, shard),
        )
        gain_grads = gains_grad + swap_tensor(gains_grad, 1)
    block_far = swap_tensor(after(block_near, (gain_grads, tokens_own)), 1)
    if fast:
        gains_grad = gain_grads[:, :QUARTER] + swap_dp(gain_grads[:, QUARTER:])
    else:
        gains_grad = gain_grads
    early = (gate_up_new, down_new, gains_grad) + ((out_far, attn_far) if fast else ())
    tokens_near = after(tokens_near, early)
    tokens_far = swap_tensor(others(tokens_near), 1)

    attn_terms = after(scatter_far(attn_near, attn_far), tokens_near)
    query_new = adam(
        query_weight, query_first, query_second, [(term, 0) for term in attn_terms], fan_in, DECAY
    )
    kv_new = adam(kv_weight, kv_first, kv_second, [(term, 2) for term in attn_terms], fan_in, DECAY)

    out_terms = scatter_far(out_near, out_far)
    out_rows = sum(term[: out_terms[-1].shape[0]].astype(F32) for term in after(out_terms, tokens_near))
    output_terms = swap_high([out_rows[:, k * 256 : (k + 1) * 256].astype(BF16) for k in range(4)])
    output_new = adam(
        output_weight,
        output_first,
        output_second,
        [(term, 0) for term in output_terms],
        RATE_FACTOR * FAN_OUT ** (-0.5),
        DECAY,
    )

    gains_grad = after(gains_grad, tokens_near)
    for mask in (2, 4):
        gains_grad = gains_grad + swap_tensor(gains_grad, mask)
    gains_grad = gains_grad.T
    gains_new = adam_step(norm_gains, gains_grad, gains_first, gains_second, GAIN_RATE, 0.0)


    def place(parts, dtype, name):
        return pl.pallas_call(
            place_kernel,
            grid_spec=pltpu.PrefetchScalarGridSpec(
                num_scalar_prefetch=1,
                grid=(4,),
                in_specs=[pl.BlockSpec((1, block, D), lambda i, info: (i, 0, 0))] * 2,
                out_specs=pl.BlockSpec((rows, D), lambda i, info: (i, 0)),
            ),
            out_shape=jax.ShapeDtypeStruct((span, D), dtype),
            compiler_params=vmem(48),
            cost_estimate=cost(5),
            name=name,
        )(info, *parts).reshape(tokens.shape)

    def place_own(parts, dtype, name):
        return pl.pallas_call(
            place_own_kernel,
            grid_spec=pltpu.PrefetchScalarGridSpec(
                num_scalar_prefetch=1,
                grid=(4,),
                in_specs=[
                    pl.BlockSpec(
                        (1, block, D), lambda i, info: (lax.bitwise_xor(info[AT_HIGH], i), 0, 0)
                    ),
                    whole((block, D)),
                    pl.BlockSpec((1, block, D), lambda i, info: (jnp.maximum(i - 1, 0), 0, 0)),
                ],
                out_specs=pl.BlockSpec(
                    (rows, D), lambda i, info: (lax.bitwise_xor(info[AT_HIGH], i), 0)
                ),
            ),
            out_shape=jax.ShapeDtypeStruct((span, D), dtype),
            compiler_params=vmem(48),
            cost_estimate=cost(5),
            name=name,
        )(info, *parts).reshape(tokens.shape)

    tokens_grad = place_own((tokens_near, tokens_own, tokens_far), F32, "tokens_grad")
    block_out = place((block_near, block_far), BF16, "block_out_rows")

    results = (query_new, output_new, kv_new, gate_up_new, down_new, gains_new)
    return (block_out, tokens_grad) + tuple(r[i] for i in range(3) for r in results)


def solution(mesh):
    wide = P(("dp", "seq"), "tensor")
    weights = (wide, wide, wide, P(("dp", "seq"), None, "tensor"), wide, P(("dp", "seq"), None))
    rows = P("dp", "seq", None)
    return jax.shard_map(
        functools.partial(body, dp_size=mesh.shape["dp"], seq_size=mesh.shape["seq"]),
        mesh=mesh,
        in_specs=(rows, rows) + weights * 3,
        out_specs=(rows, rows) + weights * 3,
        check_vma=False,
    )
```

```python
import functools

import jax
import jax.numpy as jnp
from jax import lax
from jax.experimental import pallas as pl
from jax.experimental.pallas import tpu as pltpu
from jax.sharding import PartitionSpec as P

D = 2048
FF = 8192
HEADS = 32
KV_HEADS = 8
HEAD_DIM = 64
STEP = 10
FAN_OUT = 2

EPS_NORM = 1e-05
ROPE_BASE = 500000.0
BETA_ONE = 0.9
BETA_TWO = 0.95
ADAM_EPS = 1e-08
DECAY = 0.1
RATE_FACTOR = 3.0
GAIN_RATE = 1.0
MASKED = -1e30

F32 = jnp.float32
BF16 = jnp.bfloat16
GROUP = HEADS // KV_HEADS
QUARTER = D // 4
ORDER = (0, 2, 4, 6, 1, 3, 5, 7)
WIDTH_ORDER = (0, 2, 1, 3)
HIGH_GROUPS = [[0, 2, 4, 6], [1, 3, 5, 7]]
AT_TENSOR, AT_OFFSET, AT_SEQ, AT_LOW, AT_HIGH = 4, 5, 6, 7, 8


def vmem(mib):
    return pltpu.CompilerParams(vmem_limit_bytes=mib * 1024 * 1024)


COST_SCALE = 0.5


def cost(us):
    return pl.CostEstimate(flops=0, bytes_accessed=int(COST_SCALE * us * 3.69e6), transcendentals=0)


def dot(a, b):
    return lax.dot_general(a, b, (((1,), (0,)), ((), ())), preferred_element_type=F32)


def dot_nt(a, b):
    return lax.dot_general(a, b, (((1,), (1,)), ((), ())), preferred_element_type=F32)


def swap_halves(values):
    lane = lax.broadcasted_iota(jnp.int32, values.shape, 1)
    half = HEAD_DIM // 2
    return jnp.where(
        lane % HEAD_DIM < half,
        pltpu.roll(values, 128 - half, 1),
        pltpu.roll(values, half, 1),
    )


def width_block(info, place):
    return pl.ds(pl.multiple_of(info[place] * QUARTER, QUARTER), QUARTER)


def project_kernel(info, tok, w0, w1, w2, w3, cosine, sine, normed, q_out, kv_out, gains, gain_rows):
    pieces = (w0, w1, w2, w3)

    @pl.when(pl.program_id(0) == 0)
    def _():
        for place, piece in enumerate(pieces):
            turned = piece[:, 384:512].astype(F32).T
            gain_rows[:, place * QUARTER : (place + 1) * QUARTER] = turned[0:8]
        natural_store(info, gains, gain_rows[...])

    parts = [tok[:, width_block(info, place)].astype(F32) for place in range(4)]
    square = sum(jnp.sum(part * part, axis=1, keepdims=True) for part in parts)
    inverse = lax.rsqrt(square * (1.0 / D) + EPS_NORM)
    total = None
    for place, (part, piece) in enumerate(zip(parts, pieces)):
        cols = slice(place * QUARTER, (place + 1) * QUARTER)
        low = (part * inverse * gain_rows[0:1, cols]).astype(BF16)
        normed[:, cols] = low
        term = dot(low, piece[:, 0:384])
        total = term if total is None else total + term
    cos, sin = cosine[...], sine[...]
    for c in (0, 128):
        raw = total[:, c : c + 128]
        q_out[:, c : c + 128] = (raw * cos + swap_halves(raw) * sin).astype(BF16)
    raw = total[:, 256:384]
    turned = raw * cos + swap_halves(raw) * sin
    lane = lax.broadcasted_iota(jnp.int32, raw.shape, 1)
    kv_out[...] = jnp.where(lane < HEAD_DIM, turned, raw).astype(BF16)


def heads_wide(turned):
    return jnp.concatenate(
        [turned[h * HEAD_DIM : (h + 1) * HEAD_DIM] for h in range(GROUP)], axis=1
    )


def heads_tall(wide, rows):
    return jnp.concatenate([wide[:, h * rows : (h + 1) * rows] for h in range(GROUP)], axis=0)


def diagonal_mask(rows, keys, shift):
    key = lax.broadcasted_iota(jnp.int32, (keys, GROUP * rows), 0)
    query = lax.broadcasted_iota(jnp.int32, (keys, GROUP * rows), 1) % rows
    return key <= query + shift


def diagonal_block(rows, keys, step, info):
    start = info[AT_OFFSET] + step
    ratio = keys // rows
    diagonal = lax.div(start, jnp.int32(ratio))
    return diagonal, (start - diagonal * ratio) * rows


def attend_kernel(
    rows, keys, info, q, kv, out, log_out, kv_turned, acc, high
):
    step = pl.program_id(0)

    @pl.when(step == 0)
    def _():
        turned = kv[...].T
        row = lax.broadcasted_iota(jnp.int32, turned.shape, 0)
        kv_turned[...] = jnp.where(row < HEAD_DIM, jnp.ones_like(turned), turned)

    wide = heads_wide((q[...] * (HEAD_DIM**-0.5)).astype(F32).T).astype(BF16)
    wide = jnp.concatenate([wide, jnp.zeros_like(wide)], axis=0)
    diagonal, shift = diagonal_block(rows, keys, step, info)

    def scores_of(j):
        return dot(kv[pl.ds(pl.multiple_of(j * keys, keys), keys), :], wide)

    def values_of(j):
        return kv_turned[:, pl.ds(pl.multiple_of(j * keys, keys), keys)]

    scores = jnp.where(diagonal_mask(rows, keys, shift), scores_of(diagonal), MASKED)
    top = jnp.max(scores, axis=0, keepdims=True)
    high[...] = top
    acc[...] = dot(values_of(diagonal), jnp.exp(scores - top).astype(BF16))

    def body(j, carry):
        scores = scores_of(j)
        old = high[...]
        top = jnp.maximum(old, jnp.max(scores, axis=0, keepdims=True))
        high[...] = top
        chances = jnp.exp(scores - top).astype(BF16)
        acc[...] = acc[...] * jnp.exp(old - top) + dot(values_of(j), chances)
        return carry

    lax.fori_loop(0, diagonal, body, 0)
    total = acc[0:1, :]
    log_out[0] = high[...] + jnp.log(total)
    result = acc[HEAD_DIM:, :] * (1.0 / total)
    out[...] = heads_tall(result, rows).T.astype(BF16)


def attend_back_kernel(
    rows, keys, spans, info, q, grad0, grad1, grad2, grad3, att, log_in, kv, cosine, sine,
    dq_out, piece0, piece1, piece2, piece3, dkv_out, kv_turned, dkv, dq_acc, grad,
):
    step = pl.program_id(0)

    @pl.when(step == 0)
    def _():
        kv_turned[...] = kv[...].T[0:HEAD_DIM]
        dkv[...] = jnp.zeros_like(dkv)

    for k, piece in enumerate((grad0, grad1, grad2, grad3)):

        @pl.when(lax.bitwise_xor(step, info[AT_HIGH]) == k)
        def _():
            grad[...] = piece[...]

    scaled = q[...] * (HEAD_DIM**-0.5)
    grads = grad[...]
    zero_tall = jnp.zeros((GROUP * rows, HEAD_DIM), BF16)
    q_tall = jnp.concatenate(
        [scaled[:, h * HEAD_DIM : (h + 1) * HEAD_DIM] for h in range(GROUP)], axis=0
    ).astype(BF16)
    g_tall = jnp.concatenate(
        [grads[:, h * HEAD_DIM : (h + 1) * HEAD_DIM] for h in range(GROUP)], axis=0
    )
    q_tall = jnp.concatenate([q_tall, zero_tall], axis=1)
    g_tall = jnp.concatenate([zero_tall, g_tall], axis=1)
    q_wide = heads_wide(scaled.astype(F32).T).astype(BF16)
    g_turned = grads.astype(F32).T
    g_wide = heads_wide(g_turned).astype(BF16)
    zero_wide = jnp.zeros_like(g_wide)
    product = heads_wide(g_turned * att[...].astype(F32).T)
    delta = jnp.sum(product, axis=0, keepdims=True)
    q_wide = jnp.concatenate([q_wide, zero_wide], axis=0)
    g_wide = jnp.concatenate([zero_wide, g_wide], axis=0)
    logs = log_in[0]
    diagonal, shift = diagonal_block(rows, keys, step, info)

    def one_block(j, mask):
        place = pl.ds(pl.multiple_of(j * keys, keys), keys)
        block = kv[place, :]
        chances = jnp.exp(dot(block, q_wide) - logs)
        if mask is not None:
            chances = jnp.where(mask, chances, 0.0)
        chance_grad = dot(block, g_wide)
        score_grad = (chances * (chance_grad - delta)).astype(BF16)
        dkv[place, :] += dot(score_grad, q_tall) + dot(chances.astype(BF16), g_tall)
        return dot(kv_turned[:, place], score_grad)

    dq_acc[...] = one_block(diagonal, diagonal_mask(rows, keys, shift))

    def body(j, carry):
        dq_acc[...] += one_block(j, None)
        return carry

    lax.fori_loop(0, diagonal, body, 0)
    dq = heads_tall(dq_acc[...] * (HEAD_DIM**-0.5), rows).T
    cos, sin = cosine[...], sine[...]
    for c in (0, 128):
        raw = dq[:, c : c + 128]
        dq_out[:, c : c + 128] = (raw * cos - swap_halves(raw) * sin).astype(BF16)
    for k, piece in enumerate((piece0, piece1, piece2, piece3)):

        @pl.when(lax.bitwise_xor(step, info[AT_HIGH]) == k)
        def _():
            piece[...] = dq_out[...]

    @pl.when(step == pl.num_programs(0) - 1)
    def _():
        span = dkv_out.shape[1]
        for r in range(spans):
            at = lax.bitwise_xor(info[AT_SEQ], jnp.int32(r)) * span
            dkv_out[r] = dkv[pl.ds(pl.multiple_of(at, span), span), :].astype(BF16)


def out_kernel(info, att, w0, w1, w2, w3, keep, send, total):
    half = keep.shape[0]
    low = info[AT_LOW]
    for place, w in enumerate((w0, w1, w2, w3)):
        cols = width_block(info, place)
        total[...] = sum(dot_nt(att[k], w[k]) for k in range(4))
        keep[:, cols] = total[pl.ds(pl.multiple_of(low * half, half), half), :]
        send[:, cols] = total[pl.ds(pl.multiple_of((1 - low) * half, half), half), :].astype(BF16)


def norm_kernel(info, keep, got, tok, gains, resid_out, low_a, low_b):
    resid = tok[...].astype(F32) + keep[...] + got[...].astype(F32)
    resid_out[...] = resid
    inverse = lax.rsqrt(jnp.mean(resid * resid, axis=1, keepdims=True) + EPS_NORM)
    low = (resid * inverse * gains[1:2, :]).astype(BF16)
    half = low.shape[0] // 2
    low_a[...] = low[:half]
    low_b[...] = low[half:]


def mlp_kernel(
    info, near, far, dy, gate_up_all, down_all, *rest,
):
    mlp_keep, mlp_send, two_keep, two_send, hidden_out, grad_out, x, gate_up, down, sems = rest[-10:]
    step = pl.program_id(0)
    wide = FF // 8
    n = x.shape[0]

    def copies(group):
        cols = pl.ds(group * 256, 256)
        up_cols = pl.ds(wide + group * 256, 256)
        for k, (src, dst, c) in enumerate(
            ((gate_up_all, gate_up, cols), (gate_up_all, gate_up, up_cols), (down_all, down, cols))
        ):
            yield pltpu.make_async_copy(src.at[:, c], dst.at[:, c], sems.at[group, k])

    @pl.when(step == 0)
    def _():
        for group in range(4):
            for copy in copies(group):
                copy.start()
        x[: n // 2] = near[...]
        x[n // 2 :] = far[...]

    for group in range(4):

        @pl.when(step == group)
        def _():
            for copy in copies(group):
                copy.wait()
            cols = slice(group * 256, (group + 1) * 256)
            up_cols = slice(wide + group * 256, wide + (group + 1) * 256)
            gate = dot(x[...], gate_up[:, cols])
            up = dot(x[...], gate_up[:, up_cols])
            hidden_grad = dot(dy[0], down[:, cols])
            sigmoid = 1.0 / (1.0 + jnp.exp(-gate))
            silu = gate * sigmoid
            hidden_out[:, cols] = (silu * up).astype(BF16)
            grad_out[:, cols] = (
                hidden_grad * up * (sigmoid * (1.0 + gate * (1.0 - sigmoid)))
            ).astype(BF16)
            grad_out[:, up_cols] = (hidden_grad * silu).astype(BF16)

    @pl.when(step >= 4)
    def _():
        rows = pl.ds(pl.multiple_of((step - 4) * QUARTER, QUARTER), QUARTER)
        two = dot_nt(grad_out[...], gate_up[rows, :]).astype(BF16)
        two_keep[...] = two[: n // 2]
        two_send[...] = two[n // 2 :]
        mlp = dot_nt(hidden_out[...], down[rows, :]).astype(BF16)
        size = n // 8
        for i in range(4):
            owner = lax.bitwise_xor(info[AT_HIGH], jnp.int32(i))
            mlp_keep[owner] = mlp[i * size : (i + 1) * size]
            mlp_send[owner] = mlp[n // 2 + i * size : n // 2 + (i + 1) * size]


def norm_back(values, incoming, gain):
    inverse = lax.rsqrt(jnp.mean(values * values, axis=1, keepdims=True) + EPS_NORM)
    scaled = incoming * gain
    gain_grad = jnp.sum(incoming * values * inverse, axis=0, keepdims=True)
    inner = jnp.mean(scaled * values, axis=1, keepdims=True)
    return inverse * scaled - values * (inverse * inverse * inverse * inner), gain_grad


def summed(parts):
    return sum(part[...].astype(F32) for part in parts)


def norm_back_kernel(info, *refs):
    parts_a, parts_b = refs[0:4], refs[4:8]
    resid, dy, gains, resid_grad, resid_low, gain_grad = refs[8:]
    half = dy.shape[1]
    sums = []
    for i, parts in enumerate((parts_a, parts_b)):
        rows = slice(i * half, (i + 1) * half)
        back, gain_part = norm_back(resid[rows], summed(parts), gains[1:2, :])
        full = dy[i].astype(F32) + back
        resid_grad[rows] = full
        resid_low[rows] = full.astype(BF16)
        sums.append(gain_part)
    gain_grad[...] = sums[0] + sums[1]


def out_back_kernel(info, own, other, w0, w1, w2, w3, both, g0, g1, g2, g3):
    half = own.shape[0]
    low = info[AT_LOW]
    for place in range(4):
        cols = slice(place * QUARTER, (place + 1) * QUARTER)
        natural = width_block(info, place)
        both[pl.ds(pl.multiple_of(low * half, half), half), cols] = own[:, natural]
        both[pl.ds(pl.multiple_of((1 - low) * half, half), half), cols] = other[:, natural]
    for k, out in enumerate((g0, g1, g2, g3)):
        high = lax.bitwise_xor(info[AT_HIGH], jnp.int32(k))
        out[...] = sum(
            dot(both[:, place * QUARTER : (place + 1) * QUARTER], w[high])
            for place, w in enumerate((w0, w1, w2, w3))
        ).astype(BF16)


def natural_store(info, out, value):
    for place in range(4):
        out[:, width_block(info, place)] = value[:, place * QUARTER : (place + 1) * QUARTER]


def kv_back_kernel(info, dkv, dkv_more, cosine, sine, out, p0, p1, p2, p3):
    raw = dkv[...].astype(F32) + dkv_more[...].astype(F32)
    turned = raw * cosine[...] - swap_halves(raw) * sine[...]
    lane = lax.broadcasted_iota(jnp.int32, raw.shape, 1)
    out[...] = jnp.where(lane < HEAD_DIM, turned, raw).astype(BF16)
    rows = p0.shape[0]
    for k, piece in enumerate((p0, p1, p2, p3)):
        at = lax.bitwise_xor(info[AT_HIGH], jnp.int32(k)) * rows
        piece[...] = out[pl.ds(pl.multiple_of(at, rows), rows), :]


def one_kernel(info, q0, q1, q2, q3, k0, k1, k2, k3, w0, w1, w2, w3, keep, send, total):
    half = keep.shape[0]
    low = info[AT_LOW]
    both = [
        jnp.concatenate([q[...], k[...]], axis=1)
        for q, k in zip((q0, q1, q2, q3), (k0, k1, k2, k3))
    ]
    for place, w in enumerate((w0, w1, w2, w3)):
        cols = width_block(info, place)
        total[...] = sum(
            dot_nt(part, w[k]) for k, part in enumerate(both)
        )
        keep[:, cols] = total[pl.ds(pl.multiple_of(low * half, half), half), :]
        send[:, cols] = total[pl.ds(pl.multiple_of((1 - low) * half, half), half), :].astype(BF16)


def tokens_back_kernel(info, keep, got, tok, resid_grad, gains, low):
    back, unused = norm_back(
        tok[...].astype(F32), keep[...] + got[...].astype(F32), gains[0:1, :]
    )
    low[...] = (resid_grad[...] + back).astype(BF16)


def block_out_kernel(parts_a, parts_b, resid, low):
    half = parts_a.shape[1]
    for i, parts in enumerate((parts_a, parts_b)):
        rows = slice(i * half, (i + 1) * half)
        low[rows] = (sum(parts[k].astype(F32) for k in range(4)) + resid[rows]).astype(BF16)


def reorder_kernel(info, src, out):
    half = out.shape[1]
    out[0] = src[:half]
    out[1] = src[half:]


def place_kernel(info, near, far, out):
    size = near.shape[1]
    at = info[AT_LOW] * size
    out[pl.ds(pl.multiple_of(at, size), size), :] = near[0].astype(out.dtype)
    out[pl.ds(pl.multiple_of(size - at, size), size), :] = far[0].astype(out.dtype)


def place_own_kernel(info, near, own, far, out):
    size = near.shape[1]
    at = info[AT_LOW] * size
    out[pl.ds(pl.multiple_of(at, size), size), :] = near[0].astype(out.dtype)
    other = pl.ds(pl.multiple_of(size - at, size), size)

    @pl.when(pl.program_id(0) == 0)
    def _():
        out[other, :] = own[...].astype(out.dtype)

    @pl.when(pl.program_id(0) > 0)
    def _():
        out[other, :] = far[0].astype(out.dtype)


def weight_grad_kernel(a, b, *outs):
    result = lax.dot_general(
        a[...], b[...], (((0,), (0,)), ((), ())), preferred_element_type=F32
    ).astype(BF16)
    if len(outs) == 1:
        outs[0][...] = result
        return

    @pl.when(pl.program_id(0) < 2)
    def _():
        outs[0][...] = result

    @pl.when(pl.program_id(0) >= 2)
    def _():
        outs[1][...] = result


def mlp_grad_kernel(x, gate_up_back, dy, hidden, out):
    for a, b, cols in (
        (x, gate_up_back, slice(0, gate_up_back.shape[1])),
        (dy, hidden, slice(gate_up_back.shape[1], out.shape[1])),
    ):
        out[:, cols] = lax.dot_general(
            a[...], b[...], (((0,), (0,)), ((), ())), preferred_element_type=F32
        ).astype(BF16)


def pair_sum_kernel(a, b, out):
    out[...] = (a[...].astype(F32) + b[...].astype(F32)).astype(BF16)


def adam_kernel(rate, decay, weight, one, two, *refs):
    outs = refs[-3:]
    if len(weight.shape) == 2:
        grad = summed(refs[:-3])
        results = adam_step(weight[...], grad, one[...], two[...], rate, decay)
        for out, result in zip(outs, results):
            out[...] = result
        return
    wide = weight.shape[2]
    for k in range(2):
        cols = slice(k * wide, (k + 1) * wide)
        grad = sum(ref[:, cols].astype(F32) for ref in refs[:-3])
        results = adam_step(weight[:, k, :], grad, one[:, k, :], two[:, k, :], rate, decay)
        for out, result in zip(outs, results):
            out[:, k, :] = result


def step_owner(step):
    return lax.rem(step, 4) * 2 + lax.div(step, 4)


def tensor_block(step, info):
    return lax.bitwise_xor(info[AT_TENSOR], step_owner(step))


def adam_step(weight, grad_sum, moment_one, moment_two, step_rate, decay_rate):
    first_new = BETA_ONE * moment_one + (1.0 - BETA_ONE) * grad_sum
    second_new = BETA_TWO * moment_two + (1.0 - BETA_TWO) * grad_sum * grad_sum
    first_hat = first_new / (1.0 - BETA_ONE**STEP)
    second_hat = second_new / (1.0 - BETA_TWO**STEP)
    updated = weight - step_rate * (
        first_hat / (jnp.sqrt(second_hat) + ADAM_EPS) + decay_rate * weight
    )
    return (updated, first_new, second_new)


def rope_tables(positions):
    half_dim = HEAD_DIM // 2
    exponent = jnp.arange(half_dim, dtype=F32) * (2.0 / HEAD_DIM)
    inverse = jnp.power(F32(ROPE_BASE), -exponent)
    angles = positions.astype(F32)[:, None] * inverse[None, :]
    cosine, sine = jnp.cos(angles), jnp.sin(angles)
    return (
        jnp.concatenate([cosine] * 4, axis=1),
        jnp.concatenate([-sine, sine, -sine, sine], axis=1),
    )


def whole(shape, dims=None):
    zeros = (0,) * len(shape)
    return pl.BlockSpec(shape, lambda *unused: zeros)


def body(
    tokens, cotangent, query_weight, output_weight, kv_weight, gate_up_weight, down_weight, norm_gains,
    query_first, output_first, kv_first, gate_up_first, down_first, gains_first,
    query_second, output_second, kv_second, gate_up_second, down_second, gains_second,
    *, dp_size, seq_size,
):
    fast = dp_size == 2 and seq_size == 2
    span = tokens.shape[1]
    length = span * seq_size
    rows = span // 4
    keys = max(rows, 128)
    block = span // 8
    half_block = block // 2
    tensor_id = lax.axis_index("tensor").astype(jnp.int32)
    seq_id = lax.axis_index("seq").astype(jnp.int32)
    dp_id = lax.axis_index("dp").astype(jnp.int32)
    own_width = dp_id * 2 + seq_id if fast else jnp.int32(0)
    order = WIDTH_ORDER if fast else (0, 1, 2, 3)
    info = jnp.stack(
        [lax.bitwise_xor(own_width, jnp.int32(o)) for o in order]
        + [tensor_id, seq_id * 4, seq_id if fast else jnp.int32(0), tensor_id % 2, tensor_id // 2]
    )

    def by_xor(parts):
        return [
            lax.dynamic_index_in_dim(
                parts, lax.bitwise_xor(info[AT_HIGH], jnp.int32(k)), 0, keepdims=False
            )
            for k in range(4)
        ]

    def others(near):
        return jnp.stack(by_xor(near)[1:], axis=0)

    def after(value, point):
        return lax.optimization_barrier((value, point))[0]

    def swap_tensor(value, mask):
        return lax.ppermute(value, "tensor", [(i, i ^ mask) for i in range(8)])

    def swap_dp(value):
        return lax.ppermute(value, "dp", [(0, 1), (1, 0)])

    def swap_seq(value):
        return lax.ppermute(value, "seq", [(0, 1), (1, 0)])

    def gather_width(shard, point=None, last=None):
        if fast:
            other = swap_dp(shard)
            own = shard
            if last is not None:
                own, other = after(own, point), after(other, last)
            return [shard, other, swap_seq(own), swap_seq(other)]
        axis = shard.ndim - 2
        full = lax.all_gather(shard, ("dp", "seq"), axis=axis, tiled=True)
        return [lax.slice_in_dim(full, i * QUARTER, (i + 1) * QUARTER, axis=axis) for i in range(4)]

    def gather_all(shard):
        return lax.all_gather(shard, ("dp", "seq"), axis=0, tiled=True)

    def scatter_all(full):
        return lax.psum_scatter(full, ("dp", "seq"), scatter_dimension=0, tiled=True)

    def weight_full(a, b, halves=False):
        n, width = b.shape
        if halves:
            specs = [
                pl.BlockSpec((QUARTER, width), lambda i: (jnp.minimum(i, 1), 0)),
                pl.BlockSpec((QUARTER, width), lambda i: (jnp.maximum(i - 2, 0), 0)),
            ]
        else:
            specs = [pl.BlockSpec((QUARTER, width), lambda i: (i, 0))]
        outs = pl.pallas_call(
            weight_grad_kernel,
            grid=(4,),
            in_specs=[pl.BlockSpec((n, QUARTER), lambda i: (0, i)), whole((n, width))],
            out_specs=specs,
            out_shape=[jax.ShapeDtypeStruct((D // len(specs), width), BF16)] * len(specs),
            compiler_params=vmem(56),
            cost_estimate=cost(n * width / 160000),
            name="weight_grad",
        )(a, b)
        return tuple(outs) if halves else outs[0]

    def weight_halves(a, b):
        return weight_full(a, b, True)

    def pair_sum(a, b, place):
        part = pl.BlockSpec((QUARTER, a.shape[1]), lambda i: (place, 0))
        return pl.pallas_call(
            pair_sum_kernel,
            grid=(1,),
            in_specs=[part, part],
            out_specs=whole((QUARTER, a.shape[1])),
            out_shape=jax.ShapeDtypeStruct((QUARTER, a.shape[1]), BF16),
            compiler_params=vmem(48),
            cost_estimate=cost(1.5),
            name="pair_sum",
        )(a, b)

    def scatter_near(halves, point):
        keep, send = halves
        if not fast:
            return keep, send, None
        got = after(swap_seq(send), point)
        return keep, got, pair_sum(keep, got, 1)

    def send_far(near):
        return swap_dp(near[2]) if fast else None

    def scatter_far(near, far):
        keep, got, low = near
        if fast:
            return [keep, got, far]
        full = jnp.concatenate([keep, got], axis=0)
        return [lax.psum_scatter(full, ("dp", "seq"), scatter_dimension=0, tiled=True)]

    def swap_high(pieces):
        return [pieces[0]] + [swap_tensor(pieces[k], 2 * k) for k in (1, 2, 3)]

    def scatter_parts(total):
        n = total.shape[0] // 4
        return [total[:n]] + [
            swap_tensor(total[i * n : (i + 1) * n].astype(BF16), mask)
            for i, mask in ((1, 2), (2, 4), (3, 6))
        ]

    def gather_near(own):
        return jnp.concatenate([own] + [swap_tensor(own, mask) for mask in (2, 4, 6)], axis=0)

    attn_low = jnp.concatenate(
        [query_weight, kv_weight, jnp.pad(norm_gains, ((0, 0), (0, 126)))], axis=1
    ).astype(BF16)
    back_low = jnp.concatenate([query_weight, kv_weight], axis=1).astype(BF16)
    output_low = after(output_weight.astype(BF16), attn_low)
    output_near = lax.all_gather(output_low, "tensor", axis=0, axis_index_groups=HIGH_GROUPS)
    token_rows = tokens.reshape(span, D)
    cot_rows = cotangent.reshape(span, D)
    positions = seq_id * span + jnp.arange(span, dtype=jnp.int32)
    cosine, sine = rope_tables(positions)
    attn_w = gather_width(attn_low, attn_low, (cosine, sine))
    half_span = span // 2
    dy = pl.pallas_call(
        reorder_kernel,
        grid_spec=pltpu.PrefetchScalarGridSpec(
            num_scalar_prefetch=1,
            grid=(8,),
            in_specs=[pl.BlockSpec((block, D), lambda i, info: (tensor_block(i, info), 0))],
            out_specs=pl.BlockSpec((2, half_block, D), lambda i, info: (0, i, 0)),
        ),
        out_shape=jax.ShapeDtypeStruct((2, half_span, D), BF16),
        cost_estimate=cost(7.5),
        name="reorder",
    )(info, cot_rows)

    normed_one, queries, kv_own, gains = pl.pallas_call(
        project_kernel,
        grid_spec=pltpu.PrefetchScalarGridSpec(
            num_scalar_prefetch=1,
            grid=(span // rows,),
            in_specs=[pl.BlockSpec((rows, D), lambda i, info: (i, 0))]
            + [whole((QUARTER, 512))] * 4
            + [pl.BlockSpec((rows, 128), lambda i, info: (i, 0))] * 2,
            out_specs=[
                pl.BlockSpec((rows, D), lambda i, info: (i, 0)),
                pl.BlockSpec((rows, 256), lambda i, info: (i, 0)),
                pl.BlockSpec((rows, 128), lambda i, info: (i, 0)),
                whole((8, D)),
            ],
            scratch_shapes=[pltpu.VMEM((8, D), F32)],
        ),
        out_shape=[
            jax.ShapeDtypeStruct((span, D), BF16),
            jax.ShapeDtypeStruct((span, 256), BF16),
            jax.ShapeDtypeStruct((span, 128), BF16),
            jax.ShapeDtypeStruct((8, D), F32),
        ],
        compiler_params=vmem(48),
        cost_estimate=cost(7),
        name="project",
    )(info, token_rows, *attn_w, cosine, sine)

    gate_up_late, down_late = after((gate_up_weight, down_weight), queries)
    gate_up_low = jnp.concatenate(
        [gate_up_late[:, 0, :], gate_up_late[:, 1, :]], axis=1
    ).astype(BF16)
    down_low = down_late.astype(BF16)

    if fast:
        kv_other = swap_seq(kv_own)
        kv_all = jnp.where(
            seq_id == 0,
            jnp.concatenate([kv_own, kv_other], axis=0),
            jnp.concatenate([kv_other, kv_own], axis=0),
        )
    else:
        kv_all = lax.all_gather(kv_own, "seq", axis=0, tiled=True)

    steps = 4
    attended, logs = pl.pallas_call(
        functools.partial(attend_kernel, rows, max(keys, 2 * rows)),
        grid_spec=pltpu.PrefetchScalarGridSpec(
            num_scalar_prefetch=1,
            grid=(steps,),
            in_specs=[
                pl.BlockSpec((rows, 256), lambda i, info: (i, 0)),
                whole((length, 128)),
            ],
            out_specs=[
                pl.BlockSpec((rows, 256), lambda i, info: (i, 0)),
                pl.BlockSpec((1, 1, GROUP * rows), lambda i, info: (i, 0, 0)),
            ],
            scratch_shapes=[
                pltpu.VMEM((128, length), BF16),
                pltpu.VMEM((128, GROUP * rows), F32),
                pltpu.VMEM((1, GROUP * rows), F32),
            ],
        ),
        out_shape=[
            jax.ShapeDtypeStruct((span, 256), BF16),
            jax.ShapeDtypeStruct((steps, 1, GROUP * rows), F32),
        ],
        compiler_params=vmem(48),
        cost_estimate=cost(18),
        name="attend",
    )(info, queries, kv_all)

    gate_up_w = gather_all(gate_up_low)
    down_w = gather_all(down_low)
    att_parts = lax.all_to_all(
        attended.reshape(4, rows, 256), "tensor", 0, 0, axis_index_groups=HIGH_GROUPS
    )
    att_parts = after(att_parts, dy)
    output_w = gather_width(after(output_near, queries), att_parts, att_parts)

    out_keep, out_send = pl.pallas_call(
        out_kernel,
        grid_spec=pltpu.PrefetchScalarGridSpec(
            num_scalar_prefetch=1,
            grid=(1,),
            in_specs=[whole((4, rows, 256))] + [whole((4, QUARTER, 256))] * 4,
            out_specs=[whole((block, D))] * 2,
            scratch_shapes=[pltpu.VMEM((rows, QUARTER), F32)],
        ),
        out_shape=[jax.ShapeDtypeStruct((block, D), F32), jax.ShapeDtypeStruct((block, D), BF16)],
        compiler_params=vmem(48),
        cost_estimate=cost(3.8),
        name="attention_out",
    )(info, att_parts, *output_w)
    out_got = swap_tensor(out_send, 1)
    own_rows = pl.BlockSpec((block, D), lambda i, info: (info[AT_TENSOR], 0))
    resid_one, low_a, low_b = pl.pallas_call(
        norm_kernel,
        grid_spec=pltpu.PrefetchScalarGridSpec(
            num_scalar_prefetch=1,
            grid=(1,),
            in_specs=[whole((block, D))] * 2 + [own_rows, whole((8, D))],
            out_specs=[whole((block, D)), whole((half_block, D)), whole((half_block, D))],
        ),
        out_shape=[
            jax.ShapeDtypeStruct((block, D), F32),
            jax.ShapeDtypeStruct((half_block, D), BF16),
            jax.ShapeDtypeStruct((half_block, D), BF16),
        ],
        cost_estimate=cost(3.5),
        name="second_norm",
    )(info, out_keep, out_got, token_rows, gains)

    def mlp(chunk, near, far, before):
        n = half_span
        anywhere = pl.BlockSpec(memory_space=pl.ANY)
        late_columns = pl.BlockSpec(
            (4, half_block, QUARTER), lambda i, info: (0, 0, jnp.maximum(i - 4, 0))
        )
        late_half = pl.BlockSpec((n // 2, QUARTER), lambda i, info: (0, jnp.maximum(i - 4, 0)))
        return pl.pallas_call(
            mlp_kernel,
            grid_spec=pltpu.PrefetchScalarGridSpec(
                num_scalar_prefetch=1,
                grid=(8,),
                in_specs=[whole((n // 2, D))] * 2
                + [pl.BlockSpec((1, n, D), lambda i, info: (chunk, 0, 0))]
                + [anywhere] * (2 + len(before)),
                out_specs=[
                    late_columns,
                    late_columns,
                    late_half,
                    late_half,
                    pl.BlockSpec((n, 1024), lambda i, info: (chunk, 0)),
                    pl.BlockSpec((n, 2048), lambda i, info: (chunk, 0)),
                    pl.BlockSpec((n, D), lambda i, info: (chunk, 0)),
                ],
                scratch_shapes=[
                    pltpu.VMEM((D, 2048), BF16),
                    pltpu.VMEM((D, 1024), BF16),
                    pltpu.SemaphoreType.DMA((4, 3)),
                ],
            ),
            out_shape=[
                jax.ShapeDtypeStruct((4, half_block, D), BF16),
                jax.ShapeDtypeStruct((4, half_block, D), BF16),
                jax.ShapeDtypeStruct((n // 2, D), BF16),
                jax.ShapeDtypeStruct((n // 2, D), BF16),
                jax.ShapeDtypeStruct((span, 1024), BF16),
                jax.ShapeDtypeStruct((span, 2048), BF16),
                jax.ShapeDtypeStruct((span, D), BF16),
            ],
            input_output_aliases={6: 4, 7: 5, 8: 6} if before else {},
            compiler_params=vmem(56),
            cost_estimate=cost(22.5),
            name="mlp",
        )(info, near, far, dy, gate_up_w, down_w, *before)

    near_a = gather_near(low_a)
    near_b = gather_near(low_b)
    far_a = after(swap_tensor(near_a, 1), near_b)
    far_b = swap_tensor(near_b, 1)
    mlp_keep_a, mlp_send_a, two_keep_a, two_send_a, hidden, gate_up_back, x = mlp(
        0, near_a, far_a, ()
    )
    two_got_a = swap_tensor(two_send_a, 1)
    back_low = after(back_low, near_b)
    back_parts = [swap_tensor(back_low, mask) for mask in (2, 4, 6)]
    mlp_keep_b, mlp_send_b, two_keep_b, two_send_b, hidden, gate_up_back, x = mlp(
        1, near_b, far_b, (hidden, gate_up_back, x)
    )
    two_got_b = swap_tensor(two_send_b, 1)
    total_a = two_keep_a.astype(F32) + after(two_got_a, two_send_b).astype(F32)
    two_a = scatter_parts(total_a)
    back_near = jnp.stack(after([back_low] + back_parts, two_send_b), axis=0)
    hidden, gate_up_back = after((hidden, gate_up_back), (total_a, back_near))
    narrow = pl.BlockSpec((span, QUARTER), lambda i: (0, i))
    mlp_full = pl.pallas_call(
        mlp_grad_kernel,
        grid=(4,),
        in_specs=[narrow, whole((span, 2048)), narrow, whole((span, 1024))],
        out_specs=pl.BlockSpec((QUARTER, 3072), lambda i: (i, 0)),
        out_shape=jax.ShapeDtypeStruct((D, 3072), BF16),
        compiler_params=vmem(56),
        cost_estimate=cost(22),
        name="mlp_grad",
    )(x, gate_up_back, dy.reshape(span, D), hidden)
    total_b = two_keep_b.astype(F32) + after(
        two_got_b, (mlp_full, two_a)
    ).astype(F32)
    two_b = scatter_parts(total_b)
    mlp_grad = scatter_all(after(mlp_full, total_b))
    mlp_got_a = swap_tensor(after(mlp_send_a, total_b), 1)

    resid_grad, resid_low, gain_two_grad = pl.pallas_call(
        norm_back_kernel,
        grid_spec=pltpu.PrefetchScalarGridSpec(
            num_scalar_prefetch=1,
            grid=(1,),
            in_specs=[whole((half_block, D))] * 8
            + [
                whole((block, D)),
                pl.BlockSpec((2, half_block, D), lambda i, info: (0, 0, 0)),
                whole((8, D)),
            ],
            out_specs=[whole((block, D)), whole((block, D)), whole((1, D))],
        ),
        out_shape=[
            jax.ShapeDtypeStruct((block, D), F32),
            jax.ShapeDtypeStruct((block, D), BF16),
            jax.ShapeDtypeStruct((1, D), F32),
        ],
        cost_estimate=cost(4.7),
        name="second_norm_back",
    )(info, *two_a, *two_b, resid_one, dy, gains)
    resid_other = swap_tensor(resid_low, 1)
    mlp_total_a = (mlp_keep_a.astype(F32) + after(mlp_got_a, resid_low).astype(F32)).astype(BF16)
    mlp_parts_a = lax.all_to_all(mlp_total_a, "tensor", 0, 0, axis_index_groups=HIGH_GROUPS)
    resid_other = after(resid_other, mlp_total_a)
    mlp_got_b = swap_tensor(after(mlp_send_b, resid_other), 1)
    resid_both, *grad_pieces = pl.pallas_call(
        out_back_kernel,
        grid_spec=pltpu.PrefetchScalarGridSpec(
            num_scalar_prefetch=1,
            grid=(1,),
            in_specs=[whole((block, D))] * 2 + [whole((4, QUARTER, 256))] * 4,
            out_specs=[whole((rows, D))] + [whole((rows, 256))] * 4,
        ),
        out_shape=[jax.ShapeDtypeStruct((rows, D), BF16)]
        + [jax.ShapeDtypeStruct((rows, 256), BF16)] * 4,
        compiler_params=vmem(48),
        cost_estimate=cost(3.9),
        name="attention_out_back",
    )(info, resid_low, resid_other, *output_w)
    grad_parts = swap_high(grad_pieces)
    mlp_total_b = (mlp_keep_b.astype(F32) + after(mlp_got_b, grad_parts).astype(F32)).astype(BF16)
    mlp_parts_b = lax.all_to_all(mlp_total_b, "tensor", 0, 0, axis_index_groups=HIGH_GROUPS)
    back_w = gather_width(back_near, resid_low, resid_low)
    grad_parts = after(grad_parts, (mlp_total_b, back_w))

    spans = seq_size if fast else length // span
    dq, *dq_pieces, dkv = pl.pallas_call(
        functools.partial(attend_back_kernel, rows, keys, spans),
        grid_spec=pltpu.PrefetchScalarGridSpec(
            num_scalar_prefetch=1,
            grid=(steps,),
            in_specs=[pl.BlockSpec((rows, 256), lambda i, info: (i, 0))]
            + [whole((rows, 256))] * 4
            + [
                pl.BlockSpec((rows, 256), lambda i, info: (i, 0)),
                pl.BlockSpec((1, 1, GROUP * rows), lambda i, info: (i, 0, 0)),
                whole((length, 128)),
                pl.BlockSpec((rows, 128), lambda i, info: (i, 0)),
                pl.BlockSpec((rows, 128), lambda i, info: (i, 0)),
            ],
            out_specs=[pl.BlockSpec((rows, 256), lambda i, info: (i, 0))]
            + [whole((rows, 256))] * 4
            + [whole((spans, span, 128))],
            scratch_shapes=[
                pltpu.VMEM((HEAD_DIM, length), BF16),
                pltpu.VMEM((length, 128), F32),
                pltpu.VMEM((HEAD_DIM, GROUP * rows), F32),
                pltpu.VMEM((rows, 256), BF16),
            ],
        ),
        out_shape=[jax.ShapeDtypeStruct((span, 256), BF16)]
        + [jax.ShapeDtypeStruct((rows, 256), BF16)] * 4
        + [jax.ShapeDtypeStruct((spans, span, 128), BF16)],
        compiler_params=vmem(48),
        cost_estimate=cost(23),
        name="attend_back",
    )(info, queries, *grad_parts, attended, logs, kv_all, cosine, sine)

    if fast:
        dkv_own, dkv_more = dkv[0], swap_seq(dkv[1])
    else:
        dkv_own = lax.psum_scatter(dkv.reshape(length, 128), "seq", scatter_dimension=0, tiled=True)
        dkv_more = jnp.zeros_like(dkv_own)
    dq_parts = swap_high(dq_pieces)
    dkv_more = after(dkv_more, dq_parts)
    dkv_low, *dkv_pieces = pl.pallas_call(
        kv_back_kernel,
        grid_spec=pltpu.PrefetchScalarGridSpec(
            num_scalar_prefetch=1,
            grid=(1,),
            in_specs=[whole((span, 128))] * 4,
            out_specs=[whole((span, 128))] + [whole((rows, 128))] * 4,
        ),
        out_shape=[jax.ShapeDtypeStruct((span, 128), BF16)]
        + [jax.ShapeDtypeStruct((rows, 128), BF16)] * 4,
        cost_estimate=cost(3.2),
        name="kv_back",
    )(info, dkv_own, dkv_more, cosine, sine)

    dkv_parts = swap_high(dkv_pieces)
    block_low = pl.pallas_call(
        block_out_kernel,
        out_shape=jax.ShapeDtypeStruct((block, D), BF16),
        cost_estimate=cost(3),
        name="block_out",
    )(*after((mlp_parts_a, mlp_parts_b), dkv_low), resid_one)
    dkv_parts = after(dkv_parts, (mlp_grad, block_low))
    one_keep, one_send = pl.pallas_call(
        one_kernel,
        grid_spec=pltpu.PrefetchScalarGridSpec(
            num_scalar_prefetch=1,
            grid=(1,),
            in_specs=[whole((rows, 256))] * 4
            + [whole((rows, 128))] * 4
            + [whole((4, QUARTER, 384))] * 4,
            out_specs=[whole((block, D))] * 2,
            scratch_shapes=[pltpu.VMEM((rows, QUARTER), F32)],
        ),
        out_shape=[jax.ShapeDtypeStruct((block, D), F32), jax.ShapeDtypeStruct((block, D), BF16)],
        compiler_params=vmem(48),
        cost_estimate=cost(5.8),
        name="attention_in_back",
    )(info, *dq_parts, *dkv_parts, *back_w)
    one_got = swap_tensor(one_send, 1)
    dqkv = after(jnp.concatenate([dq, dkv_low], axis=1), one_send)
    attn_halves = weight_halves(normed_one, dqkv)
    out_halves = weight_halves(
        after(resid_both, one_send), jnp.concatenate(by_xor(att_parts), axis=1)
    )

    block_near = lax.all_gather(block_low, "tensor", axis=0, axis_index_groups=HIGH_GROUPS)
    one_got = after(one_got, (attn_halves, out_halves))
    out_near = scatter_near(out_halves, one_got)
    out_far = send_far(out_near)

    tokens_low = pl.pallas_call(
        tokens_back_kernel,
        grid_spec=pltpu.PrefetchScalarGridSpec(
            num_scalar_prefetch=1,
            grid=(1,),
            in_specs=[whole((block, D))] * 2 + [own_rows, whole((block, D)), whole((8, D))],
            out_specs=whole((block, D)),
        ),
        out_shape=jax.ShapeDtypeStruct((block, D), BF16),
        cost_estimate=cost(4.3),
        name="first_norm_back",
    )(info, one_keep, one_got, token_rows, resid_grad, gains)
    tokens_own = swap_tensor(tokens_low, 1)
    tokens_near = lax.all_gather(tokens_low, "tensor", axis=0, axis_index_groups=HIGH_GROUPS)

    attn_near = scatter_near(attn_halves, one_send)
    attn_far = send_far(attn_near)

    def adam(weight, one, two, terms, rate, decay):
        size = weight.shape[0] // 4
        if weight.ndim == 3:
            mine = pl.BlockSpec((size, 2, weight.shape[2]), lambda i: (i, 0, 0))
            wide = 2 * weight.shape[2]
        else:
            mine = pl.BlockSpec((size, weight.shape[1]), lambda i: (i, 0))
            wide = weight.shape[1]
        return pl.pallas_call(
            functools.partial(adam_kernel, rate, decay),
            grid=(4,),
            in_specs=[mine] * 3
            + [
                pl.BlockSpec((size, wide), lambda i, column=column: (i, column))
                for term, column in terms
            ],
            out_specs=[mine] * 3,
            out_shape=[jax.ShapeDtypeStruct(weight.shape, F32)] * 3,
            compiler_params=vmem(56),
            cost_estimate=cost(weight.size / 75000),
            name="adam",
        )(weight, one, two, *[term for term, column in terms])

    fan_in = RATE_FACTOR * D ** (-0.5)
    mlp_grad = after(mlp_grad, tokens_low)
    gate_up_new = adam(
        gate_up_weight, gate_up_first, gate_up_second, [(mlp_grad, 0)], fan_in, DECAY
    )
    down_new = adam(
        down_weight, down_first, down_second, [(mlp_grad, 2)], RATE_FACTOR * FF ** (-0.5), DECAY
    )

    products = jnp.concatenate(
        [
            jnp.sum(
                attn_halves[i // 2][(i % 2) * QUARTER : (i % 2 + 1) * QUARTER].astype(F32)
                * w[:, :384].astype(F32),
                axis=1,
            )
            / w[:, 384].astype(F32)
            for i, w in enumerate(attn_w)
        ]
    )
    gain_grads = jnp.stack(
        [
            products,
            jnp.concatenate(
                [lax.dynamic_slice(gain_two_grad[0], (info[i] * QUARTER,), (QUARTER,)) for i in range(4)]
            ),
        ]
    )
    if fast:
        gain_grads = gain_grads[:, : 2 * QUARTER] + swap_seq(gain_grads[:, 2 * QUARTER :])
        gain_got = swap_tensor(gain_grads, 1)
    else:
        shard = norm_gains.shape[0]
        gains_grad = lax.dynamic_slice(
            lax.psum(gain_grads, ("dp", "seq")),
            (0, (dp_id * seq_size + seq_id) * shard),
            (2, shard),
        )
        gain_grads = gains_grad
        gain_got = swap_tensor(gains_grad, 1)
    block_far = swap_tensor(after(block_near, tokens_own), 1)
    gain_grads = gain_grads + gain_got
    early = (gate_up_new, down_new, gain_grads) + ((out_far, attn_far) if fast else ())
    tokens_near = after(tokens_near, early)
    tokens_far = swap_tensor(others(tokens_near), 1)

    attn_terms = after(scatter_far(attn_near, attn_far), tokens_near)
    query_new = adam(
        query_weight, query_first, query_second, [(term, 0) for term in attn_terms], fan_in, DECAY
    )
    kv_new = adam(kv_weight, kv_first, kv_second, [(term, 2) for term in attn_terms], fan_in, DECAY)

    out_terms = scatter_far(out_near, out_far)
    out_rows = sum(term[: out_terms[-1].shape[0]].astype(F32) for term in after(out_terms, tokens_near))
    output_terms = swap_high([out_rows[:, k * 256 : (k + 1) * 256].astype(BF16) for k in range(4)])
    output_new = adam(
        output_weight,
        output_first,
        output_second,
        [(term, 0) for term in output_terms],
        RATE_FACTOR * FAN_OUT ** (-0.5),
        DECAY,
    )

    gain_grads = after(gain_grads, tokens_near)
    if fast:
        gains_grad = gain_grads[:, :QUARTER] + swap_dp(gain_grads[:, QUARTER:])
    else:
        gains_grad = gain_grads
    for mask in (2, 4):
        gains_grad = gains_grad + swap_tensor(gains_grad, mask)
    gains_grad = gains_grad.T
    gains_new = adam_step(norm_gains, gains_grad, gains_first, gains_second, GAIN_RATE, 0.0)


    def place(parts, dtype, name):
        return pl.pallas_call(
            place_kernel,
            grid_spec=pltpu.PrefetchScalarGridSpec(
                num_scalar_prefetch=1,
                grid=(4,),
                in_specs=[pl.BlockSpec((1, block, D), lambda i, info: (i, 0, 0))] * 2,
                out_specs=pl.BlockSpec((rows, D), lambda i, info: (i, 0)),
            ),
            out_shape=jax.ShapeDtypeStruct((span, D), dtype),
            compiler_params=vmem(48),
            cost_estimate=cost(5),
            name=name,
        )(info, *parts).reshape(tokens.shape)

    def place_own(parts, dtype, name):
        return pl.pallas_call(
            place_own_kernel,
            grid_spec=pltpu.PrefetchScalarGridSpec(
                num_scalar_prefetch=1,
                grid=(4,),
                in_specs=[
                    pl.BlockSpec(
                        (1, block, D), lambda i, info: (lax.bitwise_xor(info[AT_HIGH], i), 0, 0)
                    ),
                    whole((block, D)),
                    pl.BlockSpec((1, block, D), lambda i, info: (jnp.maximum(i - 1, 0), 0, 0)),
                ],
                out_specs=pl.BlockSpec(
                    (rows, D), lambda i, info: (lax.bitwise_xor(info[AT_HIGH], i), 0)
                ),
            ),
            out_shape=jax.ShapeDtypeStruct((span, D), dtype),
            compiler_params=vmem(48),
            cost_estimate=cost(5),
            name=name,
        )(info, *parts).reshape(tokens.shape)

    tokens_grad = place_own((tokens_near, tokens_own, tokens_far), F32, "tokens_grad")
    block_out = place((block_near, block_far), BF16, "block_out_rows")

    results = (query_new, output_new, kv_new, gate_up_new, down_new, gains_new)
    return (block_out, tokens_grad) + tuple(r[i] for i in range(3) for r in results)


def solution(mesh):
    wide = P(("dp", "seq"), "tensor")
    weights = (wide, wide, wide, P(("dp", "seq"), None, "tensor"), wide, P(("dp", "seq"), None))
    rows = P("dp", "seq", None)
    return jax.shard_map(
        functools.partial(body, dp_size=mesh.shape["dp"], seq_size=mesh.shape["seq"]),
        mesh=mesh,
        in_specs=(rows, rows) + weights * 3,
        out_specs=(rows, rows) + weights * 3,
        check_vma=False,
    )
```

```python
import functools

import jax
import jax.numpy as jnp
from jax import lax
from jax.experimental import pallas as pl
from jax.experimental.pallas import tpu as pltpu
from jax.sharding import PartitionSpec as P

D = 2048
FF = 8192
HEADS = 32
KV_HEADS = 8
HEAD_DIM = 64
STEP = 10
FAN_OUT = 2

EPS_NORM = 1e-05
ROPE_BASE = 500000.0
BETA_ONE = 0.9
BETA_TWO = 0.95
ADAM_EPS = 1e-08
DECAY = 0.1
RATE_FACTOR = 3.0
GAIN_RATE = 1.0
MASKED = -1e30

F32 = jnp.float32
BF16 = jnp.bfloat16
GROUP = HEADS // KV_HEADS
QUARTER = D // 4
ORDER = (0, 2, 4, 6, 1, 3, 5, 7)
WIDTH_ORDER = (0, 2, 1, 3)
HIGH_GROUPS = [[0, 2, 4, 6], [1, 3, 5, 7]]
AT_TENSOR, AT_OFFSET, AT_SEQ, AT_LOW, AT_HIGH = 4, 5, 6, 7, 8


def vmem(mib):
    return pltpu.CompilerParams(vmem_limit_bytes=mib * 1024 * 1024)


COST_SCALE = 0.5


def cost(us):
    return pl.CostEstimate(flops=0, bytes_accessed=int(COST_SCALE * us * 3.69e6), transcendentals=0)


def dot(a, b):
    return lax.dot_general(a, b, (((1,), (0,)), ((), ())), preferred_element_type=F32)


def dot_nt(a, b):
    return lax.dot_general(a, b, (((1,), (1,)), ((), ())), preferred_element_type=F32)


def swap_halves(values):
    lane = lax.broadcasted_iota(jnp.int32, values.shape, 1)
    half = HEAD_DIM // 2
    return jnp.where(
        lane % HEAD_DIM < half,
        pltpu.roll(values, 128 - half, 1),
        pltpu.roll(values, half, 1),
    )


def width_block(info, place):
    return pl.ds(pl.multiple_of(info[place] * QUARTER, QUARTER), QUARTER)


def project_kernel(info, tok, w0, w1, w2, w3, cosine, sine, normed, q_out, kv_out, gains, gain_rows):
    pieces = (w0, w1, w2, w3)

    @pl.when(pl.program_id(0) == 0)
    def _():
        for place, piece in enumerate(pieces):
            turned = piece[:, 384:512].astype(F32).T
            gain_rows[:, place * QUARTER : (place + 1) * QUARTER] = turned[0:8]
        natural_store(info, gains, gain_rows[...])

    parts = [tok[:, width_block(info, place)].astype(F32) for place in range(4)]
    square = sum(jnp.sum(part * part, axis=1, keepdims=True) for part in parts)
    inverse = lax.rsqrt(square * (1.0 / D) + EPS_NORM)
    total = None
    for place, (part, piece) in enumerate(zip(parts, pieces)):
        cols = slice(place * QUARTER, (place + 1) * QUARTER)
        low = (part * inverse * gain_rows[0:1, cols]).astype(BF16)
        normed[:, cols] = low
        term = dot(low, piece[:, 0:384])
        total = term if total is None else total + term
    cos, sin = cosine[...], sine[...]
    for c in (0, 128):
        raw = total[:, c : c + 128]
        q_out[:, c : c + 128] = (raw * cos + swap_halves(raw) * sin).astype(BF16)
    raw = total[:, 256:384]
    turned = raw * cos + swap_halves(raw) * sin
    lane = lax.broadcasted_iota(jnp.int32, raw.shape, 1)
    kv_out[...] = jnp.where(lane < HEAD_DIM, turned, raw).astype(BF16)


def heads_wide(turned):
    return jnp.concatenate(
        [turned[h * HEAD_DIM : (h + 1) * HEAD_DIM] for h in range(GROUP)], axis=1
    )


def heads_tall(wide, rows):
    return jnp.concatenate([wide[:, h * rows : (h + 1) * rows] for h in range(GROUP)], axis=0)


def diagonal_mask(rows, keys, shift):
    key = lax.broadcasted_iota(jnp.int32, (keys, GROUP * rows), 0)
    query = lax.broadcasted_iota(jnp.int32, (keys, GROUP * rows), 1) % rows
    return key <= query + shift


def diagonal_block(rows, keys, step, info):
    start = info[AT_OFFSET] + step
    ratio = keys // rows
    diagonal = lax.div(start, jnp.int32(ratio))
    return diagonal, (start - diagonal * ratio) * rows


def attend_kernel(
    rows, keys, info, q, kv, out, log_out, kv_turned, acc, high
):
    step = pl.program_id(0)

    @pl.when(step == 0)
    def _():
        turned = kv[...].T
        row = lax.broadcasted_iota(jnp.int32, turned.shape, 0)
        kv_turned[...] = jnp.where(row < HEAD_DIM, jnp.ones_like(turned), turned)

    wide = heads_wide((q[...] * (HEAD_DIM**-0.5)).astype(F32).T).astype(BF16)
    wide = jnp.concatenate([wide, jnp.zeros_like(wide)], axis=0)
    diagonal, shift = diagonal_block(rows, keys, step, info)

    def scores_of(j):
        return dot(kv[pl.ds(pl.multiple_of(j * keys, keys), keys), :], wide)

    def values_of(j):
        return kv_turned[:, pl.ds(pl.multiple_of(j * keys, keys), keys)]

    scores = jnp.where(diagonal_mask(rows, keys, shift), scores_of(diagonal), MASKED)
    top = jnp.max(scores, axis=0, keepdims=True)
    high[...] = top
    acc[...] = dot(values_of(diagonal), jnp.exp(scores - top).astype(BF16))

    def body(j, carry):
        scores = scores_of(j)
        old = high[...]
        top = jnp.maximum(old, jnp.max(scores, axis=0, keepdims=True))
        high[...] = top
        chances = jnp.exp(scores - top).astype(BF16)
        acc[...] = acc[...] * jnp.exp(old - top) + dot(values_of(j), chances)
        return carry

    lax.fori_loop(0, diagonal, body, 0)
    total = acc[0:1, :]
    log_out[0] = high[...] + jnp.log(total)
    result = acc[HEAD_DIM:, :] * (1.0 / total)
    out[...] = heads_tall(result, rows).T.astype(BF16)


def attend_back_kernel(
    rows, keys, spans, info, q, grad0, grad1, grad2, grad3, att, log_in, kv, cosine, sine,
    dq_out, piece0, piece1, piece2, piece3, dkv_out, kv_turned, dkv, dq_acc, grad,
):
    step = pl.program_id(0)

    @pl.when(step == 0)
    def _():
        kv_turned[...] = kv[...].T[0:HEAD_DIM]
        dkv[...] = jnp.zeros_like(dkv)

    for k, piece in enumerate((grad0, grad1, grad2, grad3)):

        @pl.when(lax.bitwise_xor(step, info[AT_HIGH]) == k)
        def _():
            grad[...] = piece[...]

    scaled = q[...] * (HEAD_DIM**-0.5)
    grads = grad[...]
    zero_tall = jnp.zeros((GROUP * rows, HEAD_DIM), BF16)
    q_tall = jnp.concatenate(
        [scaled[:, h * HEAD_DIM : (h + 1) * HEAD_DIM] for h in range(GROUP)], axis=0
    ).astype(BF16)
    g_tall = jnp.concatenate(
        [grads[:, h * HEAD_DIM : (h + 1) * HEAD_DIM] for h in range(GROUP)], axis=0
    )
    q_tall = jnp.concatenate([q_tall, zero_tall], axis=1)
    g_tall = jnp.concatenate([zero_tall, g_tall], axis=1)
    q_wide = heads_wide(scaled.astype(F32).T).astype(BF16)
    g_turned = grads.astype(F32).T
    g_wide = heads_wide(g_turned).astype(BF16)
    zero_wide = jnp.zeros_like(g_wide)
    product = heads_wide(g_turned * att[...].astype(F32).T)
    delta = jnp.sum(product, axis=0, keepdims=True)
    q_wide = jnp.concatenate([q_wide, zero_wide], axis=0)
    g_wide = jnp.concatenate([zero_wide, g_wide], axis=0)
    logs = log_in[0]
    diagonal, shift = diagonal_block(rows, keys, step, info)

    def one_block(j, mask):
        place = pl.ds(pl.multiple_of(j * keys, keys), keys)
        block = kv[place, :]
        chances = jnp.exp(dot(block, q_wide) - logs)
        if mask is not None:
            chances = jnp.where(mask, chances, 0.0)
        chance_grad = dot(block, g_wide)
        score_grad = (chances * (chance_grad - delta)).astype(BF16)
        dkv[place, :] += dot(score_grad, q_tall) + dot(chances.astype(BF16), g_tall)
        return dot(kv_turned[:, place], score_grad)

    dq_acc[...] = one_block(diagonal, diagonal_mask(rows, keys, shift))

    def body(j, carry):
        dq_acc[...] += one_block(j, None)
        return carry

    lax.fori_loop(0, diagonal, body, 0)
    dq = heads_tall(dq_acc[...] * (HEAD_DIM**-0.5), rows).T
    cos, sin = cosine[...], sine[...]
    for c in (0, 128):
        raw = dq[:, c : c + 128]
        dq_out[:, c : c + 128] = (raw * cos - swap_halves(raw) * sin).astype(BF16)
    for k, piece in enumerate((piece0, piece1, piece2, piece3)):

        @pl.when(lax.bitwise_xor(step, info[AT_HIGH]) == k)
        def _():
            piece[...] = dq_out[...]

    @pl.when(step == pl.num_programs(0) - 1)
    def _():
        span = dkv_out.shape[1]
        for r in range(spans):
            at = lax.bitwise_xor(info[AT_SEQ], jnp.int32(r)) * span
            dkv_out[r] = dkv[pl.ds(pl.multiple_of(at, span), span), :].astype(BF16)


def out_kernel(info, att, w0, w1, w2, w3, keep, send, total):
    half = keep.shape[0]
    low = info[AT_LOW]
    for place, w in enumerate((w0, w1, w2, w3)):
        cols = width_block(info, place)
        total[...] = sum(dot_nt(att[k], w[k]) for k in range(4))
        keep[:, cols] = total[pl.ds(pl.multiple_of(low * half, half), half), :]
        send[:, cols] = total[pl.ds(pl.multiple_of((1 - low) * half, half), half), :].astype(BF16)


def norm_kernel(info, keep, got, tok, gains, resid_out, low_a, low_b):
    resid = tok[...].astype(F32) + keep[...] + got[...].astype(F32)
    resid_out[...] = resid
    inverse = lax.rsqrt(jnp.mean(resid * resid, axis=1, keepdims=True) + EPS_NORM)
    low = (resid * inverse * gains[1:2, :]).astype(BF16)
    half = low.shape[0] // 2
    low_a[...] = low[:half]
    low_b[...] = low[half:]


def mlp_kernel(
    parts, info, *refs,
):
    sources, (dy, weights, *rest) = refs[: 2 * parts], refs[2 * parts :]
    mlp_keep, mlp_send, two_keep, two_send, hidden_out, grad_out, x, gate_up, down, sems = rest[-10:]
    step = pl.program_id(0)
    wide = FF // 8
    n = x.shape[0]

    def copies(group):
        cols = pl.ds(group * 256, 256)
        up_cols = pl.ds(wide + group * 256, 256)
        for k, (src, dst, c) in enumerate(
            ((cols, gate_up, cols), (up_cols, gate_up, up_cols), (pl.ds(2 * wide + group * 256, 256), down, cols))
        ):
            yield pltpu.make_async_copy(weights.at[:, src], dst.at[:, c], sems.at[group, k])

    @pl.when(step == 0)
    def _():
        for group in range(4):
            for copy in copies(group):
                copy.start()
        size = n // 8
        piece = size // parts
        for i, source in enumerate(sources):
            half, part = divmod(i, parts)
            for k in range(4):
                at = (half * 4 + k) * size + part * piece
                x[at : at + piece] = source[k * piece : (k + 1) * piece]

    for group in range(4):

        @pl.when(step == group)
        def _():
            for copy in copies(group):
                copy.wait()
            cols = slice(group * 256, (group + 1) * 256)
            up_cols = slice(wide + group * 256, wide + (group + 1) * 256)
            gate = dot(x[...], gate_up[:, cols])
            up = dot(x[...], gate_up[:, up_cols])
            hidden_grad = dot(dy[0], down[:, cols])
            sigmoid = 1.0 / (1.0 + jnp.exp(-gate))
            silu = gate * sigmoid
            hidden_out[:, cols] = (silu * up).astype(BF16)
            grad_out[:, cols] = (
                hidden_grad * up * (sigmoid * (1.0 + gate * (1.0 - sigmoid)))
            ).astype(BF16)
            grad_out[:, up_cols] = (hidden_grad * silu).astype(BF16)

    @pl.when(step >= 4)
    def _():
        rows = pl.ds(pl.multiple_of((step - 4) * QUARTER, QUARTER), QUARTER)
        two = dot_nt(grad_out[...], gate_up[rows, :]).astype(BF16)
        two_keep[...] = two[: n // 2]
        two_send[...] = two[n // 2 :]
        mlp = dot_nt(hidden_out[...], down[rows, :]).astype(BF16)
        size = n // 8
        for i in range(4):
            owner = lax.bitwise_xor(info[AT_HIGH], jnp.int32(i))
            mlp_keep[owner] = mlp[i * size : (i + 1) * size]
            mlp_send[owner] = mlp[n // 2 + i * size : n // 2 + (i + 1) * size]


def norm_back(values, incoming, gain):
    inverse = lax.rsqrt(jnp.mean(values * values, axis=1, keepdims=True) + EPS_NORM)
    scaled = incoming * gain
    gain_grad = jnp.sum(incoming * values * inverse, axis=0, keepdims=True)
    inner = jnp.mean(scaled * values, axis=1, keepdims=True)
    return inverse * scaled - values * (inverse * inverse * inverse * inner), gain_grad


def summed(parts):
    return sum(part[...].astype(F32) for part in parts)


def norm_back_kernel(info, *refs):
    parts_a, parts_b = refs[0:4], refs[4:8]
    resid, dy, gains, resid_grad, resid_low, gain_grad = refs[8:]
    half = dy.shape[1]
    sums = []
    for i, parts in enumerate((parts_a, parts_b)):
        rows = slice(i * half, (i + 1) * half)
        back, gain_part = norm_back(resid[rows], summed(parts), gains[1:2, :])
        full = dy[i].astype(F32) + back
        resid_grad[rows] = full
        resid_low[rows] = full.astype(BF16)
        sums.append(gain_part)
    gain_grad[...] = sums[0] + sums[1]


def out_back_kernel(info, own, other, w0, w1, w2, w3, both, g0, g1, g2, g3):
    half = own.shape[0]
    low = info[AT_LOW]
    for place in range(4):
        cols = slice(place * QUARTER, (place + 1) * QUARTER)
        natural = width_block(info, place)
        both[pl.ds(pl.multiple_of(low * half, half), half), cols] = own[:, natural]
        both[pl.ds(pl.multiple_of((1 - low) * half, half), half), cols] = other[:, natural]
    for k, out in enumerate((g0, g1, g2, g3)):
        high = lax.bitwise_xor(info[AT_HIGH], jnp.int32(k))
        out[...] = sum(
            dot(both[:, place * QUARTER : (place + 1) * QUARTER], w[high])
            for place, w in enumerate((w0, w1, w2, w3))
        ).astype(BF16)


def natural_store(info, out, value):
    for place in range(4):
        out[:, width_block(info, place)] = value[:, place * QUARTER : (place + 1) * QUARTER]


def kv_back_kernel(info, dkv, dkv_more, cosine, sine, out, p0, p1, p2, p3):
    raw = dkv[...].astype(F32) + dkv_more[...].astype(F32)
    turned = raw * cosine[...] - swap_halves(raw) * sine[...]
    lane = lax.broadcasted_iota(jnp.int32, raw.shape, 1)
    out[...] = jnp.where(lane < HEAD_DIM, turned, raw).astype(BF16)
    rows = p0.shape[0]
    for k, piece in enumerate((p0, p1, p2, p3)):
        at = lax.bitwise_xor(info[AT_HIGH], jnp.int32(k)) * rows
        piece[...] = out[pl.ds(pl.multiple_of(at, rows), rows), :]


def one_kernel(info, q0, q1, q2, q3, k0, k1, k2, k3, w0, w1, w2, w3, keep, send, total):
    half = keep.shape[0]
    low = info[AT_LOW]
    both = [
        jnp.concatenate([q[...], k[...]], axis=1)
        for q, k in zip((q0, q1, q2, q3), (k0, k1, k2, k3))
    ]
    for place, w in enumerate((w0, w1, w2, w3)):
        cols = width_block(info, place)
        total[...] = sum(
            dot_nt(part, w[k]) for k, part in enumerate(both)
        )
        keep[:, cols] = total[pl.ds(pl.multiple_of(low * half, half), half), :]
        send[:, cols] = total[pl.ds(pl.multiple_of((1 - low) * half, half), half), :].astype(BF16)


def tokens_back_kernel(info, keep, got, tok, resid_grad, gains, low):
    back, unused = norm_back(
        tok[...].astype(F32), keep[...] + got[...].astype(F32), gains[0:1, :]
    )
    low[...] = (resid_grad[...] + back).astype(BF16)


def block_out_kernel(parts_a, parts_b, resid, low):
    half = parts_a.shape[1]
    for i, parts in enumerate((parts_a, parts_b)):
        rows = slice(i * half, (i + 1) * half)
        low[rows] = (sum(parts[k].astype(F32) for k in range(4)) + resid[rows]).astype(BF16)


def reorder_kernel(info, src, out):
    half = out.shape[1]
    out[0] = src[:half]
    out[1] = src[half:]


def place_kernel(info, near, far, out):
    size = near.shape[1]
    at = info[AT_LOW] * size
    out[pl.ds(pl.multiple_of(at, size), size), :] = near[0].astype(out.dtype)
    out[pl.ds(pl.multiple_of(size - at, size), size), :] = far[0].astype(out.dtype)


def place_own_kernel(info, near, own, far, out):
    size = near.shape[1]
    at = info[AT_LOW] * size
    out[pl.ds(pl.multiple_of(at, size), size), :] = near[0].astype(out.dtype)
    other = pl.ds(pl.multiple_of(size - at, size), size)

    @pl.when(pl.program_id(0) == 0)
    def _():
        out[other, :] = own[...].astype(out.dtype)

    @pl.when(pl.program_id(0) > 0)
    def _():
        out[other, :] = far[0].astype(out.dtype)


def weight_grad_kernel(a, b, *outs):
    result = lax.dot_general(
        a[...], b[...], (((0,), (0,)), ((), ())), preferred_element_type=F32
    ).astype(BF16)
    if len(outs) == 1:
        outs[0][...] = result
        return

    @pl.when(pl.program_id(0) < 2)
    def _():
        outs[0][...] = result

    @pl.when(pl.program_id(0) >= 2)
    def _():
        outs[1][...] = result


def mlp_grad_kernel(x, gate_up_back, dy, hidden, out):
    for a, b, cols in (
        (x, gate_up_back, slice(0, gate_up_back.shape[1])),
        (dy, hidden, slice(gate_up_back.shape[1], out.shape[1])),
    ):
        out[:, cols] = lax.dot_general(
            a[...], b[...], (((0,), (0,)), ((), ())), preferred_element_type=F32
        ).astype(BF16)


def pair_sum_kernel(a, b, out):
    out[...] = (a[...].astype(F32) + b[...].astype(F32)).astype(BF16)


def adam_kernel(rate, decay, weight, one, two, *refs):
    outs = refs[-3:]
    if len(weight.shape) == 2:
        grad = summed(refs[:-3])
        results = adam_step(weight[...], grad, one[...], two[...], rate, decay)
        for out, result in zip(outs, results):
            out[...] = result
        return
    wide = weight.shape[2]
    for k in range(2):
        cols = slice(k * wide, (k + 1) * wide)
        grad = sum(ref[:, cols].astype(F32) for ref in refs[:-3])
        results = adam_step(weight[:, k, :], grad, one[:, k, :], two[:, k, :], rate, decay)
        for out, result in zip(outs, results):
            out[:, k, :] = result


def step_owner(step):
    return lax.rem(step, 4) * 2 + lax.div(step, 4)


def tensor_block(step, info):
    return lax.bitwise_xor(info[AT_TENSOR], step_owner(step))


def adam_step(weight, grad_sum, moment_one, moment_two, step_rate, decay_rate):
    first_new = BETA_ONE * moment_one + (1.0 - BETA_ONE) * grad_sum
    second_new = BETA_TWO * moment_two + (1.0 - BETA_TWO) * grad_sum * grad_sum
    first_hat = first_new / (1.0 - BETA_ONE**STEP)
    second_hat = second_new / (1.0 - BETA_TWO**STEP)
    updated = weight - step_rate * (
        first_hat / (jnp.sqrt(second_hat) + ADAM_EPS) + decay_rate * weight
    )
    return (updated, first_new, second_new)


def rope_tables(positions):
    half_dim = HEAD_DIM // 2
    exponent = jnp.arange(half_dim, dtype=F32) * (2.0 / HEAD_DIM)
    inverse = jnp.power(F32(ROPE_BASE), -exponent)
    angles = positions.astype(F32)[:, None] * inverse[None, :]
    cosine, sine = jnp.cos(angles), jnp.sin(angles)
    return (
        jnp.concatenate([cosine] * 4, axis=1),
        jnp.concatenate([-sine, sine, -sine, sine], axis=1),
    )


def whole(shape, dims=None):
    zeros = (0,) * len(shape)
    return pl.BlockSpec(shape, lambda *unused: zeros)


def body(
    tokens, cotangent, query_weight, output_weight, kv_weight, gate_up_weight, down_weight, norm_gains,
    query_first, output_first, kv_first, gate_up_first, down_first, gains_first,
    query_second, output_second, kv_second, gate_up_second, down_second, gains_second,
    *, dp_size, seq_size,
):
    fast = dp_size == 2 and seq_size == 2
    span = tokens.shape[1]
    length = span * seq_size
    rows = span // 4
    keys = max(rows, 128)
    block = span // 8
    half_block = block // 2
    tensor_id = lax.axis_index("tensor").astype(jnp.int32)
    seq_id = lax.axis_index("seq").astype(jnp.int32)
    dp_id = lax.axis_index("dp").astype(jnp.int32)
    own_width = dp_id * 2 + seq_id if fast else jnp.int32(0)
    order = WIDTH_ORDER if fast else (0, 1, 2, 3)
    info = jnp.stack(
        [lax.bitwise_xor(own_width, jnp.int32(o)) for o in order]
        + [tensor_id, seq_id * 4, seq_id if fast else jnp.int32(0), tensor_id % 2, tensor_id // 2]
    )

    def by_xor(parts):
        return [
            lax.dynamic_index_in_dim(
                parts, lax.bitwise_xor(info[AT_HIGH], jnp.int32(k)), 0, keepdims=False
            )
            for k in range(4)
        ]

    def others(near):
        return jnp.stack(by_xor(near)[1:], axis=0)

    def after(value, point):
        return lax.optimization_barrier((value, point))[0]

    def swap_tensor(value, mask):
        return lax.ppermute(value, "tensor", [(i, i ^ mask) for i in range(8)])

    def swap_dp(value):
        return lax.ppermute(value, "dp", [(0, 1), (1, 0)])

    def swap_seq(value):
        return lax.ppermute(value, "seq", [(0, 1), (1, 0)])

    def gather_width(shard, point=None, last=None):
        if fast:
            other = swap_dp(shard)
            own = shard
            if last is not None:
                own, other = after(own, point), after(other, last)
            return [shard, other, swap_seq(own), swap_seq(other)]
        axis = shard.ndim - 2
        full = lax.all_gather(shard, ("dp", "seq"), axis=axis, tiled=True)
        return [lax.slice_in_dim(full, i * QUARTER, (i + 1) * QUARTER, axis=axis) for i in range(4)]

    def gather_all(shard):
        return lax.all_gather(shard, ("dp", "seq"), axis=0, tiled=True)

    def scatter_all(full):
        return lax.psum_scatter(full, ("dp", "seq"), scatter_dimension=0, tiled=True)

    def weight_full(a, b, halves=False):
        n, width = b.shape
        if halves:
            specs = [
                pl.BlockSpec((QUARTER, width), lambda i: (jnp.minimum(i, 1), 0)),
                pl.BlockSpec((QUARTER, width), lambda i: (jnp.maximum(i - 2, 0), 0)),
            ]
        else:
            specs = [pl.BlockSpec((QUARTER, width), lambda i: (i, 0))]
        outs = pl.pallas_call(
            weight_grad_kernel,
            grid=(4,),
            in_specs=[pl.BlockSpec((n, QUARTER), lambda i: (0, i)), whole((n, width))],
            out_specs=specs,
            out_shape=[jax.ShapeDtypeStruct((D // len(specs), width), BF16)] * len(specs),
            compiler_params=vmem(56),
            cost_estimate=cost(n * width / 160000),
            name="weight_grad",
        )(a, b)
        return tuple(outs) if halves else outs[0]

    def weight_halves(a, b):
        return weight_full(a, b, True)

    def pair_sum(a, b, place):
        part = pl.BlockSpec((QUARTER, a.shape[1]), lambda i: (place, 0))
        return pl.pallas_call(
            pair_sum_kernel,
            grid=(1,),
            in_specs=[part, part],
            out_specs=whole((QUARTER, a.shape[1])),
            out_shape=jax.ShapeDtypeStruct((QUARTER, a.shape[1]), BF16),
            compiler_params=vmem(48),
            cost_estimate=cost(1.5),
            name="pair_sum",
        )(a, b)

    def scatter_near(halves, point):
        keep, send = halves
        if not fast:
            return keep, send, None
        got = after(swap_seq(send), point)
        return keep, got, pair_sum(keep, got, 1)

    def send_far(near):
        return swap_dp(near[2]) if fast else None

    def scatter_far(near, far):
        keep, got, low = near
        if fast:
            return [keep, got, far]
        full = jnp.concatenate([keep, got], axis=0)
        return [lax.psum_scatter(full, ("dp", "seq"), scatter_dimension=0, tiled=True)]

    def swap_high(pieces):
        return [pieces[0]] + [swap_tensor(pieces[k], 2 * k) for k in (1, 2, 3)]

    def scatter_parts(total):
        n = total.shape[0] // 4
        return [total[:n]] + [
            swap_tensor(total[i * n : (i + 1) * n].astype(BF16), mask)
            for i, mask in ((1, 2), (2, 4), (3, 6))
        ]

    def gather_near(own):
        return jnp.concatenate([own] + [swap_tensor(own, mask) for mask in (2, 4, 6)], axis=0)

    attn_low = jnp.concatenate(
        [query_weight, kv_weight, jnp.pad(norm_gains, ((0, 0), (0, 126)))], axis=1
    ).astype(BF16)
    back_low = jnp.concatenate([query_weight, kv_weight], axis=1).astype(BF16)
    output_low = after(output_weight.astype(BF16), attn_low)
    output_near = lax.all_gather(output_low, "tensor", axis=0, axis_index_groups=HIGH_GROUPS)
    token_rows = tokens.reshape(span, D)
    cot_rows = cotangent.reshape(span, D)
    positions = seq_id * span + jnp.arange(span, dtype=jnp.int32)
    cosine, sine = rope_tables(positions)
    attn_w = gather_width(attn_low, attn_low, (cosine, sine))
    half_span = span // 2
    dy = pl.pallas_call(
        reorder_kernel,
        grid_spec=pltpu.PrefetchScalarGridSpec(
            num_scalar_prefetch=1,
            grid=(8,),
            in_specs=[pl.BlockSpec((block, D), lambda i, info: (tensor_block(i, info), 0))],
            out_specs=pl.BlockSpec((2, half_block, D), lambda i, info: (0, i, 0)),
        ),
        out_shape=jax.ShapeDtypeStruct((2, half_span, D), BF16),
        cost_estimate=cost(7.5),
        name="reorder",
    )(info, cot_rows)

    normed_one, queries, kv_own, gains = pl.pallas_call(
        project_kernel,
        grid_spec=pltpu.PrefetchScalarGridSpec(
            num_scalar_prefetch=1,
            grid=(span // rows,),
            in_specs=[pl.BlockSpec((rows, D), lambda i, info: (i, 0))]
            + [whole((QUARTER, 512))] * 4
            + [pl.BlockSpec((rows, 128), lambda i, info: (i, 0))] * 2,
            out_specs=[
                pl.BlockSpec((rows, D), lambda i, info: (i, 0)),
                pl.BlockSpec((rows, 256), lambda i, info: (i, 0)),
                pl.BlockSpec((rows, 128), lambda i, info: (i, 0)),
                whole((8, D)),
            ],
            scratch_shapes=[pltpu.VMEM((8, D), F32)],
        ),
        out_shape=[
            jax.ShapeDtypeStruct((span, D), BF16),
            jax.ShapeDtypeStruct((span, 256), BF16),
            jax.ShapeDtypeStruct((span, 128), BF16),
            jax.ShapeDtypeStruct((8, D), F32),
        ],
        compiler_params=vmem(48),
        cost_estimate=cost(7),
        name="project",
    )(info, token_rows, *attn_w, cosine, sine)

    gate_up_late, down_late = after((gate_up_weight, down_weight), queries)
    gate_up_low = jnp.concatenate(
        [gate_up_late[:, 0, :], gate_up_late[:, 1, :]], axis=1
    ).astype(BF16)
    down_low = down_late.astype(BF16)

    if fast:
        kv_other = swap_seq(kv_own)
        kv_all = jnp.where(
            seq_id == 0,
            jnp.concatenate([kv_own, kv_other], axis=0),
            jnp.concatenate([kv_other, kv_own], axis=0),
        )
    else:
        kv_all = lax.all_gather(kv_own, "seq", axis=0, tiled=True)

    steps = 4
    attended, logs = pl.pallas_call(
        functools.partial(attend_kernel, rows, max(keys, 2 * rows)),
        grid_spec=pltpu.PrefetchScalarGridSpec(
            num_scalar_prefetch=1,
            grid=(steps,),
            in_specs=[
                pl.BlockSpec((rows, 256), lambda i, info: (i, 0)),
                whole((length, 128)),
            ],
            out_specs=[
                pl.BlockSpec((rows, 256), lambda i, info: (i, 0)),
                pl.BlockSpec((1, 1, GROUP * rows), lambda i, info: (i, 0, 0)),
            ],
            scratch_shapes=[
                pltpu.VMEM((128, length), BF16),
                pltpu.VMEM((128, GROUP * rows), F32),
                pltpu.VMEM((1, GROUP * rows), F32),
            ],
        ),
        out_shape=[
            jax.ShapeDtypeStruct((span, 256), BF16),
            jax.ShapeDtypeStruct((steps, 1, GROUP * rows), F32),
        ],
        compiler_params=vmem(48),
        cost_estimate=cost(18),
        name="attend",
    )(info, queries, kv_all)

    mlp_w = gather_all(jnp.concatenate([gate_up_low, down_low], axis=1))
    att_parts = lax.all_to_all(
        attended.reshape(4, rows, 256), "tensor", 0, 0, axis_index_groups=HIGH_GROUPS
    )
    att_parts = after(att_parts, dy)
    output_w = gather_width(after(output_near, queries), att_parts, att_parts)

    out_keep, out_send = pl.pallas_call(
        out_kernel,
        grid_spec=pltpu.PrefetchScalarGridSpec(
            num_scalar_prefetch=1,
            grid=(1,),
            in_specs=[whole((4, rows, 256))] + [whole((4, QUARTER, 256))] * 4,
            out_specs=[whole((block, D))] * 2,
            scratch_shapes=[pltpu.VMEM((rows, QUARTER), F32)],
        ),
        out_shape=[jax.ShapeDtypeStruct((block, D), F32), jax.ShapeDtypeStruct((block, D), BF16)],
        compiler_params=vmem(48),
        cost_estimate=cost(3.8),
        name="attention_out",
    )(info, att_parts, *output_w)
    out_got = swap_tensor(out_send, 1)
    own_rows = pl.BlockSpec((block, D), lambda i, info: (info[AT_TENSOR], 0))
    resid_one, low_a, low_b = pl.pallas_call(
        norm_kernel,
        grid_spec=pltpu.PrefetchScalarGridSpec(
            num_scalar_prefetch=1,
            grid=(1,),
            in_specs=[whole((block, D))] * 2 + [own_rows, whole((8, D))],
            out_specs=[whole((block, D)), whole((half_block, D)), whole((half_block, D))],
        ),
        out_shape=[
            jax.ShapeDtypeStruct((block, D), F32),
            jax.ShapeDtypeStruct((half_block, D), BF16),
            jax.ShapeDtypeStruct((half_block, D), BF16),
        ],
        cost_estimate=cost(3.5),
        name="second_norm",
    )(info, out_keep, out_got, token_rows, gains)

    def mlp(chunk, nears, fars, before):
        n = half_span
        anywhere = pl.BlockSpec(memory_space=pl.ANY)
        late_columns = pl.BlockSpec(
            (4, half_block, QUARTER), lambda i, info: (0, 0, jnp.maximum(i - 4, 0))
        )
        late_half = pl.BlockSpec((n // 2, QUARTER), lambda i, info: (0, jnp.maximum(i - 4, 0)))
        return pl.pallas_call(
            functools.partial(mlp_kernel, len(nears)),
            grid_spec=pltpu.PrefetchScalarGridSpec(
                num_scalar_prefetch=1,
                grid=(8,),
                in_specs=[whole((n // 2 // len(nears), D))] * (2 * len(nears))
                + [pl.BlockSpec((1, n, D), lambda i, info: (chunk, 0, 0))]
                + [anywhere] * (1 + len(before)),
                out_specs=[
                    late_columns,
                    late_columns,
                    late_half,
                    late_half,
                    pl.BlockSpec((n, 1024), lambda i, info: (chunk, 0)),
                    pl.BlockSpec((n, 2048), lambda i, info: (chunk, 0)),
                    pl.BlockSpec((n, D), lambda i, info: (chunk, 0)),
                ],
                scratch_shapes=[
                    pltpu.VMEM((D, 2048), BF16),
                    pltpu.VMEM((D, 1024), BF16),
                    pltpu.SemaphoreType.DMA((4, 3)),
                ],
            ),
            out_shape=[
                jax.ShapeDtypeStruct((4, half_block, D), BF16),
                jax.ShapeDtypeStruct((4, half_block, D), BF16),
                jax.ShapeDtypeStruct((n // 2, D), BF16),
                jax.ShapeDtypeStruct((n // 2, D), BF16),
                jax.ShapeDtypeStruct((span, 1024), BF16),
                jax.ShapeDtypeStruct((span, 2048), BF16),
                jax.ShapeDtypeStruct((span, D), BF16),
            ],
            input_output_aliases={5: 4, 6: 5, 7: 6} if before else {},
            compiler_params=vmem(56),
            cost_estimate=cost(22.5),
            name="mlp",
        )(info, *nears, *fars, dy, mlp_w, *before)

    near_a = gather_near(low_a)
    near_b = gather_near(low_b)
    far_a = after(swap_tensor(near_a, 1), near_b)
    far_b = swap_tensor(near_b, 1)
    mlp_keep_a, mlp_send_a, two_keep_a, two_send_a, hidden, gate_up_back, x = mlp(
        0, (near_a,), (far_a,), ()
    )
    two_got_a = swap_tensor(two_send_a, 1)
    back_low = after(back_low, near_b)
    back_parts = [swap_tensor(back_low, mask) for mask in (2, 4, 6)]
    mlp_keep_b, mlp_send_b, two_keep_b, two_send_b, hidden, gate_up_back, x = mlp(
        1, (near_b,), (far_b,), (hidden, gate_up_back, x)
    )
    two_got_b = swap_tensor(two_send_b, 1)
    total_a = two_keep_a.astype(F32) + after(two_got_a, two_send_b).astype(F32)
    two_a = scatter_parts(total_a)
    back_near = jnp.stack(after([back_low] + back_parts, two_send_b), axis=0)
    hidden, gate_up_back = after((hidden, gate_up_back), (total_a, back_near))
    narrow = pl.BlockSpec((span, QUARTER), lambda i: (0, i))
    mlp_full = pl.pallas_call(
        mlp_grad_kernel,
        grid=(4,),
        in_specs=[narrow, whole((span, 2048)), narrow, whole((span, 1024))],
        out_specs=pl.BlockSpec((QUARTER, 3072), lambda i: (i, 0)),
        out_shape=jax.ShapeDtypeStruct((D, 3072), BF16),
        compiler_params=vmem(56),
        cost_estimate=cost(22),
        name="mlp_grad",
    )(x, gate_up_back, dy.reshape(span, D), hidden)
    total_b = two_keep_b.astype(F32) + after(
        two_got_b, (mlp_full, two_a)
    ).astype(F32)
    two_b = scatter_parts(total_b)
    mlp_grad = scatter_all(after(mlp_full, total_b))
    mlp_got_a = swap_tensor(after(mlp_send_a, total_b), 1)

    resid_grad, resid_low, gain_two_grad = pl.pallas_call(
        norm_back_kernel,
        grid_spec=pltpu.PrefetchScalarGridSpec(
            num_scalar_prefetch=1,
            grid=(1,),
            in_specs=[whole((half_block, D))] * 8
            + [
                whole((block, D)),
                pl.BlockSpec((2, half_block, D), lambda i, info: (0, 0, 0)),
                whole((8, D)),
            ],
            out_specs=[whole((block, D)), whole((block, D)), whole((1, D))],
        ),
        out_shape=[
            jax.ShapeDtypeStruct((block, D), F32),
            jax.ShapeDtypeStruct((block, D), BF16),
            jax.ShapeDtypeStruct((1, D), F32),
        ],
        cost_estimate=cost(4.7),
        name="second_norm_back",
    )(info, *two_a, *two_b, resid_one, dy, gains)
    resid_other = swap_tensor(resid_low, 1)
    mlp_total_a = (mlp_keep_a.astype(F32) + after(mlp_got_a, resid_low).astype(F32)).astype(BF16)
    mlp_parts_a = lax.all_to_all(mlp_total_a, "tensor", 0, 0, axis_index_groups=HIGH_GROUPS)
    resid_other = after(resid_other, mlp_total_a)
    mlp_got_b = swap_tensor(after(mlp_send_b, resid_other), 1)
    resid_both, *grad_pieces = pl.pallas_call(
        out_back_kernel,
        grid_spec=pltpu.PrefetchScalarGridSpec(
            num_scalar_prefetch=1,
            grid=(1,),
            in_specs=[whole((block, D))] * 2 + [whole((4, QUARTER, 256))] * 4,
            out_specs=[whole((rows, D))] + [whole((rows, 256))] * 4,
        ),
        out_shape=[jax.ShapeDtypeStruct((rows, D), BF16)]
        + [jax.ShapeDtypeStruct((rows, 256), BF16)] * 4,
        compiler_params=vmem(48),
        cost_estimate=cost(3.9),
        name="attention_out_back",
    )(info, resid_low, resid_other, *output_w)
    grad_parts = swap_high(grad_pieces)
    mlp_total_b = (mlp_keep_b.astype(F32) + after(mlp_got_b, grad_parts).astype(F32)).astype(BF16)
    mlp_parts_b = lax.all_to_all(mlp_total_b, "tensor", 0, 0, axis_index_groups=HIGH_GROUPS)
    back_w = gather_width(back_near, resid_low, resid_low)
    grad_parts = after(grad_parts, (mlp_total_b, back_w))

    spans = seq_size if fast else length // span
    dq, *dq_pieces, dkv = pl.pallas_call(
        functools.partial(attend_back_kernel, rows, keys, spans),
        grid_spec=pltpu.PrefetchScalarGridSpec(
            num_scalar_prefetch=1,
            grid=(steps,),
            in_specs=[pl.BlockSpec((rows, 256), lambda i, info: (i, 0))]
            + [whole((rows, 256))] * 4
            + [
                pl.BlockSpec((rows, 256), lambda i, info: (i, 0)),
                pl.BlockSpec((1, 1, GROUP * rows), lambda i, info: (i, 0, 0)),
                whole((length, 128)),
                pl.BlockSpec((rows, 128), lambda i, info: (i, 0)),
                pl.BlockSpec((rows, 128), lambda i, info: (i, 0)),
            ],
            out_specs=[pl.BlockSpec((rows, 256), lambda i, info: (i, 0))]
            + [whole((rows, 256))] * 4
            + [whole((spans, span, 128))],
            scratch_shapes=[
                pltpu.VMEM((HEAD_DIM, length), BF16),
                pltpu.VMEM((length, 128), F32),
                pltpu.VMEM((HEAD_DIM, GROUP * rows), F32),
                pltpu.VMEM((rows, 256), BF16),
            ],
        ),
        out_shape=[jax.ShapeDtypeStruct((span, 256), BF16)]
        + [jax.ShapeDtypeStruct((rows, 256), BF16)] * 4
        + [jax.ShapeDtypeStruct((spans, span, 128), BF16)],
        compiler_params=vmem(48),
        cost_estimate=cost(23),
        name="attend_back",
    )(info, queries, *grad_parts, attended, logs, kv_all, cosine, sine)

    if fast:
        dkv_own, dkv_more = dkv[0], swap_seq(dkv[1])
    else:
        dkv_own = lax.psum_scatter(dkv.reshape(length, 128), "seq", scatter_dimension=0, tiled=True)
        dkv_more = jnp.zeros_like(dkv_own)
    dq_parts = swap_high(dq_pieces)
    dkv_more = after(dkv_more, dq_parts)
    dkv_low, *dkv_pieces = pl.pallas_call(
        kv_back_kernel,
        grid_spec=pltpu.PrefetchScalarGridSpec(
            num_scalar_prefetch=1,
            grid=(1,),
            in_specs=[whole((span, 128))] * 4,
            out_specs=[whole((span, 128))] + [whole((rows, 128))] * 4,
        ),
        out_shape=[jax.ShapeDtypeStruct((span, 128), BF16)]
        + [jax.ShapeDtypeStruct((rows, 128), BF16)] * 4,
        cost_estimate=cost(3.2),
        name="kv_back",
    )(info, dkv_own, dkv_more, cosine, sine)

    dkv_parts = swap_high(dkv_pieces)
    block_low = pl.pallas_call(
        block_out_kernel,
        out_shape=jax.ShapeDtypeStruct((block, D), BF16),
        cost_estimate=cost(3),
        name="block_out",
    )(*after((mlp_parts_a, mlp_parts_b), dkv_low), resid_one)
    dkv_parts = after(dkv_parts, (mlp_grad, block_low))
    one_keep, one_send = pl.pallas_call(
        one_kernel,
        grid_spec=pltpu.PrefetchScalarGridSpec(
            num_scalar_prefetch=1,
            grid=(1,),
            in_specs=[whole((rows, 256))] * 4
            + [whole((rows, 128))] * 4
            + [whole((4, QUARTER, 384))] * 4,
            out_specs=[whole((block, D))] * 2,
            scratch_shapes=[pltpu.VMEM((rows, QUARTER), F32)],
        ),
        out_shape=[jax.ShapeDtypeStruct((block, D), F32), jax.ShapeDtypeStruct((block, D), BF16)],
        compiler_params=vmem(48),
        cost_estimate=cost(5.8),
        name="attention_in_back",
    )(info, *dq_parts, *dkv_parts, *back_w)
    one_got = swap_tensor(one_send, 1)
    dqkv = after(jnp.concatenate([dq, dkv_low], axis=1), one_send)
    attn_halves = weight_halves(normed_one, dqkv)
    out_halves = weight_halves(
        after(resid_both, one_send), jnp.concatenate(by_xor(att_parts), axis=1)
    )

    block_near = lax.all_gather(block_low, "tensor", axis=0, axis_index_groups=HIGH_GROUPS)
    one_got = after(one_got, (attn_halves, out_halves))
    out_near = scatter_near(out_halves, one_got)
    out_far = send_far(out_near)

    tokens_low = pl.pallas_call(
        tokens_back_kernel,
        grid_spec=pltpu.PrefetchScalarGridSpec(
            num_scalar_prefetch=1,
            grid=(1,),
            in_specs=[whole((block, D))] * 2 + [own_rows, whole((block, D)), whole((8, D))],
            out_specs=whole((block, D)),
        ),
        out_shape=jax.ShapeDtypeStruct((block, D), BF16),
        cost_estimate=cost(4.3),
        name="first_norm_back",
    )(info, one_keep, one_got, token_rows, resid_grad, gains)
    tokens_own = swap_tensor(tokens_low, 1)
    tokens_near = lax.all_gather(tokens_low, "tensor", axis=0, axis_index_groups=HIGH_GROUPS)

    attn_near = scatter_near(attn_halves, one_send)
    attn_far = send_far(attn_near)

    def adam(weight, one, two, terms, rate, decay):
        size = weight.shape[0] // 4
        if weight.ndim == 3:
            mine = pl.BlockSpec((size, 2, weight.shape[2]), lambda i: (i, 0, 0))
            wide = 2 * weight.shape[2]
        else:
            mine = pl.BlockSpec((size, weight.shape[1]), lambda i: (i, 0))
            wide = weight.shape[1]
        return pl.pallas_call(
            functools.partial(adam_kernel, rate, decay),
            grid=(4,),
            in_specs=[mine] * 3
            + [
                pl.BlockSpec((size, wide), lambda i, column=column: (i, column))
                for term, column in terms
            ],
            out_specs=[mine] * 3,
            out_shape=[jax.ShapeDtypeStruct(weight.shape, F32)] * 3,
            compiler_params=vmem(56),
            cost_estimate=cost(weight.size / 75000),
            name="adam",
        )(weight, one, two, *[term for term, column in terms])

    fan_in = RATE_FACTOR * D ** (-0.5)
    mlp_grad = after(mlp_grad, tokens_low)
    gate_up_new = adam(
        gate_up_weight, gate_up_first, gate_up_second, [(mlp_grad, 0)], fan_in, DECAY
    )
    down_new = adam(
        down_weight, down_first, down_second, [(mlp_grad, 2)], RATE_FACTOR * FF ** (-0.5), DECAY
    )

    products = jnp.concatenate(
        [
            jnp.sum(
                attn_halves[i // 2][(i % 2) * QUARTER : (i % 2 + 1) * QUARTER].astype(F32)
                * w[:, :384].astype(F32),
                axis=1,
            )
            / w[:, 384].astype(F32)
            for i, w in enumerate(attn_w)
        ]
    )
    gain_grads = jnp.stack(
        [
            products,
            jnp.concatenate(
                [lax.dynamic_slice(gain_two_grad[0], (info[i] * QUARTER,), (QUARTER,)) for i in range(4)]
            ),
        ]
    )
    if fast:
        gain_grads = gain_grads[:, : 2 * QUARTER] + swap_seq(gain_grads[:, 2 * QUARTER :])
        gain_got = swap_tensor(gain_grads, 1)
    else:
        shard = norm_gains.shape[0]
        gains_grad = lax.dynamic_slice(
            lax.psum(gain_grads, ("dp", "seq")),
            (0, (dp_id * seq_size + seq_id) * shard),
            (2, shard),
        )
        gain_grads = gains_grad
        gain_got = swap_tensor(gains_grad, 1)
    block_far = swap_tensor(after(block_near, tokens_own), 1)
    gain_grads = gain_grads + gain_got
    early = (gate_up_new, down_new, gain_grads) + ((out_far, attn_far) if fast else ())
    tokens_near = after(tokens_near, early)
    tokens_far = swap_tensor(others(tokens_near), 1)

    attn_terms = after(scatter_far(attn_near, attn_far), tokens_near)
    query_new = adam(
        query_weight, query_first, query_second, [(term, 0) for term in attn_terms], fan_in, DECAY
    )
    kv_new = adam(kv_weight, kv_first, kv_second, [(term, 2) for term in attn_terms], fan_in, DECAY)

    out_terms = scatter_far(out_near, out_far)
    out_rows = sum(term[: out_terms[-1].shape[0]].astype(F32) for term in after(out_terms, tokens_near))
    output_terms = swap_high([out_rows[:, k * 256 : (k + 1) * 256].astype(BF16) for k in range(4)])
    output_new = adam(
        output_weight,
        output_first,
        output_second,
        [(term, 0) for term in output_terms],
        RATE_FACTOR * FAN_OUT ** (-0.5),
        DECAY,
    )

    gain_grads = after(gain_grads, tokens_near)
    if fast:
        gains_grad = gain_grads[:, :QUARTER] + swap_dp(gain_grads[:, QUARTER:])
    else:
        gains_grad = gain_grads
    for mask in (2, 4):
        gains_grad = gains_grad + swap_tensor(gains_grad, mask)
    gains_grad = gains_grad.T
    gains_new = adam_step(norm_gains, gains_grad, gains_first, gains_second, GAIN_RATE, 0.0)


    def place(parts, dtype, name):
        return pl.pallas_call(
            place_kernel,
            grid_spec=pltpu.PrefetchScalarGridSpec(
                num_scalar_prefetch=1,
                grid=(4,),
                in_specs=[pl.BlockSpec((1, block, D), lambda i, info: (i, 0, 0))] * 2,
                out_specs=pl.BlockSpec((rows, D), lambda i, info: (i, 0)),
            ),
            out_shape=jax.ShapeDtypeStruct((span, D), dtype),
            compiler_params=vmem(48),
            cost_estimate=cost(5),
            name=name,
        )(info, *parts).reshape(tokens.shape)

    def place_own(parts, dtype, name):
        return pl.pallas_call(
            place_own_kernel,
            grid_spec=pltpu.PrefetchScalarGridSpec(
                num_scalar_prefetch=1,
                grid=(4,),
                in_specs=[
                    pl.BlockSpec(
                        (1, block, D), lambda i, info: (lax.bitwise_xor(info[AT_HIGH], i), 0, 0)
                    ),
                    whole((block, D)),
                    pl.BlockSpec((1, block, D), lambda i, info: (jnp.maximum(i - 1, 0), 0, 0)),
                ],
                out_specs=pl.BlockSpec(
                    (rows, D), lambda i, info: (lax.bitwise_xor(info[AT_HIGH], i), 0)
                ),
            ),
            out_shape=jax.ShapeDtypeStruct((span, D), dtype),
            compiler_params=vmem(48),
            cost_estimate=cost(5),
            name=name,
        )(info, *parts).reshape(tokens.shape)

    tokens_grad = place_own((tokens_near, tokens_own, tokens_far), F32, "tokens_grad")
    block_out = place((block_near, block_far), BF16, "block_out_rows")

    results = (query_new, output_new, kv_new, gate_up_new, down_new, gains_new)
    return (block_out, tokens_grad) + tuple(r[i] for i in range(3) for r in results)


def solution(mesh):
    wide = P(("dp", "seq"), "tensor")
    weights = (wide, wide, wide, P(("dp", "seq"), None, "tensor"), wide, P(("dp", "seq"), None))
    rows = P("dp", "seq", None)
    return jax.shard_map(
        functools.partial(body, dp_size=mesh.shape["dp"], seq_size=mesh.shape["seq"]),
        mesh=mesh,
        in_specs=(rows, rows) + weights * 3,
        out_specs=(rows, rows) + weights * 3,
        check_vma=False,
    )
```

```python
import functools

import jax
import jax.numpy as jnp
from jax import lax
from jax.experimental import pallas as pl
from jax.experimental.pallas import tpu as pltpu
from jax.sharding import PartitionSpec as P

D = 2048
FF = 8192
HEADS = 32
KV_HEADS = 8
HEAD_DIM = 64
STEP = 10
FAN_OUT = 2

EPS_NORM = 1e-05
ROPE_BASE = 500000.0
BETA_ONE = 0.9
BETA_TWO = 0.95
ADAM_EPS = 1e-08
DECAY = 0.1
RATE_FACTOR = 3.0
GAIN_RATE = 1.0
MASKED = -1e30

F32 = jnp.float32
BF16 = jnp.bfloat16
GROUP = HEADS // KV_HEADS
QUARTER = D // 4
ORDER = (0, 2, 4, 6, 1, 3, 5, 7)
WIDTH_ORDER = (0, 2, 1, 3)
HIGH_GROUPS = [[0, 2, 4, 6], [1, 3, 5, 7]]
AT_TENSOR, AT_OFFSET, AT_SEQ, AT_LOW, AT_HIGH = 4, 5, 6, 7, 8


def vmem(mib):
    return pltpu.CompilerParams(vmem_limit_bytes=mib * 1024 * 1024)


COST_SCALE = 0.5


def cost(us):
    return pl.CostEstimate(flops=0, bytes_accessed=int(COST_SCALE * us * 3.69e6), transcendentals=0)


def dot(a, b):
    return lax.dot_general(a, b, (((1,), (0,)), ((), ())), preferred_element_type=F32)


def dot_nt(a, b):
    return lax.dot_general(a, b, (((1,), (1,)), ((), ())), preferred_element_type=F32)


def swap_halves(values):
    lane = lax.broadcasted_iota(jnp.int32, values.shape, 1)
    half = HEAD_DIM // 2
    return jnp.where(
        lane % HEAD_DIM < half,
        pltpu.roll(values, 128 - half, 1),
        pltpu.roll(values, half, 1),
    )


def width_block(info, place):
    return pl.ds(pl.multiple_of(info[place] * QUARTER, QUARTER), QUARTER)


def project_kernel(info, tok, w0, w1, w2, w3, cosine, sine, normed, q_out, kv_out, gains, gain_rows):
    pieces = (w0, w1, w2, w3)

    @pl.when(pl.program_id(0) == 0)
    def _():
        for place, piece in enumerate(pieces):
            turned = piece[:, 384:512].astype(F32).T
            gain_rows[:, place * QUARTER : (place + 1) * QUARTER] = turned[0:8]
        natural_store(info, gains, gain_rows[...])

    parts = [tok[:, width_block(info, place)].astype(F32) for place in range(4)]
    square = sum(jnp.sum(part * part, axis=1, keepdims=True) for part in parts)
    inverse = lax.rsqrt(square * (1.0 / D) + EPS_NORM)
    total = None
    for place, (part, piece) in enumerate(zip(parts, pieces)):
        cols = slice(place * QUARTER, (place + 1) * QUARTER)
        low = (part * inverse * gain_rows[0:1, cols]).astype(BF16)
        normed[:, cols] = low
        term = dot(low, piece[:, 0:384])
        total = term if total is None else total + term
    cos, sin = cosine[...], sine[...]
    for c in (0, 128):
        raw = total[:, c : c + 128]
        q_out[:, c : c + 128] = (raw * cos + swap_halves(raw) * sin).astype(BF16)
    raw = total[:, 256:384]
    turned = raw * cos + swap_halves(raw) * sin
    lane = lax.broadcasted_iota(jnp.int32, raw.shape, 1)
    kv_out[...] = jnp.where(lane < HEAD_DIM, turned, raw).astype(BF16)


def heads_wide(turned):
    return jnp.concatenate(
        [turned[h * HEAD_DIM : (h + 1) * HEAD_DIM] for h in range(GROUP)], axis=1
    )


def heads_tall(wide, rows):
    return jnp.concatenate([wide[:, h * rows : (h + 1) * rows] for h in range(GROUP)], axis=0)


def diagonal_mask(rows, keys, shift):
    key = lax.broadcasted_iota(jnp.int32, (keys, GROUP * rows), 0)
    query = lax.broadcasted_iota(jnp.int32, (keys, GROUP * rows), 1) % rows
    return key <= query + shift


def diagonal_block(rows, keys, step, info):
    start = info[AT_OFFSET] + step
    ratio = keys // rows
    diagonal = lax.div(start, jnp.int32(ratio))
    return diagonal, (start - diagonal * ratio) * rows


def attend_kernel(
    rows, keys, info, q, kv, out, log_out, kv_turned, acc, high
):
    step = pl.program_id(0)

    @pl.when(step == 0)
    def _():
        turned = kv[...].T
        row = lax.broadcasted_iota(jnp.int32, turned.shape, 0)
        kv_turned[...] = jnp.where(row < HEAD_DIM, jnp.ones_like(turned), turned)

    wide = heads_wide((q[...] * (HEAD_DIM**-0.5)).astype(F32).T).astype(BF16)
    wide = jnp.concatenate([wide, jnp.zeros_like(wide)], axis=0)
    diagonal, shift = diagonal_block(rows, keys, step, info)

    def scores_of(j):
        return dot(kv[pl.ds(pl.multiple_of(j * keys, keys), keys), :], wide)

    def values_of(j):
        return kv_turned[:, pl.ds(pl.multiple_of(j * keys, keys), keys)]

    scores = jnp.where(diagonal_mask(rows, keys, shift), scores_of(diagonal), MASKED)
    top = jnp.max(scores, axis=0, keepdims=True)
    high[...] = top
    acc[...] = dot(values_of(diagonal), jnp.exp(scores - top).astype(BF16))

    def body(j, carry):
        scores = scores_of(j)
        old = high[...]
        top = jnp.maximum(old, jnp.max(scores, axis=0, keepdims=True))
        high[...] = top
        chances = jnp.exp(scores - top).astype(BF16)
        acc[...] = acc[...] * jnp.exp(old - top) + dot(values_of(j), chances)
        return carry

    lax.fori_loop(0, diagonal, body, 0)
    total = acc[0:1, :]
    log_out[0] = high[...] + jnp.log(total)
    result = acc[HEAD_DIM:, :] * (1.0 / total)
    out[...] = heads_tall(result, rows).T.astype(BF16)


def attend_back_kernel(
    rows, keys, spans, info, q, grad0, grad1, grad2, grad3, att, log_in, kv, cosine, sine,
    dq_out, piece0, piece1, piece2, piece3, dkv_out, kv_turned, dkv, dq_acc, grad,
):
    step = pl.program_id(0)

    @pl.when(step == 0)
    def _():
        kv_turned[...] = kv[...].T[0:HEAD_DIM]
        dkv[...] = jnp.zeros_like(dkv)

    for k, piece in enumerate((grad0, grad1, grad2, grad3)):

        @pl.when(lax.bitwise_xor(step, info[AT_HIGH]) == k)
        def _():
            grad[...] = piece[...]

    scaled = q[...] * (HEAD_DIM**-0.5)
    grads = grad[...]
    zero_tall = jnp.zeros((GROUP * rows, HEAD_DIM), BF16)
    q_tall = jnp.concatenate(
        [scaled[:, h * HEAD_DIM : (h + 1) * HEAD_DIM] for h in range(GROUP)], axis=0
    ).astype(BF16)
    g_tall = jnp.concatenate(
        [grads[:, h * HEAD_DIM : (h + 1) * HEAD_DIM] for h in range(GROUP)], axis=0
    )
    q_tall = jnp.concatenate([q_tall, zero_tall], axis=1)
    g_tall = jnp.concatenate([zero_tall, g_tall], axis=1)
    q_wide = heads_wide(scaled.astype(F32).T).astype(BF16)
    g_turned = grads.astype(F32).T
    g_wide = heads_wide(g_turned).astype(BF16)
    zero_wide = jnp.zeros_like(g_wide)
    product = heads_wide(g_turned * att[...].astype(F32).T)
    delta = jnp.sum(product, axis=0, keepdims=True)
    q_wide = jnp.concatenate([q_wide, zero_wide], axis=0)
    g_wide = jnp.concatenate([zero_wide, g_wide], axis=0)
    logs = log_in[0]
    diagonal, shift = diagonal_block(rows, keys, step, info)

    def one_block(j, mask):
        place = pl.ds(pl.multiple_of(j * keys, keys), keys)
        block = kv[place, :]
        chances = jnp.exp(dot(block, q_wide) - logs)
        if mask is not None:
            chances = jnp.where(mask, chances, 0.0)
        chance_grad = dot(block, g_wide)
        score_grad = (chances * (chance_grad - delta)).astype(BF16)
        dkv[place, :] += dot(score_grad, q_tall) + dot(chances.astype(BF16), g_tall)
        return dot(kv_turned[:, place], score_grad)

    dq_acc[...] = one_block(diagonal, diagonal_mask(rows, keys, shift))

    def body(j, carry):
        dq_acc[...] += one_block(j, None)
        return carry

    lax.fori_loop(0, diagonal, body, 0)
    dq = heads_tall(dq_acc[...] * (HEAD_DIM**-0.5), rows).T
    cos, sin = cosine[...], sine[...]
    for c in (0, 128):
        raw = dq[:, c : c + 128]
        dq_out[:, c : c + 128] = (raw * cos - swap_halves(raw) * sin).astype(BF16)
    for k, piece in enumerate((piece0, piece1, piece2, piece3)):

        @pl.when(lax.bitwise_xor(step, info[AT_HIGH]) == k)
        def _():
            piece[...] = dq_out[...]

    @pl.when(step == pl.num_programs(0) - 1)
    def _():
        span = dkv_out.shape[1]
        for r in range(spans):
            at = lax.bitwise_xor(info[AT_SEQ], jnp.int32(r)) * span
            dkv_out[r] = dkv[pl.ds(pl.multiple_of(at, span), span), :].astype(BF16)


def out_kernel(info, att, w0, w1, w2, w3, keep, send, total):
    half = keep.shape[0]
    low = info[AT_LOW]
    for place, w in enumerate((w0, w1, w2, w3)):
        cols = width_block(info, place)
        total[...] = sum(dot_nt(att[k], w[k]) for k in range(4))
        keep[:, cols] = total[pl.ds(pl.multiple_of(low * half, half), half), :]
        send[:, cols] = total[pl.ds(pl.multiple_of((1 - low) * half, half), half), :].astype(BF16)


def norm_kernel(info, keep, got, tok, gains, resid_out, low_a, low_b):
    resid = tok[...].astype(F32) + keep[...] + got[...].astype(F32)
    resid_out[...] = resid
    inverse = lax.rsqrt(jnp.mean(resid * resid, axis=1, keepdims=True) + EPS_NORM)
    low = (resid * inverse * gains[1:2, :]).astype(BF16)
    half = low.shape[0] // 2
    low_a[...] = low[:half]
    low_b[...] = low[half:]


def mlp_kernel(
    parts, info, *refs,
):
    sources, (dy, weights, *rest) = refs[: 2 * parts], refs[2 * parts :]
    mlp_keep, mlp_send, two_keep, two_send, hidden_out, grad_out, x, gate_up, down, sems = rest[-10:]
    step = pl.program_id(0)
    wide = FF // 8
    n = x.shape[0]

    def copies(group):
        cols = pl.ds(group * 256, 256)
        up_cols = pl.ds(wide + group * 256, 256)
        for k, (src, dst, c) in enumerate(
            ((cols, gate_up, cols), (up_cols, gate_up, up_cols), (pl.ds(2 * wide + group * 256, 256), down, cols))
        ):
            yield pltpu.make_async_copy(weights.at[:, src], dst.at[:, c], sems.at[group, k])

    @pl.when(step == 0)
    def _():
        for group in range(4):
            for copy in copies(group):
                copy.start()
        size = n // 8
        piece = size // parts
        for i, source in enumerate(sources):
            half, part = divmod(i, parts)
            for k in range(4):
                at = (half * 4 + k) * size + part * piece
                x[at : at + piece] = source[k * piece : (k + 1) * piece]

    for group in range(4):

        @pl.when(step == group)
        def _():
            for copy in copies(group):
                copy.wait()
            cols = slice(group * 256, (group + 1) * 256)
            up_cols = slice(wide + group * 256, wide + (group + 1) * 256)
            gate = dot(x[...], gate_up[:, cols])
            up = dot(x[...], gate_up[:, up_cols])
            hidden_grad = dot(dy[0], down[:, cols])
            sigmoid = 1.0 / (1.0 + jnp.exp(-gate))
            silu = gate * sigmoid
            hidden_out[:, cols] = (silu * up).astype(BF16)
            grad_out[:, cols] = (
                hidden_grad * up * (sigmoid * (1.0 + gate * (1.0 - sigmoid)))
            ).astype(BF16)
            grad_out[:, up_cols] = (hidden_grad * silu).astype(BF16)

    @pl.when(step >= 4)
    def _():
        rows = pl.ds(pl.multiple_of((step - 4) * QUARTER, QUARTER), QUARTER)
        two = dot_nt(grad_out[...], gate_up[rows, :]).astype(BF16)
        two_keep[...] = two[: n // 2]
        two_send[...] = two[n // 2 :]
        mlp = dot_nt(hidden_out[...], down[rows, :]).astype(BF16)
        size = n // 8
        for i in range(4):
            owner = lax.bitwise_xor(info[AT_HIGH], jnp.int32(i))
            mlp_keep[owner] = mlp[i * size : (i + 1) * size]
            mlp_send[owner] = mlp[n // 2 + i * size : n // 2 + (i + 1) * size]


def norm_back(values, incoming, gain):
    inverse = lax.rsqrt(jnp.mean(values * values, axis=1, keepdims=True) + EPS_NORM)
    scaled = incoming * gain
    gain_grad = jnp.sum(incoming * values * inverse, axis=0, keepdims=True)
    inner = jnp.mean(scaled * values, axis=1, keepdims=True)
    return inverse * scaled - values * (inverse * inverse * inverse * inner), gain_grad


def summed(parts):
    return sum(part[...].astype(F32) for part in parts)


def norm_back_kernel(info, *refs):
    parts_a, parts_b = refs[0:4], refs[4:8]
    resid, dy, gains, resid_grad, resid_low, gain_grad = refs[8:]
    half = dy.shape[1]
    sums = []
    for i, parts in enumerate((parts_a, parts_b)):
        rows = slice(i * half, (i + 1) * half)
        back, gain_part = norm_back(resid[rows], summed(parts), gains[1:2, :])
        full = dy[i].astype(F32) + back
        resid_grad[rows] = full
        resid_low[rows] = full.astype(BF16)
        sums.append(gain_part)
    gain_grad[...] = sums[0] + sums[1]


def out_back_kernel(info, own, other, w0, w1, w2, w3, both, g0, g1, g2, g3):
    half = own.shape[0]
    low = info[AT_LOW]
    for place in range(4):
        cols = slice(place * QUARTER, (place + 1) * QUARTER)
        natural = width_block(info, place)
        both[pl.ds(pl.multiple_of(low * half, half), half), cols] = own[:, natural]
        both[pl.ds(pl.multiple_of((1 - low) * half, half), half), cols] = other[:, natural]
    for k, out in enumerate((g0, g1, g2, g3)):
        high = lax.bitwise_xor(info[AT_HIGH], jnp.int32(k))
        out[...] = sum(
            dot(both[:, place * QUARTER : (place + 1) * QUARTER], w[high])
            for place, w in enumerate((w0, w1, w2, w3))
        ).astype(BF16)


def natural_store(info, out, value):
    for place in range(4):
        out[:, width_block(info, place)] = value[:, place * QUARTER : (place + 1) * QUARTER]


def kv_back_kernel(info, dkv, dkv_more, cosine, sine, out, p0, p1, p2, p3):
    raw = dkv[...].astype(F32) + dkv_more[...].astype(F32)
    turned = raw * cosine[...] - swap_halves(raw) * sine[...]
    lane = lax.broadcasted_iota(jnp.int32, raw.shape, 1)
    out[...] = jnp.where(lane < HEAD_DIM, turned, raw).astype(BF16)
    rows = p0.shape[0]
    for k, piece in enumerate((p0, p1, p2, p3)):
        at = lax.bitwise_xor(info[AT_HIGH], jnp.int32(k)) * rows
        piece[...] = out[pl.ds(pl.multiple_of(at, rows), rows), :]


def one_kernel(info, q0, q1, q2, q3, k0, k1, k2, k3, w0, w1, w2, w3, keep, send, total):
    half = keep.shape[0]
    low = info[AT_LOW]
    both = [
        jnp.concatenate([q[...], k[...]], axis=1)
        for q, k in zip((q0, q1, q2, q3), (k0, k1, k2, k3))
    ]
    for place, w in enumerate((w0, w1, w2, w3)):
        cols = width_block(info, place)
        total[...] = sum(
            dot_nt(part, w[k]) for k, part in enumerate(both)
        )
        keep[:, cols] = total[pl.ds(pl.multiple_of(low * half, half), half), :]
        send[:, cols] = total[pl.ds(pl.multiple_of((1 - low) * half, half), half), :].astype(BF16)


def tokens_back_kernel(info, keep, got, tok, resid_grad, gains, low):
    back, unused = norm_back(
        tok[...].astype(F32), keep[...] + got[...].astype(F32), gains[0:1, :]
    )
    low[...] = (resid_grad[...] + back).astype(BF16)


def block_out_kernel(parts_a, parts_b, resid, low):
    half = parts_a.shape[1]
    for i, parts in enumerate((parts_a, parts_b)):
        rows = slice(i * half, (i + 1) * half)
        low[rows] = (sum(parts[k].astype(F32) for k in range(4)) + resid[rows]).astype(BF16)


def reorder_kernel(info, src, out):
    half = out.shape[1]
    out[0] = src[:half]
    out[1] = src[half:]


def place_kernel(info, near, far, out):
    size = near.shape[1]
    at = info[AT_LOW] * size
    out[pl.ds(pl.multiple_of(at, size), size), :] = near[0].astype(out.dtype)
    out[pl.ds(pl.multiple_of(size - at, size), size), :] = far[0].astype(out.dtype)


def place_own_kernel(info, near, own, out):
    size = near.shape[1]
    at = info[AT_LOW] * size
    out[pl.ds(pl.multiple_of(at, size), size), :] = near[0].astype(out.dtype)
    other = pl.ds(pl.multiple_of(size - at, size), size)

    @pl.when(pl.program_id(0) == 0)
    def _():
        out[other, :] = own[...].astype(out.dtype)


def place_far_kernel(info, placed, far, out):
    out[...] = far[0].astype(out.dtype)


def weight_grad_kernel(a, b, *outs):
    result = lax.dot_general(
        a[...], b[...], (((0,), (0,)), ((), ())), preferred_element_type=F32
    ).astype(BF16)
    if len(outs) == 1:
        outs[0][...] = result
        return

    @pl.when(pl.program_id(0) < 2)
    def _():
        outs[0][...] = result

    @pl.when(pl.program_id(0) >= 2)
    def _():
        outs[1][...] = result


def mlp_grad_kernel(x, gate_up_back, dy, hidden, out):
    for a, b, cols in (
        (x, gate_up_back, slice(0, gate_up_back.shape[1])),
        (dy, hidden, slice(gate_up_back.shape[1], out.shape[1])),
    ):
        out[:, cols] = lax.dot_general(
            a[...], b[...], (((0,), (0,)), ((), ())), preferred_element_type=F32
        ).astype(BF16)


def pair_sum_kernel(a, b, out):
    out[...] = (a[...].astype(F32) + b[...].astype(F32)).astype(BF16)


def adam_kernel(rate, decay, weight, one, two, *refs):
    outs = refs[-3:]
    if len(weight.shape) == 2:
        grad = summed(refs[:-3])
        results = adam_step(weight[...], grad, one[...], two[...], rate, decay)
        for out, result in zip(outs, results):
            out[...] = result
        return
    wide = weight.shape[2]
    for k in range(2):
        cols = slice(k * wide, (k + 1) * wide)
        grad = sum(ref[:, cols].astype(F32) for ref in refs[:-3])
        results = adam_step(weight[:, k, :], grad, one[:, k, :], two[:, k, :], rate, decay)
        for out, result in zip(outs, results):
            out[:, k, :] = result


def step_owner(step):
    return lax.rem(step, 4) * 2 + lax.div(step, 4)


def tensor_block(step, info):
    return lax.bitwise_xor(info[AT_TENSOR], step_owner(step))


def adam_step(weight, grad_sum, moment_one, moment_two, step_rate, decay_rate):
    first_new = BETA_ONE * moment_one + (1.0 - BETA_ONE) * grad_sum
    second_new = BETA_TWO * moment_two + (1.0 - BETA_TWO) * grad_sum * grad_sum
    first_hat = first_new / (1.0 - BETA_ONE**STEP)
    second_hat = second_new / (1.0 - BETA_TWO**STEP)
    updated = weight - step_rate * (
        first_hat / (jnp.sqrt(second_hat) + ADAM_EPS) + decay_rate * weight
    )
    return (updated, first_new, second_new)


def rope_tables(positions):
    half_dim = HEAD_DIM // 2
    exponent = jnp.arange(half_dim, dtype=F32) * (2.0 / HEAD_DIM)
    inverse = jnp.power(F32(ROPE_BASE), -exponent)
    angles = positions.astype(F32)[:, None] * inverse[None, :]
    cosine, sine = jnp.cos(angles), jnp.sin(angles)
    return (
        jnp.concatenate([cosine] * 4, axis=1),
        jnp.concatenate([-sine, sine, -sine, sine], axis=1),
    )


def whole(shape, dims=None):
    zeros = (0,) * len(shape)
    return pl.BlockSpec(shape, lambda *unused: zeros)


def body(
    tokens, cotangent, query_weight, output_weight, kv_weight, gate_up_weight, down_weight, norm_gains,
    query_first, output_first, kv_first, gate_up_first, down_first, gains_first,
    query_second, output_second, kv_second, gate_up_second, down_second, gains_second,
    *, dp_size, seq_size,
):
    fast = dp_size == 2 and seq_size == 2
    span = tokens.shape[1]
    length = span * seq_size
    rows = span // 4
    keys = max(rows, 128)
    block = span // 8
    half_block = block // 2
    tensor_id = lax.axis_index("tensor").astype(jnp.int32)
    seq_id = lax.axis_index("seq").astype(jnp.int32)
    dp_id = lax.axis_index("dp").astype(jnp.int32)
    own_width = dp_id * 2 + seq_id if fast else jnp.int32(0)
    order = WIDTH_ORDER if fast else (0, 1, 2, 3)
    info = jnp.stack(
        [lax.bitwise_xor(own_width, jnp.int32(o)) for o in order]
        + [tensor_id, seq_id * 4, seq_id if fast else jnp.int32(0), tensor_id % 2, tensor_id // 2]
    )

    def by_xor(parts):
        return [
            lax.dynamic_index_in_dim(
                parts, lax.bitwise_xor(info[AT_HIGH], jnp.int32(k)), 0, keepdims=False
            )
            for k in range(4)
        ]

    def others(near):
        return jnp.stack(by_xor(near)[1:], axis=0)

    def after(value, point):
        return lax.optimization_barrier((value, point))[0]

    def swap_tensor(value, mask):
        return lax.ppermute(value, "tensor", [(i, i ^ mask) for i in range(8)])

    def swap_dp(value):
        return lax.ppermute(value, "dp", [(0, 1), (1, 0)])

    def swap_seq(value):
        return lax.ppermute(value, "seq", [(0, 1), (1, 0)])

    def gather_width(shard, point=None, last=None):
        if fast:
            other = swap_dp(shard)
            own = shard
            if last is not None:
                own, other = after(own, point), after(other, last)
            return [shard, other, swap_seq(own), swap_seq(other)]
        axis = shard.ndim - 2
        full = lax.all_gather(shard, ("dp", "seq"), axis=axis, tiled=True)
        return [lax.slice_in_dim(full, i * QUARTER, (i + 1) * QUARTER, axis=axis) for i in range(4)]

    def gather_all(shard):
        return lax.all_gather(shard, ("dp", "seq"), axis=0, tiled=True)

    def scatter_all(full):
        return lax.psum_scatter(full, ("dp", "seq"), scatter_dimension=0, tiled=True)

    def weight_full(a, b, halves=False):
        n, width = b.shape
        if halves:
            specs = [
                pl.BlockSpec((QUARTER, width), lambda i: (jnp.minimum(i, 1), 0)),
                pl.BlockSpec((QUARTER, width), lambda i: (jnp.maximum(i - 2, 0), 0)),
            ]
        else:
            specs = [pl.BlockSpec((QUARTER, width), lambda i: (i, 0))]
        outs = pl.pallas_call(
            weight_grad_kernel,
            grid=(4,),
            in_specs=[pl.BlockSpec((n, QUARTER), lambda i: (0, i)), whole((n, width))],
            out_specs=specs,
            out_shape=[jax.ShapeDtypeStruct((D // len(specs), width), BF16)] * len(specs),
            compiler_params=vmem(56),
            cost_estimate=cost(n * width / 160000),
            name="weight_grad",
        )(a, b)
        return tuple(outs) if halves else outs[0]

    def weight_halves(a, b):
        return weight_full(a, b, True)

    def pair_sum(a, b, place):
        part = pl.BlockSpec((QUARTER, a.shape[1]), lambda i: (place, 0))
        return pl.pallas_call(
            pair_sum_kernel,
            grid=(1,),
            in_specs=[part, part],
            out_specs=whole((QUARTER, a.shape[1])),
            out_shape=jax.ShapeDtypeStruct((QUARTER, a.shape[1]), BF16),
            compiler_params=vmem(48),
            cost_estimate=cost(1.5),
            name="pair_sum",
        )(a, b)

    def scatter_near(halves, point):
        keep, send = halves
        if not fast:
            return keep, send, None
        got = after(swap_seq(send), point)
        return keep, got, pair_sum(keep, got, 1)

    def send_far(near):
        return swap_dp(near[2]) if fast else None

    def scatter_far(near, far):
        keep, got, low = near
        if fast:
            return [keep, got, far]
        full = jnp.concatenate([keep, got], axis=0)
        return [lax.psum_scatter(full, ("dp", "seq"), scatter_dimension=0, tiled=True)]

    def swap_high(pieces):
        return [pieces[0]] + [swap_tensor(pieces[k], 2 * k) for k in (1, 2, 3)]

    def scatter_parts(total):
        n = total.shape[0] // 4
        return [total[:n]] + [
            swap_tensor(total[i * n : (i + 1) * n].astype(BF16), mask)
            for i, mask in ((1, 2), (2, 4), (3, 6))
        ]

    def gather_near(own):
        return jnp.concatenate([own] + [swap_tensor(own, mask) for mask in (2, 4, 6)], axis=0)

    attn_low = jnp.concatenate(
        [query_weight, kv_weight, jnp.pad(norm_gains, ((0, 0), (0, 126)))], axis=1
    ).astype(BF16)
    back_low = jnp.concatenate([query_weight, kv_weight], axis=1).astype(BF16)
    output_low = after(output_weight.astype(BF16), attn_low)
    output_near = lax.all_gather(output_low, "tensor", axis=0, axis_index_groups=HIGH_GROUPS)
    token_rows = tokens.reshape(span, D)
    cot_rows = cotangent.reshape(span, D)
    positions = seq_id * span + jnp.arange(span, dtype=jnp.int32)
    cosine, sine = rope_tables(positions)
    attn_w = gather_width(attn_low, attn_low, (cosine, sine))
    half_span = span // 2
    dy = pl.pallas_call(
        reorder_kernel,
        grid_spec=pltpu.PrefetchScalarGridSpec(
            num_scalar_prefetch=1,
            grid=(8,),
            in_specs=[pl.BlockSpec((block, D), lambda i, info: (tensor_block(i, info), 0))],
            out_specs=pl.BlockSpec((2, half_block, D), lambda i, info: (0, i, 0)),
        ),
        out_shape=jax.ShapeDtypeStruct((2, half_span, D), BF16),
        cost_estimate=cost(7.5),
        name="reorder",
    )(info, cot_rows)

    normed_one, queries, kv_own, gains = pl.pallas_call(
        project_kernel,
        grid_spec=pltpu.PrefetchScalarGridSpec(
            num_scalar_prefetch=1,
            grid=(span // rows,),
            in_specs=[pl.BlockSpec((rows, D), lambda i, info: (i, 0))]
            + [whole((QUARTER, 512))] * 4
            + [pl.BlockSpec((rows, 128), lambda i, info: (i, 0))] * 2,
            out_specs=[
                pl.BlockSpec((rows, D), lambda i, info: (i, 0)),
                pl.BlockSpec((rows, 256), lambda i, info: (i, 0)),
                pl.BlockSpec((rows, 128), lambda i, info: (i, 0)),
                whole((8, D)),
            ],
            scratch_shapes=[pltpu.VMEM((8, D), F32)],
        ),
        out_shape=[
            jax.ShapeDtypeStruct((span, D), BF16),
            jax.ShapeDtypeStruct((span, 256), BF16),
            jax.ShapeDtypeStruct((span, 128), BF16),
            jax.ShapeDtypeStruct((8, D), F32),
        ],
        compiler_params=vmem(48),
        cost_estimate=cost(7),
        name="project",
    )(info, token_rows, *attn_w, cosine, sine)

    gate_up_late, down_late = after((gate_up_weight, down_weight), queries)
    gate_up_low = jnp.concatenate(
        [gate_up_late[:, 0, :], gate_up_late[:, 1, :]], axis=1
    ).astype(BF16)
    down_low = down_late.astype(BF16)

    if fast:
        kv_other = swap_seq(kv_own)
        kv_all = jnp.where(
            seq_id == 0,
            jnp.concatenate([kv_own, kv_other], axis=0),
            jnp.concatenate([kv_other, kv_own], axis=0),
        )
    else:
        kv_all = lax.all_gather(kv_own, "seq", axis=0, tiled=True)

    steps = 4
    attended, logs = pl.pallas_call(
        functools.partial(attend_kernel, rows, max(keys, 2 * rows)),
        grid_spec=pltpu.PrefetchScalarGridSpec(
            num_scalar_prefetch=1,
            grid=(steps,),
            in_specs=[
                pl.BlockSpec((rows, 256), lambda i, info: (i, 0)),
                whole((length, 128)),
            ],
            out_specs=[
                pl.BlockSpec((rows, 256), lambda i, info: (i, 0)),
                pl.BlockSpec((1, 1, GROUP * rows), lambda i, info: (i, 0, 0)),
            ],
            scratch_shapes=[
                pltpu.VMEM((128, length), BF16),
                pltpu.VMEM((128, GROUP * rows), F32),
                pltpu.VMEM((1, GROUP * rows), F32),
            ],
        ),
        out_shape=[
            jax.ShapeDtypeStruct((span, 256), BF16),
            jax.ShapeDtypeStruct((steps, 1, GROUP * rows), F32),
        ],
        compiler_params=vmem(48),
        cost_estimate=cost(18),
        name="attend",
    )(info, queries, kv_all)

    mlp_w = gather_all(jnp.concatenate([gate_up_low, down_low], axis=1))
    att_parts = lax.all_to_all(
        attended.reshape(4, rows, 256), "tensor", 0, 0, axis_index_groups=HIGH_GROUPS
    )
    att_parts = after(att_parts, dy)
    output_w = gather_width(after(output_near, queries), att_parts, att_parts)

    out_keep, out_send = pl.pallas_call(
        out_kernel,
        grid_spec=pltpu.PrefetchScalarGridSpec(
            num_scalar_prefetch=1,
            grid=(1,),
            in_specs=[whole((4, rows, 256))] + [whole((4, QUARTER, 256))] * 4,
            out_specs=[whole((block, D))] * 2,
            scratch_shapes=[pltpu.VMEM((rows, QUARTER), F32)],
        ),
        out_shape=[jax.ShapeDtypeStruct((block, D), F32), jax.ShapeDtypeStruct((block, D), BF16)],
        compiler_params=vmem(48),
        cost_estimate=cost(3.8),
        name="attention_out",
    )(info, att_parts, *output_w)
    out_got = swap_tensor(out_send, 1)
    own_rows = pl.BlockSpec((block, D), lambda i, info: (info[AT_TENSOR], 0))
    resid_one, low_a, low_b = pl.pallas_call(
        norm_kernel,
        grid_spec=pltpu.PrefetchScalarGridSpec(
            num_scalar_prefetch=1,
            grid=(1,),
            in_specs=[whole((block, D))] * 2 + [own_rows, whole((8, D))],
            out_specs=[whole((block, D)), whole((half_block, D)), whole((half_block, D))],
        ),
        out_shape=[
            jax.ShapeDtypeStruct((block, D), F32),
            jax.ShapeDtypeStruct((half_block, D), BF16),
            jax.ShapeDtypeStruct((half_block, D), BF16),
        ],
        cost_estimate=cost(3.5),
        name="second_norm",
    )(info, out_keep, out_got, token_rows, gains)

    def mlp(chunk, nears, fars, before):
        n = half_span
        anywhere = pl.BlockSpec(memory_space=pl.ANY)
        late_columns = pl.BlockSpec(
            (4, half_block, QUARTER), lambda i, info: (0, 0, jnp.maximum(i - 4, 0))
        )
        late_half = pl.BlockSpec((n // 2, QUARTER), lambda i, info: (0, jnp.maximum(i - 4, 0)))
        return pl.pallas_call(
            functools.partial(mlp_kernel, len(nears)),
            grid_spec=pltpu.PrefetchScalarGridSpec(
                num_scalar_prefetch=1,
                grid=(8,),
                in_specs=[whole((n // 2 // len(nears), D))] * (2 * len(nears))
                + [pl.BlockSpec((1, n, D), lambda i, info: (chunk, 0, 0))]
                + [anywhere] * (1 + len(before)),
                out_specs=[
                    late_columns,
                    late_columns,
                    late_half,
                    late_half,
                    pl.BlockSpec((n, 1024), lambda i, info: (chunk, 0)),
                    pl.BlockSpec((n, 2048), lambda i, info: (chunk, 0)),
                    pl.BlockSpec((n, D), lambda i, info: (chunk, 0)),
                ],
                scratch_shapes=[
                    pltpu.VMEM((D, 2048), BF16),
                    pltpu.VMEM((D, 1024), BF16),
                    pltpu.SemaphoreType.DMA((4, 3)),
                ],
            ),
            out_shape=[
                jax.ShapeDtypeStruct((4, half_block, D), BF16),
                jax.ShapeDtypeStruct((4, half_block, D), BF16),
                jax.ShapeDtypeStruct((n // 2, D), BF16),
                jax.ShapeDtypeStruct((n // 2, D), BF16),
                jax.ShapeDtypeStruct((span, 1024), BF16),
                jax.ShapeDtypeStruct((span, 2048), BF16),
                jax.ShapeDtypeStruct((span, D), BF16),
            ],
            input_output_aliases={5: 4, 6: 5, 7: 6} if before else {},
            compiler_params=vmem(56),
            cost_estimate=cost(22.5),
            name="mlp",
        )(info, *nears, *fars, dy, mlp_w, *before)

    near_a = gather_near(low_a)
    near_b = gather_near(low_b)
    far_a = after(swap_tensor(near_a, 1), near_b)
    far_b = swap_tensor(near_b, 1)
    mlp_keep_a, mlp_send_a, two_keep_a, two_send_a, hidden, gate_up_back, x = mlp(
        0, (near_a,), (far_a,), ()
    )
    two_got_a = swap_tensor(two_send_a, 1)
    back_low = after(back_low, near_b)
    back_parts = [swap_tensor(back_low, mask) for mask in (2, 4, 6)]
    mlp_keep_b, mlp_send_b, two_keep_b, two_send_b, hidden, gate_up_back, x = mlp(
        1, (near_b,), (far_b,), (hidden, gate_up_back, x)
    )
    two_got_b = swap_tensor(two_send_b, 1)
    total_a = two_keep_a.astype(F32) + after(two_got_a, two_send_b).astype(F32)
    two_a = scatter_parts(total_a)
    back_near = jnp.stack(after([back_low] + back_parts, two_send_b), axis=0)
    hidden, gate_up_back = after((hidden, gate_up_back), (total_a, back_near))
    narrow = pl.BlockSpec((span, QUARTER), lambda i: (0, i))
    mlp_full = pl.pallas_call(
        mlp_grad_kernel,
        grid=(4,),
        in_specs=[narrow, whole((span, 2048)), narrow, whole((span, 1024))],
        out_specs=pl.BlockSpec((QUARTER, 3072), lambda i: (i, 0)),
        out_shape=jax.ShapeDtypeStruct((D, 3072), BF16),
        compiler_params=vmem(56),
        cost_estimate=cost(22),
        name="mlp_grad",
    )(x, gate_up_back, dy.reshape(span, D), hidden)
    total_b = two_keep_b.astype(F32) + after(
        two_got_b, (mlp_full, two_a)
    ).astype(F32)
    two_b = scatter_parts(total_b)
    mlp_grad = scatter_all(after(mlp_full, total_b))
    mlp_got_a = swap_tensor(after(mlp_send_a, total_b), 1)

    resid_grad, resid_low, gain_two_grad = pl.pallas_call(
        norm_back_kernel,
        grid_spec=pltpu.PrefetchScalarGridSpec(
            num_scalar_prefetch=1,
            grid=(1,),
            in_specs=[whole((half_block, D))] * 8
            + [
                whole((block, D)),
                pl.BlockSpec((2, half_block, D), lambda i, info: (0, 0, 0)),
                whole((8, D)),
            ],
            out_specs=[whole((block, D)), whole((block, D)), whole((1, D))],
        ),
        out_shape=[
            jax.ShapeDtypeStruct((block, D), F32),
            jax.ShapeDtypeStruct((block, D), BF16),
            jax.ShapeDtypeStruct((1, D), F32),
        ],
        cost_estimate=cost(4.7),
        name="second_norm_back",
    )(info, *two_a, *two_b, resid_one, dy, gains)
    resid_other = swap_tensor(resid_low, 1)
    mlp_total_a = (mlp_keep_a.astype(F32) + after(mlp_got_a, resid_low).astype(F32)).astype(BF16)
    mlp_parts_a = lax.all_to_all(mlp_total_a, "tensor", 0, 0, axis_index_groups=HIGH_GROUPS)
    resid_other = after(resid_other, mlp_total_a)
    mlp_got_b = swap_tensor(after(mlp_send_b, resid_other), 1)
    resid_both, *grad_pieces = pl.pallas_call(
        out_back_kernel,
        grid_spec=pltpu.PrefetchScalarGridSpec(
            num_scalar_prefetch=1,
            grid=(1,),
            in_specs=[whole((block, D))] * 2 + [whole((4, QUARTER, 256))] * 4,
            out_specs=[whole((rows, D))] + [whole((rows, 256))] * 4,
        ),
        out_shape=[jax.ShapeDtypeStruct((rows, D), BF16)]
        + [jax.ShapeDtypeStruct((rows, 256), BF16)] * 4,
        compiler_params=vmem(48),
        cost_estimate=cost(3.9),
        name="attention_out_back",
    )(info, resid_low, resid_other, *output_w)
    grad_parts = swap_high(grad_pieces)
    mlp_total_b = (mlp_keep_b.astype(F32) + after(mlp_got_b, grad_parts).astype(F32)).astype(BF16)
    mlp_parts_b = lax.all_to_all(mlp_total_b, "tensor", 0, 0, axis_index_groups=HIGH_GROUPS)
    back_w = gather_width(back_near, resid_low, resid_low)
    grad_parts = after(grad_parts, (mlp_total_b, back_w))

    spans = seq_size if fast else length // span
    dq, *dq_pieces, dkv = pl.pallas_call(
        functools.partial(attend_back_kernel, rows, keys, spans),
        grid_spec=pltpu.PrefetchScalarGridSpec(
            num_scalar_prefetch=1,
            grid=(steps,),
            in_specs=[pl.BlockSpec((rows, 256), lambda i, info: (i, 0))]
            + [whole((rows, 256))] * 4
            + [
                pl.BlockSpec((rows, 256), lambda i, info: (i, 0)),
                pl.BlockSpec((1, 1, GROUP * rows), lambda i, info: (i, 0, 0)),
                whole((length, 128)),
                pl.BlockSpec((rows, 128), lambda i, info: (i, 0)),
                pl.BlockSpec((rows, 128), lambda i, info: (i, 0)),
            ],
            out_specs=[pl.BlockSpec((rows, 256), lambda i, info: (i, 0))]
            + [whole((rows, 256))] * 4
            + [whole((spans, span, 128))],
            scratch_shapes=[
                pltpu.VMEM((HEAD_DIM, length), BF16),
                pltpu.VMEM((length, 128), F32),
                pltpu.VMEM((HEAD_DIM, GROUP * rows), F32),
                pltpu.VMEM((rows, 256), BF16),
            ],
        ),
        out_shape=[jax.ShapeDtypeStruct((span, 256), BF16)]
        + [jax.ShapeDtypeStruct((rows, 256), BF16)] * 4
        + [jax.ShapeDtypeStruct((spans, span, 128), BF16)],
        compiler_params=vmem(48),
        cost_estimate=cost(23),
        name="attend_back",
    )(info, queries, *grad_parts, attended, logs, kv_all, cosine, sine)

    if fast:
        dkv_own, dkv_more = dkv[0], swap_seq(dkv[1])
    else:
        dkv_own = lax.psum_scatter(dkv.reshape(length, 128), "seq", scatter_dimension=0, tiled=True)
        dkv_more = jnp.zeros_like(dkv_own)
    dq_parts = swap_high(dq_pieces)
    dkv_more = after(dkv_more, dq_parts)
    dkv_low, *dkv_pieces = pl.pallas_call(
        kv_back_kernel,
        grid_spec=pltpu.PrefetchScalarGridSpec(
            num_scalar_prefetch=1,
            grid=(1,),
            in_specs=[whole((span, 128))] * 4,
            out_specs=[whole((span, 128))] + [whole((rows, 128))] * 4,
        ),
        out_shape=[jax.ShapeDtypeStruct((span, 128), BF16)]
        + [jax.ShapeDtypeStruct((rows, 128), BF16)] * 4,
        cost_estimate=cost(3.2),
        name="kv_back",
    )(info, dkv_own, dkv_more, cosine, sine)

    dkv_parts = swap_high(dkv_pieces)
    block_low = pl.pallas_call(
        block_out_kernel,
        out_shape=jax.ShapeDtypeStruct((block, D), BF16),
        cost_estimate=cost(3),
        name="block_out",
    )(*after((mlp_parts_a, mlp_parts_b), dkv_low), resid_one)
    dkv_parts = after(dkv_parts, (mlp_grad, block_low))
    one_keep, one_send = pl.pallas_call(
        one_kernel,
        grid_spec=pltpu.PrefetchScalarGridSpec(
            num_scalar_prefetch=1,
            grid=(1,),
            in_specs=[whole((rows, 256))] * 4
            + [whole((rows, 128))] * 4
            + [whole((4, QUARTER, 384))] * 4,
            out_specs=[whole((block, D))] * 2,
            scratch_shapes=[pltpu.VMEM((rows, QUARTER), F32)],
        ),
        out_shape=[jax.ShapeDtypeStruct((block, D), F32), jax.ShapeDtypeStruct((block, D), BF16)],
        compiler_params=vmem(48),
        cost_estimate=cost(5.8),
        name="attention_in_back",
    )(info, *dq_parts, *dkv_parts, *back_w)
    one_got = swap_tensor(one_send, 1)
    dqkv = after(jnp.concatenate([dq, dkv_low], axis=1), one_send)
    attn_halves = weight_halves(normed_one, dqkv)
    out_halves = weight_halves(
        after(resid_both, one_send), jnp.concatenate(by_xor(att_parts), axis=1)
    )

    block_near = lax.all_gather(block_low, "tensor", axis=0, axis_index_groups=HIGH_GROUPS)
    one_got = after(one_got, (attn_halves, out_halves))
    out_near = scatter_near(out_halves, one_got)
    out_far = send_far(out_near)

    tokens_low = pl.pallas_call(
        tokens_back_kernel,
        grid_spec=pltpu.PrefetchScalarGridSpec(
            num_scalar_prefetch=1,
            grid=(1,),
            in_specs=[whole((block, D))] * 2 + [own_rows, whole((block, D)), whole((8, D))],
            out_specs=whole((block, D)),
        ),
        out_shape=jax.ShapeDtypeStruct((block, D), BF16),
        cost_estimate=cost(4.3),
        name="first_norm_back",
    )(info, one_keep, one_got, token_rows, resid_grad, gains)
    tokens_own = swap_tensor(tokens_low, 1)
    tokens_near = lax.all_gather(tokens_low, "tensor", axis=0, axis_index_groups=HIGH_GROUPS)

    attn_near = scatter_near(attn_halves, one_send)
    attn_far = send_far(attn_near)

    def adam(weight, one, two, terms, rate, decay):
        size = weight.shape[0] // 4
        if weight.ndim == 3:
            mine = pl.BlockSpec((size, 2, weight.shape[2]), lambda i: (i, 0, 0))
            wide = 2 * weight.shape[2]
        else:
            mine = pl.BlockSpec((size, weight.shape[1]), lambda i: (i, 0))
            wide = weight.shape[1]
        return pl.pallas_call(
            functools.partial(adam_kernel, rate, decay),
            grid=(4,),
            in_specs=[mine] * 3
            + [
                pl.BlockSpec((size, wide), lambda i, column=column: (i, column))
                for term, column in terms
            ],
            out_specs=[mine] * 3,
            out_shape=[jax.ShapeDtypeStruct(weight.shape, F32)] * 3,
            compiler_params=vmem(56),
            cost_estimate=cost(weight.size / 75000),
            name="adam",
        )(weight, one, two, *[term for term, column in terms])

    fan_in = RATE_FACTOR * D ** (-0.5)
    mlp_grad = after(mlp_grad, tokens_low)
    gate_up_new = adam(
        gate_up_weight, gate_up_first, gate_up_second, [(mlp_grad, 0)], fan_in, DECAY
    )
    down_new = adam(
        down_weight, down_first, down_second, [(mlp_grad, 2)], RATE_FACTOR * FF ** (-0.5), DECAY
    )

    products = jnp.concatenate(
        [
            jnp.sum(
                attn_halves[i // 2][(i % 2) * QUARTER : (i % 2 + 1) * QUARTER].astype(F32)
                * w[:, :384].astype(F32),
                axis=1,
            )
            / w[:, 384].astype(F32)
            for i, w in enumerate(attn_w)
        ]
    )
    gain_grads = jnp.stack(
        [
            products,
            jnp.concatenate(
                [lax.dynamic_slice(gain_two_grad[0], (info[i] * QUARTER,), (QUARTER,)) for i in range(4)]
            ),
        ]
    )
    if fast:
        gain_grads = gain_grads[:, : 2 * QUARTER] + swap_seq(gain_grads[:, 2 * QUARTER :])
        gain_got = swap_tensor(gain_grads, 1)
    else:
        shard = norm_gains.shape[0]
        gains_grad = lax.dynamic_slice(
            lax.psum(gain_grads, ("dp", "seq")),
            (0, (dp_id * seq_size + seq_id) * shard),
            (2, shard),
        )
        gain_grads = gains_grad
        gain_got = swap_tensor(gains_grad, 1)
    block_far = swap_tensor(after(block_near, tokens_own), 1)
    gain_grads = gain_grads + gain_got
    early = (gate_up_new, down_new, gain_grads) + ((out_far, attn_far) if fast else ())
    tokens_near = after(tokens_near, early)
    tokens_far = swap_tensor(others(tokens_near), 1)

    attn_terms = after(scatter_far(attn_near, attn_far), tokens_near)
    query_new = adam(
        query_weight, query_first, query_second, [(term, 0) for term in attn_terms], fan_in, DECAY
    )
    kv_new = adam(kv_weight, kv_first, kv_second, [(term, 2) for term in attn_terms], fan_in, DECAY)

    out_terms = scatter_far(out_near, out_far)
    out_rows = sum(term[: out_terms[-1].shape[0]].astype(F32) for term in after(out_terms, tokens_near))
    output_terms = swap_high([out_rows[:, k * 256 : (k + 1) * 256].astype(BF16) for k in range(4)])
    output_new = adam(
        output_weight,
        output_first,
        output_second,
        [(term, 0) for term in output_terms],
        RATE_FACTOR * FAN_OUT ** (-0.5),
        DECAY,
    )

    gain_grads = after(gain_grads, tokens_near)
    if fast:
        gains_grad = gain_grads[:, :QUARTER] + swap_dp(gain_grads[:, QUARTER:])
    else:
        gains_grad = gain_grads
    for mask in (2, 4):
        gains_grad = gains_grad + swap_tensor(gains_grad, mask)
    gains_grad = gains_grad.T
    gains_new = adam_step(norm_gains, gains_grad, gains_first, gains_second, GAIN_RATE, 0.0)


    def place(parts, dtype, name):
        return pl.pallas_call(
            place_kernel,
            grid_spec=pltpu.PrefetchScalarGridSpec(
                num_scalar_prefetch=1,
                grid=(4,),
                in_specs=[pl.BlockSpec((1, block, D), lambda i, info: (i, 0, 0))] * 2,
                out_specs=pl.BlockSpec((rows, D), lambda i, info: (i, 0)),
            ),
            out_shape=jax.ShapeDtypeStruct((span, D), dtype),
            compiler_params=vmem(48),
            cost_estimate=cost(5),
            name=name,
        )(info, *parts).reshape(tokens.shape)

    def place_own(parts, dtype, name):
        return pl.pallas_call(
            place_own_kernel,
            grid_spec=pltpu.PrefetchScalarGridSpec(
                num_scalar_prefetch=1,
                grid=(4,),
                in_specs=[
                    pl.BlockSpec(
                        (1, block, D), lambda i, info: (lax.bitwise_xor(info[AT_HIGH], i), 0, 0)
                    ),
                    whole((block, D)),
                ],
                out_specs=pl.BlockSpec(
                    (rows, D), lambda i, info: (lax.bitwise_xor(info[AT_HIGH], i), 0)
                ),
            ),
            out_shape=jax.ShapeDtypeStruct((span, D), dtype),
            compiler_params=vmem(48),
            cost_estimate=cost(5),
            name=name,
        )(info, *parts)

    placed = place_own((tokens_near, tokens_own), F32, "tokens_grad_near")
    tokens_grad = pl.pallas_call(
        place_far_kernel,
        grid_spec=pltpu.PrefetchScalarGridSpec(
            num_scalar_prefetch=1,
            grid=(3,),
            in_specs=[
                pl.BlockSpec(memory_space=pl.ANY),
                pl.BlockSpec((1, block, D), lambda i, info: (i, 0, 0)),
            ],
            out_specs=pl.BlockSpec(
                (block, D),
                lambda i, info: (
                    lax.bitwise_xor(info[AT_HIGH], i + 1) * 2 + 1 - info[AT_LOW],
                    0,
                ),
            ),
        ),
        out_shape=jax.ShapeDtypeStruct((span, D), F32),
        input_output_aliases={1: 0},
        compiler_params=vmem(48),
        name="tokens_grad_far",
    )(info, placed, tokens_far).reshape(tokens.shape)
    block_out = place((block_near, block_far), BF16, "block_out_rows")

    results = (query_new, output_new, kv_new, gate_up_new, down_new, gains_new)
    return (block_out, tokens_grad) + tuple(r[i] for i in range(3) for r in results)


def solution(mesh):
    wide = P(("dp", "seq"), "tensor")
    weights = (wide, wide, wide, P(("dp", "seq"), None, "tensor"), wide, P(("dp", "seq"), None))
    rows = P("dp", "seq", None)
    return jax.shard_map(
        functools.partial(body, dp_size=mesh.shape["dp"], seq_size=mesh.shape["seq"]),
        mesh=mesh,
        in_specs=(rows, rows) + weights * 3,
        out_specs=(rows, rows) + weights * 3,
        check_vma=False,
    )
```
